128 devices in a mesh: lon: 8 (over x, core), lat: 16 (over y, z).
Axes of the slice: x: 4, y: 4, z: 4, core: 2. Of those that a mesh axis runs over, the one named last changes fastest.
Arguments:
- radiances: bfloat16 [262144, 128], P(('lon', 'lat')), may hold values from -6 to 6
- block_tile: int32 [2048], P(('lon', 'lat')), may hold values from 0 to 15, as said below
- block_rows: int32 [2048], P(('lon', 'lat')), may hold values from 1 to 128
- row_cells: int32 [262144], P(('lon', 'lat')), may hold values from 0 to 511
- latents: bfloat16 [64, 1024, 1024], P('lat', 'lon'), may hold values from -6 to 6
- disk_pixels: bfloat16 [5, 16, 64, 1024], P(None, None, 'lat', 'lon'), may hold values from -6 to 6
- targets: float32 [64, 1024, 128], P('lat', 'lon'), may hold values from -6 to 6
- w_query: bfloat16 [1024, 1024], replicated, may hold values from -0.1875 to 0.1875
- w_key: bfloat16 [128, 1024], replicated, may hold values from -0.5 to 0.5
- w_value: bfloat16 [128, 1024], replicated, may hold values from -0.5 to 0.5
- w_disk_key: bfloat16 [16, 1024], replicated, may hold values from -1.5 to 1.5
- w_disk_value: bfloat16 [16, 1024], replicated, may hold values from -1.5 to 1.5
- w_out: bfloat16 [1024, 1024], replicated, may hold values from -0.1875 to 0.1875
- w_decode: bfloat16 [1024, 128], replicated, may hold values from -0.1875 to 0.1875
Outputs:
- total_loss: float32 [], replicated
- latent_grad: float32 [64, 1024, 1024], P('lat', 'lon')
- row_grad: bfloat16 [262144, 128], P(('lon', 'lat'))
- update_query: float32 [1024, 1024], P(('lon', 'lat'))
- update_out: float32 [1024, 1024], P(('lon', 'lat'))
- update_key: float32 [128, 1024], replicated
- update_value: float32 [128, 1024], replicated
- update_disk_key: float32 [16, 1024], replicated
- update_disk_value: float32 [16, 1024], replicated
The draws below stay inside these ranges and needn't reach their ends.
Inputs may be any that keep to these rules, and one draw needn't show every extreme that they name: `block_tile`: tile index within the reading device's longitude column. A device sends at most 2 of its 16 blocks to one tile; in every longitude column one tile gets exactly 2 blocks from every device of that column. `row_cells`: cell numbered row-major over 4 grid rows of 128 columns of the tile.
All inputs are finite; a program needn't handle non-finite values.
Results may differ from the reference program's by a relative error of at most 0.019.
Values may be sent and summed in bfloat16 or wider, within the bound.
A program may use at most 128 MiB of HBM per device.

```python
import math
import jax
import jax.numpy as jnp
from jax import lax

FEAT = 128
D = 1024
HEADS = 16
HD = 64
OUT = 128
CH = 16
DISKS = 5
BLK = 128
CAP = 2
NB = 16
CLAT = 4
CLON = 128
NBLK = 2048
ROWS = 262144
NLAT = 64
NLON = 1024
N_LON = 8
N_LAT = 16
DEVICES = 128


def permute_many(device_keys, length):

    def permute_one(single_key):
        return jax.random.permutation(single_key, length)
    return jax.vmap(permute_one)(device_keys)


def draw_block_tile(key, part):
    key = jax.random.fold_in(key, 11)
    hot_key, other_key, order_key = jax.random.split(key, 3)
    device_total = N_LON * N_LAT
    hot_tile = jax.random.randint(hot_key, (N_LON, 1), 0, N_LAT)
    hot_tile = jnp.repeat(hot_tile, N_LAT, axis=0)
    others = permute_many(jax.random.split(other_key, device_total), N_LAT - 1).astype(jnp.int32)
    others = others + (others >= hot_tile).astype(jnp.int32)
    position = jnp.arange(NB, dtype=jnp.int32)
    other_slot = jnp.maximum(position - CAP, 0) % (N_LAT - 1)
    chosen = jnp.take(others, other_slot, axis=1)
    block_tiles = jnp.where(position[None, :] < CAP, hot_tile, chosen)
    shuffle = permute_many(jax.random.split(order_key, device_total), NB).astype(jnp.int32)
    block_tiles = jnp.take_along_axis(block_tiles, shuffle, axis=1)
    return block_tiles.reshape(device_total * NB).astype(jnp.int32)


def touch_ends(entries, stream_key, low, high):
    extent = entries.shape
    place = [jax.random.randint(jax.random.fold_in(stream_key, axis), (), 0, extent[axis]) for axis in range(len(extent))]
    entries = entries.at[tuple(place)].set(low)
    longest = extent.index(max(extent))
    place[longest] = (place[longest] + 1) % extent[longest]
    return entries.at[tuple(place)].set(high)


def level_of(rng, dims, pieces, low, high):
    def one(axis_at, parts):
        draws = jax.random.uniform(jax.random.fold_in(jax.random.fold_in(rng, 6), axis_at), (parts,), jnp.float32, low / len(pieces), high / len(pieces))
        return jnp.repeat(jnp.exp(draws), dims[axis_at] // parts).reshape((-1,) + (1,) * (len(dims) - axis_at - 1))

    gain = one(*pieces[0])
    for cut in pieces[1:]:
        gain = gain * one(*cut)
    return gain


def noise(key, dims, scale, reach, pieces=(), kind=jnp.bfloat16):
    entries = jax.random.normal(key, dims, jnp.float32) * scale
    if len(pieces) > 0:
        entries = level_of(key, dims, pieces, -0.22, 0.18) * entries
    return jnp.clip(entries, min=-reach, max=reach).astype(kind)


def setup_inputs(seed: int = 0) -> dict:
    keys = jax.random.split(jax.random.key(seed), 15)
    return {
        "radiances": noise(keys[0], (ROWS, FEAT), 1.0, 6.0, ((0, 128),)),
        "block_tile": draw_block_tile(jax.random.fold_in(keys[14], 71), 0),
        "block_rows": touch_ends(jax.random.randint(keys[2], (NBLK,), 1, BLK + 1), jax.random.fold_in(keys[2], 1), 1, BLK).astype(jnp.int32),
        "row_cells": touch_ends(jax.random.randint(keys[3], (ROWS,), 0, CLAT * CLON), jax.random.fold_in(keys[3], 1), 0, (CLAT * CLON) - 1).astype(jnp.int32),
        "latents": noise(keys[4], (NLAT, NLON, D), 1.0, 6.0, ((0, 16), (1, 8))),
        "disk_pixels": noise(keys[5], (DISKS, CH, NLAT, NLON), 1.0, 6.0, ((2, 16), (3, 8))),
        "targets": noise(keys[6], (NLAT, NLON, OUT), 1.0, 6.0, ((0, 16), (1, 8)), jnp.float32),
        "w_query": noise(keys[7], (D, D), D ** -0.5, 0.1875),
        "w_key": noise(keys[8], (FEAT, D), FEAT ** -0.5, 0.5),
        "w_value": noise(keys[9], (FEAT, D), FEAT ** -0.5, 0.5),
        "w_disk_key": noise(keys[10], (CH, D), CH ** -0.5, 1.5),
        "w_disk_value": noise(keys[11], (CH, D), CH ** -0.5, 1.5),
        "w_out": noise(keys[12], (D, D), D ** -0.5, 0.1875),
        "w_decode": noise(keys[13], (D, OUT), D ** -0.5, 0.1875),
    }


def latitude_weights(row_total):
    centres = (jnp.arange(row_total, dtype=jnp.float32) + 0.5) / row_total
    return jnp.cos(math.pi / 180.0 * (-60.0 + 120.0 * centres))

def head_sums(product, head_count):
    return lax.optimization_barrier(jnp.sum(product.reshape(product.shape[0], head_count, -1), axis=2))

def per_head(head_weights, values):
    head_count = head_weights.shape[1]
    spread = head_weights[:, :, None] * values.reshape(values.shape[0], head_count, -1)
    return spread.reshape(values.shape)

def normalized(gradient):
    return gradient / jnp.sqrt(jnp.mean(gradient * gradient) + 1e-06)

def row_forward(query_low, w_key, w_value, row_feats, row_cell, row_valid, head_count, score_scale):
    key_rows = jnp.dot(row_feats, w_key, preferred_element_type=jnp.float32)
    value_rows = jnp.dot(row_feats, w_value, preferred_element_type=jnp.float32)
    query_rows = query_low[row_cell].astype(jnp.float32)
    gating = jax.nn.sigmoid(head_sums(query_rows * key_rows, head_count) * score_scale) * row_valid[:, None]
    return per_head(gating, value_rows)

def row_backward(query_low, w_key, w_value, grad_mixed, row_feats, row_cell, row_valid, head_count, score_scale):
    key_rows = jnp.dot(row_feats, w_key, preferred_element_type=jnp.float32)
    value_rows = jnp.dot(row_feats, w_value, preferred_element_type=jnp.float32)
    query_rows = query_low[row_cell].astype(jnp.float32)
    gating = jax.nn.sigmoid(head_sums(query_rows * key_rows, head_count) * score_scale) * row_valid[:, None]
    grad_rows = grad_mixed[row_cell]
    grad_value = per_head(gating, grad_rows).astype(jnp.bfloat16)
    grad_score = head_sums(grad_rows * value_rows, head_count) * gating * (1.0 - gating) * score_scale
    grad_key = per_head(grad_score, query_rows).astype(jnp.bfloat16)
    query_term = per_head(grad_score, key_rows)
    grad_wkey = jnp.dot(row_feats.T, grad_key, preferred_element_type=jnp.float32)
    grad_wvalue = jnp.dot(row_feats.T, grad_value, preferred_element_type=jnp.float32)
    back_key = jnp.dot(grad_key, w_key.T, preferred_element_type=jnp.float32)
    back_value = jnp.dot(grad_value, w_value.T, preferred_element_type=jnp.float32)
    return (query_term, grad_wkey, grad_wvalue, (back_key + back_value).astype(jnp.bfloat16))

def disk_forward(query_low, disk_flat, w_disk_key, w_disk_value, head_count, score_scale):
    query_full = query_low.astype(jnp.float32)

    def one_disk(running_sum, pixels):
        disk_key = jnp.dot(pixels.T, w_disk_key, preferred_element_type=jnp.float32)
        disk_value = jnp.dot(pixels.T, w_disk_value, preferred_element_type=jnp.float32)
        gating = jax.nn.sigmoid(head_sums(query_full * disk_key, head_count) * score_scale)
        return (running_sum + per_head(gating, disk_value), None)
    result, unused = lax.scan(one_disk, jnp.zeros(query_low.shape, jnp.float32), disk_flat)
    return result

def disk_backward(query_low, disk_flat, w_disk_key, w_disk_value, grad_mixed, head_count, score_scale):
    query_full = query_low.astype(jnp.float32)

    def one_disk(carried, pixels):
        grad_query, grad_wkey, grad_wvalue = carried
        disk_key = jnp.dot(pixels.T, w_disk_key, preferred_element_type=jnp.float32)
        disk_value = jnp.dot(pixels.T, w_disk_value, preferred_element_type=jnp.float32)
        gating = jax.nn.sigmoid(head_sums(query_full * disk_key, head_count) * score_scale)
        grad_value = per_head(gating, grad_mixed).astype(jnp.bfloat16)
        grad_score = head_sums(grad_mixed * disk_value, head_count) * gating * (1.0 - gating) * score_scale
        grad_key = per_head(grad_score, query_full).astype(jnp.bfloat16)
        grad_query = grad_query + per_head(grad_score, disk_key)
        grad_wkey = grad_wkey + jnp.dot(pixels, grad_key, preferred_element_type=jnp.float32)
        grad_wvalue = grad_wvalue + jnp.dot(pixels, grad_value, preferred_element_type=jnp.float32)
        return ((grad_query, grad_wkey, grad_wvalue), None)
    start_state = (jnp.zeros(query_low.shape, jnp.float32), jnp.zeros(w_disk_key.shape, jnp.float32), jnp.zeros(w_disk_value.shape, jnp.float32))
    result, unused = lax.scan(one_disk, start_state, disk_flat)
    return result

def reference(radiances, block_tile, block_rows, row_cells, latents, disk_pixels, targets, w_query, w_key, w_value, w_disk_key, w_disk_value, w_out, w_decode):
    cell_count = NLAT * NLON
    score_scale = 1.0 / math.sqrt(HD)
    row_ids = jnp.arange(ROWS, dtype=jnp.int32)
    block_ids = row_ids // BLK
    lon_tile = block_ids // (NB * N_LAT)
    lat_tile = block_tile[block_ids]
    grid_row = lat_tile * CLAT + row_cells // CLON
    grid_col = lon_tile * CLON + row_cells % CLON
    flat_cell = (grid_row * NLON + grid_col).astype(jnp.int32)
    row_valid = (row_ids % BLK < block_rows[block_ids]).astype(jnp.float32)
    lat_flat = latents.reshape(cell_count, D)
    query_low = jnp.dot(lat_flat, w_query, preferred_element_type=jnp.float32).astype(jnp.bfloat16)
    step_total = math.gcd(DEVICES, 16)
    group_rows = ROWS // step_total
    row_items = (radiances.reshape(step_total, group_rows, FEAT), flat_cell.reshape(step_total, group_rows), row_valid.reshape(step_total, group_rows))

    def forward_step(running_sum, block_item):
        row_feats, row_cell, valid_rows = block_item
        term = row_forward(query_low, w_key, w_value, row_feats, row_cell, valid_rows, HEADS, score_scale)
        return (running_sum + jax.ops.segment_sum(term, row_cell, num_segments=cell_count), None)
    rows_sum, unused = lax.scan(forward_step, jnp.zeros((cell_count, D), jnp.float32), row_items)
    disk_flat = disk_pixels.reshape(DISKS, CH, cell_count)
    disk_sum = disk_forward(query_low, disk_flat, w_disk_key, w_disk_value, HEADS, score_scale)
    mixed_cells = (rows_sum + disk_sum).astype(jnp.bfloat16)
    updated = (lat_flat.astype(jnp.float32) + jnp.dot(mixed_cells, w_out, preferred_element_type=jnp.float32)).astype(jnp.bfloat16)
    pred_error = jnp.dot(updated, w_decode, preferred_element_type=jnp.float32) - targets.reshape(cell_count, OUT)
    row_weight = latitude_weights(NLAT)
    weight_cell = jnp.repeat(row_weight / jnp.mean(row_weight), NLON)
    total_loss = jnp.sum(weight_cell[:, None] * 0.5 * pred_error * pred_error) / (cell_count * OUT)
    grad_pred = (weight_cell[:, None] * pred_error).astype(jnp.bfloat16)
    grad_upd = jnp.dot(grad_pred, w_decode.T, preferred_element_type=jnp.float32)
    grad_upd_low = grad_upd.astype(jnp.bfloat16)
    grad_mixed = jnp.dot(grad_upd_low, w_out.T, preferred_element_type=jnp.float32)

    def backward_step(carried, block_item):
        grad_query, grad_wkey, grad_wvalue = carried
        row_feats, row_cell, valid_rows = block_item
        query_term, step_wkey, step_wvalue, row_grad = row_backward(query_low, w_key, w_value, grad_mixed, row_feats, row_cell, valid_rows, HEADS, score_scale)
        grad_query = grad_query + jax.ops.segment_sum(query_term, row_cell, num_segments=cell_count)
        return ((grad_query, grad_wkey + step_wkey, grad_wvalue + step_wvalue), row_grad)
    start_state = (jnp.zeros((cell_count, D), jnp.float32), jnp.zeros((FEAT, D), jnp.float32), jnp.zeros((FEAT, D), jnp.float32))
    (query_rows_grad, grad_wkey, grad_wvalue), row_grads = lax.scan(backward_step, start_state, row_items)
    query_disk_grad, grad_dkey, grad_dvalue = disk_backward(query_low, disk_flat, w_disk_key, w_disk_value, grad_mixed, HEADS, score_scale)
    grad_query_low = (query_rows_grad + query_disk_grad).astype(jnp.bfloat16)
    latent_grad = grad_upd + jnp.dot(grad_query_low, w_query.T, preferred_element_type=jnp.float32)
    query_full_grad = jnp.dot(lat_flat.T, grad_query_low, preferred_element_type=jnp.float32)
    out_full_grad = jnp.dot(mixed_cells.T, grad_upd_low, preferred_element_type=jnp.float32)
    return (total_loss, latent_grad.reshape(NLAT, NLON, D), row_grads.reshape(ROWS, FEAT), normalized(query_full_grad), normalized(out_full_grad), normalized(grad_wkey), normalized(grad_wvalue), normalized(grad_dkey), normalized(grad_dvalue))
```

```python
import functools
import math

import jax
import jax.numpy as jnp
import numpy as np
from jax import lax
from jax.experimental import pallas as pl
from jax.experimental.pallas import tpu as pltpu
from jax.sharding import PartitionSpec as P

HEADS = 16
CAP = 2
CHUNK = 256
F32 = jnp.float32
BF16 = jnp.bfloat16

NN = (((1,), (0,)), ((), ()))
NT = (((1,), (1,)), ((), ()))
TN = (((0,), (0,)), ((), ()))


def mm(a, b, dims=NN):
    return lax.dot_general(a, b, dims, preferred_element_type=F32)


def vmem():
    return pl.BlockSpec(memory_space=pltpu.VMEM)


def smem():
    return pl.BlockSpec(memory_space=pltpu.SMEM)


def pack_kernel(tile_ref, rows_ref, feats_ref, cells_ref, sfeats_ref, scells_ref, slot_ref, count):
    block_count, block_len = cells_ref.shape
    tile_total = sfeats_ref.shape[0] // (CAP * block_len)
    scells_ref[...] = jnp.full(scells_ref.shape, -1, jnp.int32)
    for t in range(tile_total):
        count[t] = 0
    lane = lax.broadcasted_iota(jnp.int32, (1, block_len), 1)
    for b in range(block_count):
        t = tile_ref[b]
        n = count[t]
        count[t] = n + 1
        slot = t * CAP + n
        slot_ref[b] = slot
        sfeats_ref[pl.ds(pl.multiple_of(slot * block_len, block_len), block_len), :] = feats_ref[
            b * block_len : (b + 1) * block_len, :
        ]
        scells_ref[pl.ds(slot, 1), :] = jnp.where(lane < rows_ref[b], cells_ref[b : b + 1, :], -1)


def pack(block_tile, block_rows, radiances, row_cells, lat_count):
    block_count = block_tile.shape[0]
    rows, feat = radiances.shape
    block_len = rows // block_count
    slots = lat_count * CAP
    return pl.pallas_call(
        pack_kernel,
        out_shape=(
            jax.ShapeDtypeStruct((slots * block_len, feat), BF16),
            jax.ShapeDtypeStruct((slots, block_len), jnp.int32),
            jax.ShapeDtypeStruct((block_count,), jnp.int32),
        ),
        in_specs=[smem(), smem(), vmem(), vmem()],
        out_specs=(vmem(), vmem(), smem()),
        scratch_shapes=[pltpu.SMEM((lat_count,), jnp.int32)],
        name="pack",
    )(block_tile, block_rows, radiances, row_cells.reshape(block_count, block_len))


def tile_kernel(
    weight_ref,
    feats_ref,
    cells_ref,
    lat_ref,
    disk_ref,
    target_ref,
    wq_ref,
    wkv_ref,
    wdk_ref,
    wdv_ref,
    wo_ref,
    wd_ref,
    lgrad_ref,
    rgrad_ref,
    gq_ref,
    go_ref,
    gs_ref,
    loss_ref,
    comp,
    cellb,
    kv,
    qr,
    gate,
    acc,
    gkv,
    query,
    mixed,
    gul,
    gmix,
    px,
    bkt,
    bvt,
    gdisk,
    mdisk,
    hsum,
    hspread,
    countv,
    counts,
    csem,
    osem,
):
    slots, block_len = cells_ref.shape
    cells, width = lat_ref.shape
    feat = feats_ref.shape[1]
    disks_ch = disk_ref.shape[0]
    ch = wdk_ref.shape[0]
    disks = disks_ch // ch
    hd = width // HEADS
    scale = 1.0 / math.sqrt(hd)
    out_width = target_ref.shape[1]
    hl = hsum.shape[1]
    cw = ch * HEADS
    grid_rows = cells // 128

    valid = (cells_ref[...] >= 0).astype(jnp.int32)
    countv[...] = jnp.broadcast_to(jnp.sum(valid, axis=1, keepdims=True), countv.shape)
    copy = pltpu.make_async_copy(countv, counts, csem)
    copy.start()

    hsum[...] = jnp.where(
        lax.broadcasted_iota(jnp.int32, (width, hl), 0) // hd
        == lax.broadcasted_iota(jnp.int32, (width, hl), 1),
        1.0,
        0.0,
    ).astype(BF16)
    hspread[...] = jnp.where(
        lax.broadcasted_iota(jnp.int32, (hl, width), 1) // hd
        == lax.broadcasted_iota(jnp.int32, (hl, width), 0),
        1.0,
        0.0,
    ).astype(BF16)
    comp[...] = jnp.zeros(comp.shape, BF16)
    cellb[...] = jnp.full(cellb.shape, -1, jnp.int32)

    def project(i, _):
        r = pl.ds(pl.multiple_of(i * CHUNK, CHUNK), CHUNK)
        query[r, :] = mm(lat_ref[r, :], wq_ref[...]).astype(BF16)
        return 0

    lax.fori_loop(0, cells // CHUNK, project, 0)

    spread_ch = jnp.where(
        lax.broadcasted_iota(jnp.int32, (cw, ch), 0) // HEADS
        == lax.broadcasted_iota(jnp.int32, (cw, ch), 1),
        1.0,
        0.0,
    ).astype(BF16)
    head_mask = (
        lax.broadcasted_iota(jnp.int32, (cw, width), 0) % HEADS
        == lax.broadcasted_iota(jnp.int32, (cw, width), 1) // hd
    )
    bkt[...] = jnp.where(head_mask, mm(spread_ch, wdk_ref[...]), 0.0).astype(BF16)
    bvt[...] = jnp.where(head_mask, mm(spread_ch, wdv_ref[...]), 0.0).astype(BF16)
    sum_ch = jnp.where(
        lax.broadcasted_iota(jnp.int32, (cw, hl), 0) % HEADS
        == lax.broadcasted_iota(jnp.int32, (cw, hl), 1),
        1.0,
        0.0,
    ).astype(BF16)
    qt = mm(query[...], bkt[...], NT)
    msum = jnp.zeros((cells, cw), F32)
    for k in range(disks):
        pxk = mm(
            disk_ref[k * ch : (k + 1) * ch, :], spread_ch, (((0,), (1,)), ((), ()))
        )
        px[:, k * cw : (k + 1) * cw] = pxk.astype(BF16)
        g = jax.nn.sigmoid(mm((pxk * qt).astype(BF16), sum_ch) * scale)
        gdisk[:, k * hl : (k + 1) * hl] = g
        msum = msum + mm(g.astype(BF16), sum_ch, NT) * pxk
    mdisk[...] = msum.astype(BF16)

    def disk_mix(i, _):
        r = pl.ds(pl.multiple_of(i * CHUNK, CHUNK), CHUNK)
        acc[r, :] = mm(mdisk[r, :], bvt[...])
        return 0

    lax.fori_loop(0, cells // CHUNK, disk_mix, 0)

    copy.wait()
    padded = jnp.concatenate(
        [cells_ref[...], jnp.full((block_len - slots, block_len), -1, jnp.int32)], axis=0
    )
    columns = jnp.transpose(padded.astype(F32)).astype(jnp.int32)
    row = lax.broadcasted_iota(jnp.int32, (block_len, feat), 0)
    offset = jnp.int32(0)
    for s in range(slots):
        at = pl.ds(pl.multiple_of(offset, 16), block_len)
        got = feats_ref[s * block_len : (s + 1) * block_len, :]
        comp[at, :] = jnp.where(row < counts[s, 0], got, jnp.zeros_like(got))
        cellb[at, :] = jnp.broadcast_to(columns[:, s : s + 1], (block_len, 128))
        offset = offset + ((counts[s, 0] + 15) // 16) * 16
    chunk_total = (offset + (CHUNK - 1)) // CHUNK

    lane = lax.broadcasted_iota(jnp.int32, (CHUNK, 128), 1)

    def one_hot(r):
        cb = cellb[r, :]
        return jnp.concatenate(
            [
                jnp.where(cb == lane + 128 * j, 1.0, 0.0).astype(BF16)
                for j in range(cells // 128)
            ],
            axis=1,
        )

    def forward(i, _):
        r = pl.ds(pl.multiple_of(i * CHUNK, CHUNK), CHUNK)
        f = comp[r, :]
        both = mm(f, wkv_ref[...])
        low = both.astype(BF16)
        kv[r, :] = low
        oh = one_hot(r)
        q = mm(oh, query[...]).astype(BF16)
        qr[r, :] = q
        g = jax.nn.sigmoid(mm(q * low[:, :width], hsum[...]) * scale)
        gate[r, :] = g
        term = mm(g.astype(BF16), hspread[...]).astype(BF16) * low[:, width:]
        acc[...] += mm(oh, term, TN)
        return 0

    lax.fori_loop(0, chunk_total, forward, 0)

    lat_at = lax.axis_index("lat") * grid_rows
    tile = 128

    def middle(i, loss):
        r = pl.ds(pl.multiple_of(i * tile, tile), tile)
        m = acc[r, :].astype(BF16)
        mixed[r, :] = m
        updated = (lat_ref[r, :].astype(F32) + mm(m, wo_ref[...])).astype(BF16)
        err = mm(updated, wd_ref[...]) - target_ref[r, :]
        w = weight_ref[lat_at + i]
        gp = w * err
        gu = mm(gp.astype(BF16), wd_ref[...], NT)
        lgrad_ref[r, :] = gu
        gu_low = gu.astype(BF16)
        gul[r, :] = gu_low
        gmix[r, :] = mm(gu_low, wo_ref[...], NT).astype(BF16)
        return loss + jnp.sum((0.5 * gp * err).reshape(tile // 8, 8, out_width), axis=0)

    loss_ref[...] = lax.fori_loop(0, cells // tile, middle, jnp.zeros((8, out_width), F32))

    gt = mm(gmix[...], bvt[...], NT)
    nsum = jnp.zeros((cells, cw), F32)
    for k in range(disks):
        pxk = px[:, k * cw : (k + 1) * cw].astype(F32)
        g = gdisk[:, k * hl : (k + 1) * hl]
        ds = mm((pxk * gt).astype(BF16), sum_ch) * g * (1.0 - g) * scale
        nsum = nsum + mm(ds.astype(BF16), sum_ch, NT) * pxk
    ndisk = nsum.astype(BF16)

    def disk_weight(left, right):
        full = jnp.where(head_mask, mm(left, right, TN), 0.0)
        return jnp.sum(full.reshape(ch, HEADS, width), axis=1)

    gs_ref[2 * feat : 2 * feat + ch, :] = disk_weight(ndisk, query[...]).astype(gs_ref.dtype)
    gs_ref[2 * feat + ch :, :] = disk_weight(mdisk[...], gmix[...]).astype(gs_ref.dtype)
    mdisk[...] = ndisk

    def disk_query(i, _):
        r = pl.ds(pl.multiple_of(i * CHUNK, CHUNK), CHUNK)
        acc[r, :] = mm(mdisk[r, :], bkt[...])
        return 0

    lax.fori_loop(0, cells // CHUNK, disk_query, 0)
    gkv[...] = jnp.zeros(gkv.shape, F32)

    def backward(i, _):
        r = pl.ds(pl.multiple_of(i * CHUNK, CHUNK), CHUNK)
        oh = one_hot(r)
        gm = mm(oh, gmix[...]).astype(BF16)
        g = gate[r, :]
        ds = mm(gm * kv[r, width:], hsum[...]) * g * (1.0 - g) * scale
        ds_wide = mm(ds.astype(BF16), hspread[...]).astype(BF16)
        acc[...] += mm(oh, ds_wide * kv[r, :width], TN)
        g_wide = mm(g.astype(BF16), hspread[...]).astype(BF16)
        grads = jnp.concatenate([ds_wide * qr[r, :], g_wide * gm], axis=1)
        gkv[...] += mm(comp[r, :], grads, TN)
        comp[r, :] = mm(grads, wkv_ref[...], NT).astype(BF16)
        return 0

    lax.fori_loop(0, chunk_total, backward, 0)
    gs_ref[:feat, :] = gkv[:, :width].astype(gs_ref.dtype)
    gs_ref[feat : 2 * feat, :] = gkv[:, width:].astype(gs_ref.dtype)

    offset = jnp.int32(0)
    for s in range(slots):
        at = pl.ds(pl.multiple_of(offset, 16), block_len)
        got = comp[at, :]
        rgrad_ref[s * block_len : (s + 1) * block_len, :] = jnp.where(
            row < counts[s, 0], got, jnp.zeros_like(got)
        )
        offset = offset + ((counts[s, 0] + 15) // 16) * 16

    def finish(i, _):
        r = pl.ds(pl.multiple_of(i * tile, tile), tile)
        gq = acc[r, :].astype(BF16)
        query[r, :] = gq
        lgrad_ref[r, :] += mm(gq, wq_ref[...], NT)
        return 0

    lax.fori_loop(0, cells // tile, finish, 0)

    def weights(i, _):
        at = pl.multiple_of(i * CHUNK, CHUNK)
        c = pl.ds(at, CHUNK)
        later = pl.ds(pl.multiple_of(width + i * CHUNK, CHUNK), CHUNK)
        qr[c, :] = mm(lat_ref[:, c], query[...], TN).astype(BF16)
        pltpu.make_async_copy(qr.at[c], gq_ref.at[c], osem.at[0, i]).start()
        qr[later, :] = mm(mixed[:, c], gul[...], TN).astype(BF16)
        pltpu.make_async_copy(qr.at[later], go_ref.at[c], osem.at[1, i]).start()
        return 0

    lax.fori_loop(0, width // CHUNK, weights, 0)
    for i in range(width // CHUNK):
        c = slice(i * CHUNK, (i + 1) * CHUNK)
        later = slice(width + i * CHUNK, width + (i + 1) * CHUNK)
        pltpu.make_async_copy(qr.at[c], gq_ref.at[c], osem.at[0, i]).wait()
        pltpu.make_async_copy(qr.at[later], go_ref.at[c], osem.at[1, i]).wait()


def tile_step(weight, feats, cells, lat_flat, disk, target, wq, wkv, wdk, wdv, wo, wd):
    rows, feat = feats.shape
    cell_count, width = lat_flat.shape
    ch = wdk.shape[0]
    disks = disk.shape[0] // ch
    cw = ch * HEADS
    slots = cells.shape[0]
    return pl.pallas_call(
        tile_kernel,
        out_shape=(
            jax.ShapeDtypeStruct((cell_count, width), F32),
            jax.ShapeDtypeStruct((rows, feat), BF16),
            jax.ShapeDtypeStruct((width, width), BF16),
            jax.ShapeDtypeStruct((width, width), BF16),
            jax.ShapeDtypeStruct((2 * feat + 2 * ch, width), BF16),
            jax.ShapeDtypeStruct((8, target.shape[1]), F32),
        ),
        in_specs=[smem()] + [vmem()] * 11,
        out_specs=(vmem(), vmem(), pl.BlockSpec(memory_space=pl.ANY), pl.BlockSpec(memory_space=pl.ANY), vmem(), vmem()),
        scratch_shapes=[
            pltpu.VMEM((rows, feat), BF16),
            pltpu.VMEM((rows, 128), jnp.int32),
            pltpu.VMEM((rows, 2 * width), BF16),
            pltpu.VMEM((rows, width), BF16),
            pltpu.VMEM((rows, 128), F32),
            pltpu.VMEM((cell_count, width), F32),
            pltpu.VMEM((feat, 2 * width), F32),
            pltpu.VMEM((cell_count, width), BF16),
            pltpu.VMEM((cell_count, width), BF16),
            pltpu.VMEM((cell_count, width), BF16),
            pltpu.VMEM((cell_count, width), BF16),
            pltpu.VMEM((cell_count, disks * cw), BF16),
            pltpu.VMEM((cw, width), BF16),
            pltpu.VMEM((cw, width), BF16),
            pltpu.VMEM((cell_count, disks * 128), F32),
            pltpu.VMEM((cell_count, cw), BF16),
            pltpu.VMEM((width, 128), BF16),
            pltpu.VMEM((128, width), BF16),
            pltpu.VMEM((slots, 128), jnp.int32),
            pltpu.SMEM((slots, 128), jnp.int32),
            pltpu.SemaphoreType.DMA,
            pltpu.SemaphoreType.DMA((2, width // CHUNK)),
        ],
        compiler_params=pltpu.CompilerParams(vmem_limit_bytes=62 * 1024 * 1024),
        name="tile",
    )(weight, feats, cells, lat_flat, disk, target, wq, wkv, wdk, wdv, wo, wd)


def unpack_kernel(slot_ref, got_ref, out_ref):
    block_count = slot_ref.shape[0]
    block_len = out_ref.shape[0] // block_count
    for b in range(block_count):
        out_ref[b * block_len : (b + 1) * block_len, :] = got_ref[
            pl.ds(pl.multiple_of(slot_ref[b] * block_len, block_len), block_len), :
        ]


def unpack(slots, got, rows):
    return pl.pallas_call(
        unpack_kernel,
        out_shape=jax.ShapeDtypeStruct((rows, got.shape[1]), BF16),
        in_specs=[smem(), vmem()],
        out_specs=vmem(),
        name="unpack",
    )(slots, got)


def cell_weights(row_total):
    centres = (np.arange(row_total, dtype=np.float32) + np.float32(0.5)) / np.float32(row_total)
    weight = np.cos(np.float32(math.pi / 180.0) * (np.float32(-60.0) + np.float32(120.0) * centres))
    return (weight / np.mean(weight)).astype(np.float32)


def body(
    radiances,
    block_tile,
    block_rows,
    row_cells,
    latents,
    disk_pixels,
    targets,
    w_query,
    w_key,
    w_value,
    w_disk_key,
    w_disk_value,
    w_out,
    w_decode,
):
    lat_count = lax.axis_size("lat")
    device_count = lax.axis_size(("lon", "lat"))
    rows = radiances.shape[0]
    tile_lat, tile_lon, width = latents.shape
    out_width = targets.shape[2]
    cells = tile_lat * tile_lon
    feat = radiances.shape[1]
    ch = w_disk_key.shape[0]
    sfeats, scells, slot = pack(block_tile, block_rows, radiances, row_cells, lat_count)
    got_feats = lax.all_to_all(
        sfeats.reshape(lat_count, -1, feat), "lat", split_axis=0, concat_axis=0, tiled=True
    ).reshape(sfeats.shape)
    got_cells = lax.all_to_all(
        scells.reshape(lat_count, CAP, -1), "lat", split_axis=0, concat_axis=0, tiled=True
    ).reshape(scells.shape)
    weight = jnp.asarray(cell_weights(tile_lat * lat_count))
    lgrad, rgrad, gq, go, gs, loss = tile_step(
        weight,
        got_feats,
        got_cells,
        latents.reshape(cells, width),
        disk_pixels.reshape(-1, cells),
        targets.reshape(cells, out_width),
        w_query,
        jnp.concatenate([w_key, w_value], axis=1),
        w_disk_key,
        w_disk_value,
        w_out,
        w_decode,
    )
    returned = lax.all_to_all(
        rgrad.reshape(lat_count, -1, feat), "lat", split_axis=0, concat_axis=0, tiled=True
    ).reshape(rgrad.shape)
    row_grad = unpack(slot, returned, rows)
    axes = ("lon", "lat")
    gq_share = lax.psum_scatter(gq.astype(F32), axes, scatter_dimension=0, tiled=True)
    go_share = lax.psum_scatter(go.astype(F32), axes, scatter_dimension=0, tiled=True)
    gs_sum, loss_sum, sq, so = lax.psum(
        (
            gs.astype(F32),
            jnp.sum(loss),
            jnp.sum(gq_share * gq_share),
            jnp.sum(go_share * go_share),
        ),
        axes,
    )
    entries = width * width
    small = []
    at = 0
    for n in (feat, feat, ch, ch):
        g = gs_sum[at : at + n]
        small.append(g / jnp.sqrt(jnp.mean(g * g) + 1e-06))
        at += n
    return (
        loss_sum * (1.0 / (cells * device_count * out_width)),
        lgrad.reshape(latents.shape),
        row_grad,
        gq_share / jnp.sqrt(sq / entries + 1e-06),
        go_share / jnp.sqrt(so / entries + 1e-06),
        *small,
    )


def solution(mesh):
    both = ("lon", "lat")
    placed = (
        P(both, None),
        P(both),
        P(both),
        P(both),
        P("lat", "lon", None),
        P(None, None, "lat", "lon"),
        P("lat", "lon", None),
    ) + (P(),) * 7
    return jax.shard_map(
        body,
        mesh=mesh,
        in_specs=placed,
        out_specs=(
            P(),
            P("lat", "lon", None),
            P(both, None),
            P(both, None),
            P(both, None),
            P(),
            P(),
            P(),
            P(),
        ),
        check_vma=False,
    )
```

```python
import functools
import math

import jax
import jax.numpy as jnp
import numpy as np
from jax import lax
from jax.experimental import pallas as pl
from jax.experimental.pallas import tpu as pltpu
from jax.sharding import PartitionSpec as P

HEADS = 16
CAP = 2
CHUNK = 256
F32 = jnp.float32
BF16 = jnp.bfloat16

NN = (((1,), (0,)), ((), ()))
NT = (((1,), (1,)), ((), ()))
TN = (((0,), (0,)), ((), ()))


def mm(a, b, dims=NN):
    return lax.dot_general(a, b, dims, preferred_element_type=F32)


def vmem():
    return pl.BlockSpec(memory_space=pltpu.VMEM)


def anywhere():
    return pl.BlockSpec(memory_space=pl.ANY)


def smem():
    return pl.BlockSpec(memory_space=pltpu.SMEM)


def pack_kernel(tile_ref, rows_ref, feats_ref, cells_ref, sfeats_ref, scells_ref, slot_ref, count):
    block_count, block_len = cells_ref.shape
    tile_total = scells_ref.shape[0]
    scells_ref[...] = jnp.full(scells_ref.shape, -1, jnp.int32)
    for t in range(tile_total):
        count[t] = 0
    lane = lax.broadcasted_iota(jnp.int32, (1, block_len), 1)
    for b in range(block_count):
        t = tile_ref[b]
        n = count[t]
        count[t] = n + 1
        slot = t * CAP + n
        slot_ref[b] = slot
        sfeats_ref[pl.ds(pl.multiple_of(slot * block_len, block_len), block_len), :] = feats_ref[
            b * block_len : (b + 1) * block_len, :
        ]
        scells_ref[t, pl.ds(n, 1), :] = jnp.where(lane < rows_ref[b], cells_ref[b : b + 1, :], -1)


def pack(block_tile, block_rows, radiances, row_cells, lat_count):
    block_count = block_tile.shape[0]
    rows, feat = radiances.shape
    block_len = rows // block_count
    slots = lat_count * CAP
    return pl.pallas_call(
        pack_kernel,
        out_shape=(
            jax.ShapeDtypeStruct((slots * block_len, feat), BF16),
            jax.ShapeDtypeStruct((lat_count, 8, block_len), jnp.int32),
            jax.ShapeDtypeStruct((block_count,), jnp.int32),
        ),
        in_specs=[smem(), smem(), vmem(), vmem()],
        out_specs=(vmem(), vmem(), smem()),
        scratch_shapes=[pltpu.SMEM((lat_count,), jnp.int32)],
        name="pack",
    )(block_tile, block_rows, radiances, row_cells.reshape(block_count, block_len))


def tile_kernel(
    weight_ref,
    feats_ref,
    cells_ref,
    lat_ref,
    disk_ref,
    target_ref,
    wq_ref,
    wkv_ref,
    wdk_ref,
    wdv_ref,
    wo_ref,
    wd_ref,
    lgrad_ref,
    rgrad_ref,
    gw_ref,
    gs_ref,
    loss_ref,
    comp,
    cellb,
    kv,
    qr,
    gate,
    acc,
    gkv,
    query,
    mixed,
    gul,
    gmix,
    px,
    bkt,
    bvt,
    gdisk,
    mdisk,
    hsum,
    hspread,
    countv,
    counts,
    csem,
    osem,
):
    sources, _, block_len = cells_ref.shape
    slots = sources * CAP
    cells, width = lat_ref.shape
    feat = feats_ref.shape[1]
    disks_ch = disk_ref.shape[0]
    ch = wdk_ref.shape[0]
    disks = disks_ch // ch
    hd = width // HEADS
    scale = 1.0 / math.sqrt(hd)
    out_width = target_ref.shape[1]
    hl = hsum.shape[1]
    cw = ch * HEADS
    grid_rows = cells // 128

    def place(s):
        return (s // CAP) * 8 + s % CAP

    got_cells = cells_ref[...].reshape(sources * 8, block_len)
    valid = (got_cells >= 0).astype(jnp.int32)
    countv[...] = jnp.broadcast_to(jnp.sum(valid, axis=1, keepdims=True), countv.shape)
    copy = pltpu.make_async_copy(countv, counts, csem)
    copy.start()

    hsum[...] = jnp.where(
        lax.broadcasted_iota(jnp.int32, (width, hl), 0) // hd
        == lax.broadcasted_iota(jnp.int32, (width, hl), 1),
        1.0,
        0.0,
    ).astype(BF16)
    hspread[...] = jnp.where(
        lax.broadcasted_iota(jnp.int32, (hl, width), 1) // hd
        == lax.broadcasted_iota(jnp.int32, (hl, width), 0),
        1.0,
        0.0,
    ).astype(BF16)
    comp[...] = jnp.zeros(comp.shape, BF16)
    cellb[...] = jnp.full(cellb.shape, -1, jnp.int32)

    def project(i, _):
        r = pl.ds(pl.multiple_of(i * CHUNK, CHUNK), CHUNK)
        query[r, :] = mm(lat_ref[r, :], wq_ref[...]).astype(BF16)
        return 0

    lax.fori_loop(0, cells // CHUNK, project, 0)

    spread_ch = jnp.where(
        lax.broadcasted_iota(jnp.int32, (cw, ch), 0) // HEADS
        == lax.broadcasted_iota(jnp.int32, (cw, ch), 1),
        1.0,
        0.0,
    ).astype(BF16)
    head_mask = (
        lax.broadcasted_iota(jnp.int32, (cw, width), 0) % HEADS
        == lax.broadcasted_iota(jnp.int32, (cw, width), 1) // hd
    )
    bkt[...] = jnp.where(head_mask, mm(spread_ch, wdk_ref[...]), 0.0).astype(BF16)
    bvt[...] = jnp.where(head_mask, mm(spread_ch, wdv_ref[...]), 0.0).astype(BF16)
    sum_ch = jnp.where(
        lax.broadcasted_iota(jnp.int32, (cw, hl), 0) % HEADS
        == lax.broadcasted_iota(jnp.int32, (cw, hl), 1),
        1.0,
        0.0,
    ).astype(BF16)
    qt = mm(query[...], bkt[...], NT)
    msum = jnp.zeros((cells, cw), F32)
    for k in range(disks):
        pxk = mm(
            disk_ref[k * ch : (k + 1) * ch, :], spread_ch, (((0,), (1,)), ((), ()))
        )
        px[:, k * cw : (k + 1) * cw] = pxk.astype(BF16)
        g = jax.nn.sigmoid(mm((pxk * qt).astype(BF16), sum_ch) * scale)
        gdisk[:, k * hl : (k + 1) * hl] = g
        msum = msum + mm(g.astype(BF16), sum_ch, NT) * pxk
    mdisk[...] = msum.astype(BF16)

    def disk_mix(i, _):
        r = pl.ds(pl.multiple_of(i * CHUNK, CHUNK), CHUNK)
        acc[r, :] = mm(mdisk[r, :], bvt[...])
        return 0

    lax.fori_loop(0, cells // CHUNK, disk_mix, 0)

    copy.wait()
    columns = jnp.transpose(got_cells.astype(F32)).astype(jnp.int32)
    row = lax.broadcasted_iota(jnp.int32, (block_len, feat), 0)
    offset = jnp.int32(0)
    for s in range(slots):
        at = pl.ds(pl.multiple_of(offset, 16), block_len)
        got = feats_ref[s * block_len : (s + 1) * block_len, :]
        comp[at, :] = jnp.where(row < counts[place(s), 0], got, jnp.zeros_like(got))
        cellb[at, :] = jnp.broadcast_to(columns[:, place(s) : place(s) + 1], (block_len, 128))
        offset = offset + ((counts[place(s), 0] + 15) // 16) * 16
    chunk_total = (offset + (CHUNK - 1)) // CHUNK

    lane = lax.broadcasted_iota(jnp.int32, (CHUNK, 128), 1)

    def one_hot(r):
        cb = cellb[r, :]
        return jnp.concatenate(
            [
                jnp.where(cb == lane + 128 * j, 1.0, 0.0).astype(BF16)
                for j in range(cells // 128)
            ],
            axis=1,
        )

    def forward(i, _):
        r = pl.ds(pl.multiple_of(i * CHUNK, CHUNK), CHUNK)
        f = comp[r, :]
        both = mm(f, wkv_ref[...])
        low = both.astype(BF16)
        kv[r, :] = low
        oh = one_hot(r)
        q = mm(oh, query[...]).astype(BF16)
        qr[pl.ds(pl.multiple_of(i * (CHUNK // 16), CHUNK // 16), CHUNK // 16)] = q.reshape(
            CHUNK // 16, 16, width
        )
        g = jax.nn.sigmoid(mm(q * low[:, :width], hsum[...]) * scale)
        gate[r, :] = g
        term = mm(g.astype(BF16), hspread[...]).astype(BF16) * low[:, width:]
        acc[...] += mm(oh, term, TN)
        return 0

    lax.fori_loop(0, chunk_total, forward, 0)

    lat_at = lax.axis_index("lat") * grid_rows
    tile = 128

    def middle(i, loss):
        r = pl.ds(pl.multiple_of(i * tile, tile), tile)
        m = acc[r, :].astype(BF16)
        mixed[r, :] = m
        updated = (lat_ref[r, :].astype(F32) + mm(m, wo_ref[...])).astype(BF16)
        err = mm(updated, wd_ref[...]) - target_ref[r, :]
        w = weight_ref[lat_at + i]
        gp = w * err
        gu = mm(gp.astype(BF16), wd_ref[...], NT)
        lgrad_ref[r, :] = gu
        gu_low = gu.astype(BF16)
        gul[r, :] = gu_low
        gmix[r, :] = mm(gu_low, wo_ref[...], NT).astype(BF16)
        return loss + jnp.sum((0.5 * gp * err).reshape(tile // 8, 8, out_width), axis=0)

    loss_ref[...] = lax.fori_loop(0, cells // tile, middle, jnp.zeros((8, out_width), F32))

    gt = mm(gmix[...], bvt[...], NT)
    nsum = jnp.zeros((cells, cw), F32)
    for k in range(disks):
        pxk = px[:, k * cw : (k + 1) * cw].astype(F32)
        g = gdisk[:, k * hl : (k + 1) * hl]
        ds = mm((pxk * gt).astype(BF16), sum_ch) * g * (1.0 - g) * scale
        nsum = nsum + mm(ds.astype(BF16), sum_ch, NT) * pxk
    ndisk = nsum.astype(BF16)

    def disk_weight(left, right):
        full = jnp.where(head_mask, mm(left, right, TN), 0.0)
        return jnp.sum(full.reshape(ch, HEADS, width), axis=1)

    def small_out(at, value):
        low = value.astype(gs_ref.dtype)
        for j in range(gs_ref.shape[0]):
            gs_ref[j, at : at + value.shape[0], :] = low[:, j * 128 : (j + 1) * 128]

    small_out(2 * feat, disk_weight(ndisk, query[...]))
    small_out(2 * feat + ch, disk_weight(mdisk[...], gmix[...]))
    mdisk[...] = ndisk

    def disk_query(i, _):
        r = pl.ds(pl.multiple_of(i * CHUNK, CHUNK), CHUNK)
        acc[r, :] = mm(mdisk[r, :], bkt[...])
        return 0

    lax.fori_loop(0, cells // CHUNK, disk_query, 0)
    gkv[...] = jnp.zeros(gkv.shape, F32)

    def backward(i, _):
        r = pl.ds(pl.multiple_of(i * CHUNK, CHUNK), CHUNK)
        oh = one_hot(r)
        gm = mm(oh, gmix[...]).astype(BF16)
        g = gate[r, :]
        ds = mm(gm * kv[r, width:], hsum[...]) * g * (1.0 - g) * scale
        ds_wide = mm(ds.astype(BF16), hspread[...]).astype(BF16)
        acc[...] += mm(oh, ds_wide * kv[r, :width], TN)
        g_wide = mm(g.astype(BF16), hspread[...]).astype(BF16)
        q = qr[pl.ds(pl.multiple_of(i * (CHUNK // 16), CHUNK // 16), CHUNK // 16)]
        grads = jnp.concatenate([ds_wide * q.reshape(CHUNK, width), g_wide * gm], axis=1)
        gkv[...] += mm(comp[r, :], grads, TN)
        comp[r, :] = mm(grads, wkv_ref[...], NT).astype(BF16)
        return 0

    lax.fori_loop(0, chunk_total, backward, 0)
    small_out(0, gkv[:, :width])
    small_out(feat, gkv[:, width:])

    offset = jnp.int32(0)
    for s in range(slots):
        at = pl.ds(pl.multiple_of(offset, 16), block_len)
        got = comp[at, :]
        rgrad_ref[s * block_len : (s + 1) * block_len, :] = jnp.where(
            row < counts[place(s), 0], got, jnp.zeros_like(got)
        )
        offset = offset + ((counts[place(s), 0] + 15) // 16) * 16

    def finish(i, _):
        r = pl.ds(pl.multiple_of(i * tile, tile), tile)
        gq = acc[r, :].astype(BF16)
        query[r, :] = gq
        lgrad_ref[r, :] += mm(gq, wq_ref[...], NT)
        return 0

    lax.fori_loop(0, cells // tile, finish, 0)

    half = gw_ref.shape[1] // 2
    slabs = CHUNK // half

    def out_copy(i):
        part = pl.ds(pl.multiple_of(i * slabs, slabs), slabs)
        return pltpu.make_async_copy(stage.at[part], gw_ref.at[part], osem.at[i])

    def weights(i, _):
        c = pl.ds(pl.multiple_of(i * CHUNK, CHUNK), CHUNK)
        gq = mm(lat_ref[:, c], query[...], TN).reshape(slabs, half, width)
        go = mm(mixed[:, c], gul[...], TN).reshape(slabs, half, width)
        part = pl.ds(pl.multiple_of(i * slabs, slabs), slabs)
        stage[part] = jnp.concatenate([gq, go], axis=1).astype(BF16)
        out_copy(i).start()
        return 0

    stage = qr.at[: gw_ref.shape[0]]
    lax.fori_loop(0, width // CHUNK, weights, 0)
    for i in range(width // CHUNK):
        out_copy(i).wait()


def tile_step(devices, weight, feats, cells, lat_flat, disk, target, wq, wkv, wdk, wdv, wo, wd):
    rows, feat = feats.shape
    cell_count, width = lat_flat.shape
    ch = wdk.shape[0]
    disks = disk.shape[0] // ch
    cw = ch * HEADS
    sources = cells.shape[0]
    return pl.pallas_call(
        tile_kernel,
        out_shape=(
            jax.ShapeDtypeStruct((cell_count, width), F32),
            jax.ShapeDtypeStruct((rows, feat), BF16),
            jax.ShapeDtypeStruct((devices, 2 * width // devices, width), BF16),
            jax.ShapeDtypeStruct((width // 128, 2 * feat + 2 * ch, 128), BF16),
            jax.ShapeDtypeStruct((8, target.shape[1]), F32),
        ),
        in_specs=[smem()] + [vmem()] * 11,
        out_specs=(vmem(), vmem(), anywhere(), vmem(), vmem()),
        scratch_shapes=[
            pltpu.VMEM((rows, feat), BF16),
            pltpu.VMEM((rows, 128), jnp.int32),
            pltpu.VMEM((rows, 2 * width), BF16),
            pltpu.VMEM((rows // 16, 16, width), BF16),
            pltpu.VMEM((rows, 128), F32),
            pltpu.VMEM((cell_count, width), F32),
            pltpu.VMEM((feat, 2 * width), F32),
            pltpu.VMEM((cell_count, width), BF16),
            pltpu.VMEM((cell_count, width), BF16),
            pltpu.VMEM((cell_count, width), BF16),
            pltpu.VMEM((cell_count, width), BF16),
            pltpu.VMEM((cell_count, disks * cw), BF16),
            pltpu.VMEM((cw, width), BF16),
            pltpu.VMEM((cw, width), BF16),
            pltpu.VMEM((cell_count, disks * 128), F32),
            pltpu.VMEM((cell_count, cw), BF16),
            pltpu.VMEM((width, 128), BF16),
            pltpu.VMEM((128, width), BF16),
            pltpu.VMEM((8 * sources, 128), jnp.int32),
            pltpu.SMEM((8 * sources, 128), jnp.int32),
            pltpu.SemaphoreType.DMA,
            pltpu.SemaphoreType.DMA((width // CHUNK,)),
        ],
        compiler_params=pltpu.CompilerParams(vmem_limit_bytes=62 * 1024 * 1024),
        name="tile",
    )(weight, feats, cells, lat_flat, disk, target, wq, wkv, wdk, wdv, wo, wd)


SIDE = 4


def lat_peer(p, k):
    y = lax.rem(p // SIDE + k // SIDE, SIDE)
    z = lax.rem(p % SIDE + k % SIDE, SIDE)
    return y * SIDE + z


def loop(count, step, start=0):
    def run(i, carry):
        step(i)
        return carry

    lax.fori_loop(start, count, run, 0)


def send_kernel(feats_ref, cells_ref, got_ref, gcells_ref, fsend, frecv, csend, crecv, local):
    lats = cells_ref.shape[0]
    p = lax.axis_index("lat")
    barrier = pltpu.get_barrier_semaphore()

    def greet(k):
        pl.semaphore_signal(
            barrier, inc=1, device_id={"lat": lat_peer(p, k)}, device_id_type=pl.DeviceIdType.MESH
        )

    loop(lats, greet, 1)
    own = pltpu.make_async_copy(feats_ref.at[p], got_ref.at[p], local.at[0])
    own.start()
    own_cells = pltpu.make_async_copy(cells_ref.at[p], gcells_ref.at[p], local.at[1])
    own_cells.start()
    pl.semaphore_wait(barrier, lats - 1)

    def feats_copy(k):
        to = lat_peer(p, k)
        return pltpu.make_async_remote_copy(
            src_ref=feats_ref.at[to],
            dst_ref=got_ref.at[p],
            send_sem=fsend.at[k],
            recv_sem=frecv.at[k],
            device_id={"lat": to},
            device_id_type=pl.DeviceIdType.MESH,
        )

    def cells_copy(k):
        to = lat_peer(p, k)
        return pltpu.make_async_remote_copy(
            src_ref=cells_ref.at[to],
            dst_ref=gcells_ref.at[p],
            send_sem=csend.at[k],
            recv_sem=crecv.at[k],
            device_id={"lat": to},
            device_id_type=pl.DeviceIdType.MESH,
        )

    def begin(k):
        feats_copy(k).start()
        cells_copy(k).start()

    def end(k):
        feats_copy(k).wait()
        cells_copy(k).wait()

    loop(lats, begin, 1)
    own.wait()
    own_cells.wait()
    loop(lats, end, 1)


def send_rows(feats, cells):
    lats = cells.shape[0]
    dma = pltpu.SemaphoreType.DMA
    return pl.pallas_call(
        send_kernel,
        out_shape=(
            jax.ShapeDtypeStruct(feats.shape, feats.dtype),
            jax.ShapeDtypeStruct(cells.shape, cells.dtype),
        ),
        in_specs=[anywhere(), anywhere()],
        out_specs=(anywhere(), anywhere()),
        scratch_shapes=[dma((lats,))] * 4 + [dma((2,))],
        compiler_params=pltpu.CompilerParams(collective_id=1, has_side_effects=True),
        name="send_rows",
    )(feats, cells)


def reduce_kernel(
    wide_a,
    gw_ref,
    gs_ref,
    loss_ref,
    rgrad_ref,
    share_ref,
    small_ref,
    stat_ref,
    back_ref,
    s1,
    r1,
    sg1,
    rg1,
    s2a,
    r2a,
    s2b,
    r2b,
    sg2,
    rg2,
    r3a,
    r3b,
    rg3,
    sg3,
    g4,
    t4,
    t5,
    mine,
    plane,
    local,
    s_core,
    r_core,
    s_back,
    r_back,
    s_a2,
    r_a2,
    s_g2,
    r_g2,
    s_b2,
    r_b2,
    s_a3,
    r_a3,
    s_b3,
    r_b3,
    s_g3,
    r_g3,
    s_g4,
    r_g4,
    s_t4,
    r_t4,
    s_g5,
    r_g5,
    s_t5,
    r_t5,
):
    xs, cores, lats, slab, width = gw_ref.shape
    lons = xs * cores
    lon = lax.axis_index("lon")
    p = lax.axis_index("lat")
    x, c = lon // cores, lon % cores
    other = 1 - c
    rest = pl.ds(wide_a, width - wide_a)
    first = pl.ds(0, wide_a)
    piece = g4.shape[1]
    pieces = small_ref.shape[1]
    blocks = lats // SIDE

    def to_lon(target, src, dst, ssem, rsem):
        return pltpu.make_async_remote_copy(
            src_ref=src,
            dst_ref=dst,
            send_sem=ssem,
            recv_sem=rsem,
            device_id={"lon": target},
            device_id_type=pl.DeviceIdType.MESH,
        )

    def to_lat(target, src, dst, ssem, rsem):
        return pltpu.make_async_remote_copy(
            src_ref=src,
            dst_ref=dst,
            send_sem=ssem,
            recv_sem=rsem,
            device_id={"lat": target},
            device_id_type=pl.DeviceIdType.MESH,
        )

    def x_peer(k):
        return lax.rem(x + k, xs)

    barrier = pltpu.get_barrier_semaphore()

    def greet_lat(k):
        pl.semaphore_signal(
            barrier, inc=1, device_id={"lat": lat_peer(p, k)}, device_id_type=pl.DeviceIdType.MESH
        )

    def greet_lon(k):
        pl.semaphore_signal(
            barrier, inc=1, device_id={"lon": lax.rem(lon + k, lons)}, device_id_type=pl.DeviceIdType.MESH
        )

    loop(lats, greet_lat, 1)
    loop(lons, greet_lon, 1)

    def own_copy(j):
        return pltpu.make_async_copy(gw_ref.at[j, c], s1.at[j], local.at[j])

    loop(xs, lambda j: own_copy(j).start())
    own_small = pltpu.make_async_copy(gs_ref.at[:, c], sg1, local.at[xs])
    own_small.start()
    own_back = pltpu.make_async_copy(rgrad_ref.at[p], back_ref.at[p], local.at[xs + 1])
    own_back.start()
    pl.semaphore_wait(barrier, lats + lons - 2)

    mate = x * cores + other

    def core_copy(k):
        j = x_peer(k)
        return to_lon(mate, gw_ref.at[j, other], r1.at[j], s_core.at[k], r_core.at[k])

    core_small = to_lon(mate, gs_ref.at[:, other], rg1, s_core.at[xs], r_core.at[xs])
    loop(xs, lambda k: core_copy(k).start(), 1)
    core_small.start()
    core_copy(0).start()

    def back_copy(k):
        to = lat_peer(p, k)
        return to_lat(to, rgrad_ref.at[to], back_ref.at[p], s_back.at[k], r_back.at[k])

    loop(lats, lambda k: back_copy(k).start(), 1)

    def a2_copy(k):
        j = x_peer(k)
        return to_lon(
            j * cores + c, s1.at[j, :, :, first], r2a.at[k - 1], s_a2.at[k], r_a2.at[k]
        )

    def g2_copy(k):
        j = x_peer(k)
        return to_lon(j * cores + c, sg1.at[j], rg2.at[k - 1], s_g2.at[k], r_g2.at[k])

    def b2_copy(k):
        to = lat_peer(p, k)
        return to_lat(to, s1.at[:, to, :, rest], r2b.at[k - 1], s_b2.at[k], r_b2.at[k])

    def add_core(j):
        def step(i):
            at = pl.ds(i * SIDE, SIDE)
            s1[j, at] = s1[j, at] + r1[j, at]

        loop(blocks, step)

    def core_step(k):
        j = x_peer(k)
        own_copy(j).wait()
        core_copy(k).wait_recv()
        add_core(j)
        a2_copy(k).start()

    loop(xs, core_step, 1)
    own_small.wait()
    core_small.wait_recv()
    sg1[...] = sg1[...] + rg1[...]
    loop(xs, lambda k: g2_copy(k).start(), 1)
    own_copy(x).wait()
    core_copy(0).wait_recv()
    add_core(x)
    loop(lats, lambda k: b2_copy(k).start(), 1)

    loop(xs, lambda k: a2_copy(k).wait_recv(), 1)
    loop(xs, lambda k: g2_copy(k).wait_recv(), 1)

    def a3_copy(k):
        to = lat_peer(p, k)
        return to_lat(to, s2a.at[to], r3a.at[k - 1], s_a3.at[k], r_a3.at[k])

    def g3_copy(k):
        to = lat_peer(p, k)
        return to_lat(to, sg2.at[to], rg3.at[k - 1], s_g3.at[k], r_g3.at[k])

    def b3_copy(k):
        j = x_peer(k)
        return to_lon(j * cores + c, s2b.at[j], r3b.at[k - 1], s_b3.at[k], r_b3.at[k])

    total = sg1[x].astype(F32)
    for k in range(xs - 1):
        total = total + rg2[k].astype(F32)
    sg2[...] = jnp.zeros(sg2.shape, BF16)
    sg2[:pieces] = total.astype(BF16).reshape(pieces, piece, total.shape[1])

    def sum_a(i):
        value = s1[x, i, :, :wide_a].astype(F32)
        for k in range(xs - 1):
            value = value + r2a[k, i].astype(F32)
        s2a[i] = value.astype(BF16)

    loop(lats, sum_a)
    loop(lats, lambda k: a3_copy(k).start(), 1)
    loop(lats, lambda k: g3_copy(k).start(), 1)
    loop(lats, lambda k: b2_copy(k).wait_recv(), 1)

    def sum_b(j):
        def add(k, value):
            return value + r2b[k, j].astype(F32)

        s2b[j] = lax.fori_loop(0, lats - 1, add, s1[j, p, :, wide_a:].astype(F32)).astype(BF16)

    loop(xs, sum_b)
    loop(xs, lambda k: b3_copy(k).start(), 1)

    loop(lats, lambda k: g3_copy(k).wait_recv(), 1)

    def add_small(k, value):
        return value + rg3[k].astype(F32)

    sg3[...] = lax.fori_loop(0, lats - 1, add_small, sg2[p].astype(F32)).astype(BF16)
    g4[p] = sg3[...]

    def g4_copy(k):
        return to_lat(lat_peer(p, k), sg3, g4.at[p], s_g4.at[k], r_g4.at[k])

    loop(lats, lambda k: g4_copy(k).start(), 1)
    loop(lats, lambda k: a3_copy(k).wait_recv(), 1)

    def add_share(k, value):
        return value + r3a[k].astype(F32)

    share_a = lax.fori_loop(0, lats - 1, add_share, s2a[p].astype(F32))
    loop(xs, lambda k: b3_copy(k).wait_recv(), 1)
    share_b = s2b[x].astype(F32)
    for k in range(xs - 1):
        share_b = share_b + r3b[k].astype(F32)
    share_ref[:, :wide_a] = share_a
    share_ref[:, wide_a:] = share_b
    half = slab // 2

    def lane_sums(value):
        value = jnp.sum(value, axis=0, keepdims=True)
        total = value[:, :128]
        for j in range(1, value.shape[1] // 128):
            total = total + value[:, j * 128 : (j + 1) * 128]
        return total

    square = jnp.concatenate([share_a * share_a, share_b * share_b], axis=1)
    row = lax.broadcasted_iota(jnp.int32, mine.shape, 0)
    mine[...] = jnp.where(
        row == 0,
        lane_sums(loss_ref[...]),
        jnp.where(
            row == 1,
            lane_sums(square[:half]),
            jnp.where(row == 2, lane_sums(square[half:]), 0.0),
        ),
    )

    def t4_copy(k):
        return to_lat(lat_peer(p, k), mine, t4.at[k - 1], s_t4.at[k], r_t4.at[k])

    loop(lats, lambda k: t4_copy(k).start(), 1)

    loop(lats, lambda k: g4_copy(k).wait_recv(), 1)

    def g5_copy(k):
        return to_lon(
            lax.rem(lon + k, lons), g4.at[pl.ds(0, pieces)], small_ref.at[lon], s_g5.at[k], r_g5.at[k]
        )

    loop(lons, lambda k: g5_copy(k).start(), 1)
    small_ref[lon] = g4[:pieces]
    loop(lats, lambda k: t4_copy(k).wait_recv(), 1)
    plane[...] = lax.fori_loop(0, lats - 1, lambda k, value: value + t4[k], mine[...])

    def t5_copy(k):
        return to_lon(lax.rem(lon + k, lons), plane, t5.at[k - 1], s_t5.at[k], r_t5.at[k])

    loop(lons, lambda k: t5_copy(k).start(), 1)
    loop(lons, lambda k: t5_copy(k).wait_recv(), 1)
    stat_ref[...] = lax.fori_loop(0, lons - 1, lambda k, value: value + t5[k], plane[...])
    loop(lons, lambda k: g5_copy(k).wait_recv(), 1)
    own_back.wait()
    loop(lats, lambda k: back_copy(k).wait_recv(), 1)

    loop(xs, lambda k: core_copy(k).wait_send())
    core_small.wait_send()

    def sent_x(k):
        a2_copy(k).wait_send()
        g2_copy(k).wait_send()
        b3_copy(k).wait_send()

    loop(xs, sent_x, 1)

    def sent_lat(k):
        back_copy(k).wait_send()
        b2_copy(k).wait_send()
        a3_copy(k).wait_send()
        g3_copy(k).wait_send()
        g4_copy(k).wait_send()
        t4_copy(k).wait_send()

    loop(lats, sent_lat, 1)

    def sent_lon(k):
        g5_copy(k).wait_send()
        t5_copy(k).wait_send()

    loop(lons, sent_lon, 1)


def reduce_all(gw, gs, loss, rgrad):
    xs, cores, lats, slab, width = gw.shape
    lons = xs * cores
    small_rows = gs.shape[2]
    piece = 32
    pieces = small_rows // piece
    wide_a = 640
    wide_b = width - wide_a
    dma = pltpu.SemaphoreType.DMA

    def buf(*shape, dtype=BF16):
        return pltpu.VMEM(shape, dtype)

    pairs = [xs + 1, lats, xs, xs, lats, lats, xs, lats, lats, lats, lons, lons]
    return pl.pallas_call(
        functools.partial(reduce_kernel, wide_a),
        out_shape=(
            jax.ShapeDtypeStruct((slab, width), F32),
            jax.ShapeDtypeStruct((lons, pieces, piece, 128), BF16),
            jax.ShapeDtypeStruct((8, 128), F32),
            jax.ShapeDtypeStruct(rgrad.shape, BF16),
        ),
        in_specs=[anywhere(), vmem(), vmem(), anywhere()],
        out_specs=(vmem(), vmem(), vmem(), anywhere()),
        scratch_shapes=[
            buf(xs, lats, slab, width),
            buf(xs, lats, slab, width),
            buf(xs, small_rows, 128),
            buf(xs, small_rows, 128),
            buf(lats, slab, wide_a),
            buf(xs - 1, lats, slab, wide_a),
            buf(xs, slab, wide_b),
            buf(lats - 1, xs, slab, wide_b),
            buf(lats, piece, 128),
            buf(xs - 1, small_rows, 128),
            buf(lats - 1, slab, wide_a),
            buf(xs - 1, slab, wide_b),
            buf(lats - 1, piece, 128),
            buf(piece, 128),
            buf(lats, piece, 128),
            buf(lats - 1, 8, 128, dtype=F32),
            buf(lons - 1, 8, 128, dtype=F32),
            buf(8, 128, dtype=F32),
            buf(8, 128, dtype=F32),
            dma((xs + 2,)),
        ]
        + [dma((n,)) for n in pairs for _ in range(2)],
        compiler_params=pltpu.CompilerParams(
            collective_id=2, has_side_effects=True, vmem_limit_bytes=40 * 1024 * 1024
        ),
        name="reduce_all",
    )(gw, gs, loss, rgrad)


def finish_kernel(
    loss_scale,
    slot_ref,
    got_ref,
    share_ref,
    small_ref,
    stat_ref,
    out_ref,
    query_ref,
    wout_ref,
    key_ref,
    value_ref,
    dkey_ref,
    dvalue_ref,
    loss_ref,
):
    block_count = slot_ref.shape[0]
    block_len = out_ref.shape[0] // block_count
    half, width = query_ref.shape
    for b in range(block_count):
        out_ref[b * block_len : (b + 1) * block_len, :] = got_ref[
            pl.ds(pl.multiple_of(slot_ref[b] * block_len, block_len), block_len), :
        ]

    loss_ref[...] = jnp.sum(stat_ref[0:1, :], axis=1, keepdims=True) * loss_scale

    def scale(total, entries):
        return 1.0 / jnp.sqrt(total / entries + 1e-06)

    def whole(value):
        return jnp.sum(jnp.sum(value, axis=0, keepdims=True), axis=1, keepdims=True)

    query_ref[...] = share_ref[:half] * scale(whole(stat_ref[1:2, :]), width * width)
    wout_ref[...] = share_ref[half:] * scale(whole(stat_ref[2:3, :]), width * width)
    lons, pieces, piece, lanes = small_ref.shape
    sums = jnp.concatenate(
        [small_ref[j].reshape(pieces * piece, lanes).astype(F32) for j in range(lons)], axis=1
    )
    at = 0
    for ref in (key_ref, value_ref, dkey_ref, dvalue_ref):
        n = ref.shape[0]
        g = sums[at : at + n]
        ref[...] = g * scale(whole(g * g), n * width)
        at += n


def finish(loss_scale, slots, got, share, small, stat, rows, feat, ch):
    width = share.shape[1]
    half = share.shape[0] // 2
    shapes = [
        ((rows, got.shape[1]), BF16),
        ((half, width), F32),
        ((half, width), F32),
        ((feat, width), F32),
        ((feat, width), F32),
        ((ch, width), F32),
        ((ch, width), F32),
        ((1, 1), F32),
    ]
    return pl.pallas_call(
        functools.partial(finish_kernel, loss_scale),
        out_shape=tuple(jax.ShapeDtypeStruct(s, d) for s, d in shapes),
        in_specs=[smem()] + [vmem()] * 4,
        out_specs=(vmem(),) * len(shapes),
        compiler_params=pltpu.CompilerParams(vmem_limit_bytes=32 * 1024 * 1024),
        name="finish",
    )(slots, got, share, small, stat)


def cell_weights(row_total):
    centres = (np.arange(row_total, dtype=np.float32) + np.float32(0.5)) / np.float32(row_total)
    weight = np.cos(np.float32(math.pi / 180.0) * (np.float32(-60.0) + np.float32(120.0) * centres))
    return (weight / np.mean(weight)).astype(np.float32)


def body(
    radiances,
    block_tile,
    block_rows,
    row_cells,
    latents,
    disk_pixels,
    targets,
    w_query,
    w_key,
    w_value,
    w_disk_key,
    w_disk_value,
    w_out,
    w_decode,
):
    lat_count = lax.axis_size("lat")
    device_count = lax.axis_size(("lon", "lat"))
    rows = radiances.shape[0]
    tile_lat, tile_lon, width = latents.shape
    out_width = targets.shape[2]
    cells = tile_lat * tile_lon
    feat = radiances.shape[1]
    ch = w_disk_key.shape[0]
    sfeats, scells, slot = pack(block_tile, block_rows, radiances, row_cells, lat_count)
    got_feats, got_cells = send_rows(sfeats.reshape(lat_count, -1, feat), scells)
    weight = jnp.asarray(cell_weights(tile_lat * lat_count))
    lgrad, rgrad, gw, gs, loss = tile_step(
        device_count,
        weight,
        got_feats.reshape(-1, feat),
        got_cells,
        latents.reshape(cells, width),
        disk_pixels.reshape(-1, cells),
        targets.reshape(cells, out_width),
        w_query,
        jnp.concatenate([w_key, w_value], axis=1),
        w_disk_key,
        w_disk_value,
        w_out,
        w_decode,
    )
    cores = 2
    xs = lax.axis_size("lon") // cores
    share, small, stat, returned = reduce_all(
        gw.reshape((xs, cores, lat_count) + gw.shape[1:]),
        gs.reshape((xs, cores) + gs.shape[1:]),
        loss,
        rgrad.reshape(lat_count, -1, feat),
    )
    row_grad, query, out, key, value, dkey, dvalue, total = finish(
        1.0 / (cells * device_count * out_width),
        slot,
        returned.reshape(-1, feat),
        share,
        small,
        stat,
        rows,
        feat,
        ch,
    )
    return (
        total.reshape(()),
        lgrad.reshape(latents.shape),
        row_grad,
        query,
        out,
        key,
        value,
        dkey,
        dvalue,
    )


def solution(mesh):
    both = ("lon", "lat")
    placed = (
        P(both, None),
        P(both),
        P(both),
        P(both),
        P("lat", "lon", None),
        P(None, None, "lat", "lon"),
        P("lat", "lon", None),
    ) + (P(),) * 7
    return jax.shard_map(
        body,
        mesh=mesh,
        in_specs=placed,
        out_specs=(
            P(),
            P("lat", "lon", None),
            P(both, None),
            P(both, None),
            P(both, None),
            P(),
            P(),
            P(),
            P(),
        ),
        check_vma=False,
    )
```

```python
import functools
import math

import jax
import jax.numpy as jnp
import numpy as np
from jax import lax
from jax.experimental import pallas as pl
from jax.experimental.pallas import tpu as pltpu
from jax.sharding import PartitionSpec as P

HEADS = 16
CAP = 2
CHUNK = 256
F32 = jnp.float32
BF16 = jnp.bfloat16

NN = (((1,), (0,)), ((), ()))
NT = (((1,), (1,)), ((), ()))
TN = (((0,), (0,)), ((), ()))


def mm(a, b, dims=NN):
    return lax.dot_general(a, b, dims, preferred_element_type=F32)


def vmem():
    return pl.BlockSpec(memory_space=pltpu.VMEM)


def anywhere():
    return pl.BlockSpec(memory_space=pl.ANY)


def smem():
    return pl.BlockSpec(memory_space=pltpu.SMEM)


def head_match(cw, width, hd):
    return (
        lax.broadcasted_iota(jnp.int32, (cw, width), 0) % HEADS
        == lax.broadcasted_iota(jnp.int32, (cw, width), 1) // hd
    )


def channel_sum(cw, lanes):
    return jnp.where(
        lax.broadcasted_iota(jnp.int32, (cw, lanes), 0) % HEADS
        == lax.broadcasted_iota(jnp.int32, (cw, lanes), 1),
        1.0,
        0.0,
    ).astype(BF16)


def pack_kernel(tile_ref, rows_ref, feats_ref, cells_ref, sfeats_ref, scells_ref, slot_ref, count):
    block_count, block_len = cells_ref.shape
    tile_total = scells_ref.shape[0]
    scells_ref[...] = jnp.full(scells_ref.shape, -1, jnp.int32)
    for t in range(tile_total):
        count[t] = 0
    lane = lax.broadcasted_iota(jnp.int32, (1, block_len), 1)
    for b in range(block_count):
        t = tile_ref[b]
        n = count[t]
        count[t] = n + 1
        slot = t * CAP + n
        slot_ref[b] = slot
        sfeats_ref[pl.ds(pl.multiple_of(slot * block_len, block_len), block_len), :] = feats_ref[
            b * block_len : (b + 1) * block_len, :
        ]
        scells_ref[t, pl.ds(n, 1), :] = jnp.where(lane < rows_ref[b], cells_ref[b : b + 1, :], -1)


def pack(block_tile, block_rows, radiances, row_cells, lat_count):
    block_count = block_tile.shape[0]
    rows, feat = radiances.shape
    block_len = rows // block_count
    slots = lat_count * CAP
    return pl.pallas_call(
        pack_kernel,
        out_shape=(
            jax.ShapeDtypeStruct((slots * block_len, feat), BF16),
            jax.ShapeDtypeStruct((lat_count, 8, block_len), jnp.int32),
            jax.ShapeDtypeStruct((block_count,), jnp.int32),
        ),
        in_specs=[smem(), smem(), vmem(), vmem()],
        out_specs=(vmem(), vmem(), smem()),
        scratch_shapes=[pltpu.SMEM((lat_count,), jnp.int32)],
        name="pack",
    )(block_tile, block_rows, radiances, row_cells.reshape(block_count, block_len))


def tile_kernel(
    weight_ref,
    feats_ref,
    cells_ref,
    lat_ref,
    query,
    px,
    gdisk,
    mdisk,
    bkt,
    bvt,
    wk_ref,
    wv_ref,
    target_hbm,
    wq_hbm,
    wo_hbm,
    wd_hbm,
    lgrad_hbm,
    rgrad_ref,
    gw_ref,
    gs_ref,
    loss_ref,
    comp,
    cellb,
    kv,
    qr,
    gate,
    acc,
    gkv,
    gquery,
    mixed,
    gul,
    gmix,
    ndisk,
    target_ref,
    wq_ref,
    wo_ref,
    wd_ref,
    lgrad_ref,
    hsum,
    hspread,
    countv,
    counts,
    csem,
    osem,
    isem,
    lsem,
):
    sources, _, block_len = cells_ref.shape
    slots = sources * CAP
    cells, width = lat_ref.shape
    feat = feats_ref.shape[1]
    cw = bkt.shape[0]
    ch = cw // HEADS
    disks = px.shape[1] // cw
    hd = width // HEADS
    scale = 1.0 / math.sqrt(hd)
    out_width = target_ref.shape[1]
    hl = hsum.shape[1]
    grid_rows = cells // 128

    def place(s):
        return (s // CAP) * 8 + s % CAP

    loads = [
        pltpu.make_async_copy(hbm, held, isem.at[i])
        for i, (hbm, held) in enumerate(
            ((wo_hbm, wo_ref), (wd_hbm, wd_ref), (target_hbm, target_ref), (wq_hbm, wq_ref))
        )
    ]
    for load in loads:
        load.start()

    got_cells = cells_ref[...].reshape(sources * 8, block_len)
    valid = (got_cells >= 0).astype(jnp.int32)
    countv[...] = jnp.broadcast_to(jnp.sum(valid, axis=1, keepdims=True), countv.shape)
    copy = pltpu.make_async_copy(countv, counts, csem)
    copy.start()

    hsum[...] = jnp.where(
        lax.broadcasted_iota(jnp.int32, (width, hl), 0) // hd
        == lax.broadcasted_iota(jnp.int32, (width, hl), 1),
        1.0,
        0.0,
    ).astype(BF16)
    hspread[...] = jnp.where(
        lax.broadcasted_iota(jnp.int32, (hl, width), 1) // hd
        == lax.broadcasted_iota(jnp.int32, (hl, width), 0),
        1.0,
        0.0,
    ).astype(BF16)
    comp[...] = jnp.zeros(comp.shape, BF16)
    cellb[...] = jnp.full(cellb.shape, -1, jnp.int32)

    def disk_mix(i, _):
        r = pl.ds(pl.multiple_of(i * CHUNK, CHUNK), CHUNK)
        acc[r, :] = mm(mdisk[r, :], bvt[...])
        return 0

    lax.fori_loop(0, cells // CHUNK, disk_mix, 0)

    copy.wait()
    columns = jnp.transpose(got_cells.astype(F32)).astype(jnp.int32)
    row = lax.broadcasted_iota(jnp.int32, (block_len, feat), 0)
    offset = jnp.int32(0)
    for s in range(slots):
        at = pl.ds(pl.multiple_of(offset, 16), block_len)
        got = feats_ref[s * block_len : (s + 1) * block_len, :]
        comp[at, :] = jnp.where(row < counts[place(s), 0], got, jnp.zeros_like(got))
        cellb[at, :] = jnp.broadcast_to(columns[:, place(s) : place(s) + 1], (block_len, 128))
        offset = offset + ((counts[place(s), 0] + 15) // 16) * 16
    chunk_total = (offset + (CHUNK - 1)) // CHUNK

    lane = lax.broadcasted_iota(jnp.int32, (CHUNK, 128), 1)

    def one_hot(r):
        cb = cellb[r, :]
        return jnp.concatenate(
            [
                jnp.where(cb == lane + 128 * j, 1.0, 0.0).astype(BF16)
                for j in range(cells // 128)
            ],
            axis=1,
        )

    def forward(i, _):
        r = pl.ds(pl.multiple_of(i * CHUNK, CHUNK), CHUNK)
        f = comp[r, :]
        key = mm(f, wk_ref[...]).astype(BF16)
        value = mm(f, wv_ref[...]).astype(BF16)
        kv[r, :width] = key
        kv[r, width:] = value
        oh = one_hot(r)
        q = mm(oh, query[...]).astype(BF16)
        qr[pl.ds(pl.multiple_of(i * (CHUNK // 16), CHUNK // 16), CHUNK // 16)] = q.reshape(
            CHUNK // 16, 16, width
        )
        g = jax.nn.sigmoid(mm(q * key, hsum[...]) * scale)
        gate[r, :] = g
        term = mm(g.astype(BF16), hspread[...]).astype(BF16) * value
        acc[...] += mm(oh, term, TN)
        return 0

    lax.fori_loop(0, chunk_total, forward, 0)

    lat_at = lax.axis_index("lat") * grid_rows
    tile = CHUNK
    lines = tile // 128
    for load in loads[:3]:
        load.wait()

    def middle(i, loss):
        r = pl.ds(pl.multiple_of(i * tile, tile), tile)
        m = acc[r, :].astype(BF16)
        mixed[r, :] = m
        updated = (lat_ref[r, :].astype(F32) + mm(m, wo_ref[...])).astype(BF16)
        err = mm(updated, wd_ref[...]) - target_ref[r, :]
        at = lat_at + i * lines
        gp = jnp.concatenate(
            [weight_ref[at + j] * err[j * 128 : (j + 1) * 128] for j in range(lines)], axis=0
        )
        gu = mm(gp.astype(BF16), wd_ref[...], NT)
        lgrad_ref[r, :] = gu
        gu_low = gu.astype(BF16)
        gul[r, :] = gu_low
        gmix[r, :] = mm(gu_low, wo_ref[...], NT).astype(BF16)
        return loss + jnp.sum((0.5 * gp * err).reshape(tile // 8, 8, out_width), axis=0)

    loss_ref[...] = lax.fori_loop(0, cells // tile, middle, jnp.zeros((8, out_width), F32))

    head_mask = head_match(cw, width, hd)
    sum_ch = channel_sum(cw, hl)
    gt = mm(gmix[...], bvt[...], NT)
    nsum = jnp.zeros((cells, cw), F32)
    for k in range(disks):
        pxk = px[:, k * cw : (k + 1) * cw].astype(F32)
        g = gdisk[:, k * hl : (k + 1) * hl]
        ds = mm((pxk * gt).astype(BF16), sum_ch) * g * (1.0 - g) * scale
        nsum = nsum + mm(ds.astype(BF16), sum_ch, NT) * pxk
    ndisk[...] = nsum.astype(BF16)

    def disk_weight(left, right):
        full = jnp.where(head_mask, mm(left, right, TN), 0.0)
        return jnp.sum(full.reshape(ch, HEADS, width), axis=1)

    def small_out(at, value):
        low = value.astype(gs_ref.dtype)
        for j in range(gs_ref.shape[0]):
            gs_ref[j, at : at + value.shape[0], :] = low[:, j * 128 : (j + 1) * 128]

    small_out(2 * feat, disk_weight(ndisk[...], query[...]))
    small_out(2 * feat + ch, disk_weight(mdisk[...], gmix[...]))

    def disk_query(i, _):
        r = pl.ds(pl.multiple_of(i * CHUNK, CHUNK), CHUNK)
        acc[r, :] = mm(ndisk[r, :], bkt[...])
        return 0

    lax.fori_loop(0, cells // CHUNK, disk_query, 0)
    gkv[...] = jnp.zeros(gkv.shape, F32)

    def backward(i, _):
        r = pl.ds(pl.multiple_of(i * CHUNK, CHUNK), CHUNK)
        oh = one_hot(r)
        gm = mm(oh, gmix[...]).astype(BF16)
        g = gate[r, :]
        ds = mm(gm * kv[r, width:], hsum[...]) * g * (1.0 - g) * scale
        ds_wide = mm(ds.astype(BF16), hspread[...]).astype(BF16)
        acc[...] += mm(oh, ds_wide * kv[r, :width], TN)
        g_wide = mm(g.astype(BF16), hspread[...]).astype(BF16)
        q = qr[pl.ds(pl.multiple_of(i * (CHUNK // 16), CHUNK // 16), CHUNK // 16)]
        grads = jnp.concatenate([ds_wide * q.reshape(CHUNK, width), g_wide * gm], axis=1)
        gkv[...] += mm(comp[r, :], grads, TN)
        back = mm(grads[:, :width], wk_ref[...], NT) + mm(grads[:, width:], wv_ref[...], NT)
        comp[r, :] = back.astype(BF16)
        return 0

    lax.fori_loop(0, chunk_total, backward, 0)
    small_out(0, gkv[:, :width])
    small_out(feat, gkv[:, width:])

    offset = jnp.int32(0)
    for s in range(slots):
        at = pl.ds(pl.multiple_of(offset, 16), block_len)
        got = comp[at, :]
        rgrad_ref[s * block_len : (s + 1) * block_len, :] = jnp.where(
            row < counts[place(s), 0], got, jnp.zeros_like(got)
        )
        offset = offset + ((counts[place(s), 0] + 15) // 16) * 16

    loads[3].wait()

    def lgrad_copy(i):
        r = pl.ds(pl.multiple_of(i * tile, tile), tile)
        return pltpu.make_async_copy(lgrad_ref.at[r], lgrad_hbm.at[r], lsem.at[i])

    def finish(i, _):
        r = pl.ds(pl.multiple_of(i * tile, tile), tile)
        gq = acc[r, :].astype(BF16)
        gquery[r, :] = gq
        lgrad_ref[r, :] += mm(gq, wq_ref[...], NT)
        lgrad_copy(i).start()
        return 0

    lax.fori_loop(0, cells // tile, finish, 0)

    half = gw_ref.shape[1] // 2
    slabs = CHUNK // half

    def out_copy(i):
        part = pl.ds(pl.multiple_of(i * slabs, slabs), slabs)
        return pltpu.make_async_copy(stage.at[part], gw_ref.at[part], osem.at[i])

    def weights(i, _):
        c = pl.ds(pl.multiple_of(i * CHUNK, CHUNK), CHUNK)
        gq = mm(lat_ref[:, c], gquery[...], TN).reshape(slabs, half, width)
        go = mm(mixed[:, c], gul[...], TN).reshape(slabs, half, width)
        part = pl.ds(pl.multiple_of(i * slabs, slabs), slabs)
        stage[part] = jnp.concatenate([gq, go], axis=1).astype(BF16)
        out_copy(i).start()
        return 0

    stage = qr.at[: gw_ref.shape[0]]
    lax.fori_loop(0, width // CHUNK, weights, 0)
    for i in range(width // CHUNK):
        out_copy(i).wait()
    for i in range(cells // tile):
        lgrad_copy(i).wait()


def tile_step(devices, weight, feats, cells, lat_flat, disk_state, wk, wv, target, wq, wo, wd):
    rows, feat = feats.shape
    cell_count, width = lat_flat.shape
    cw = disk_state[-1].shape[0]
    ch = cw // HEADS
    sources = cells.shape[0]
    return pl.pallas_call(
        tile_kernel,
        out_shape=(
            jax.ShapeDtypeStruct((cell_count, width), F32),
            jax.ShapeDtypeStruct((rows, feat), BF16),
            jax.ShapeDtypeStruct((devices, 2 * width // devices, width), BF16),
            jax.ShapeDtypeStruct((width // 128, 2 * feat + 2 * ch, 128), BF16),
            jax.ShapeDtypeStruct((8, target.shape[1]), F32),
        ),
        in_specs=[smem()] + [vmem()] * 11 + [anywhere()] * 4,
        out_specs=(anywhere(), vmem(), anywhere(), vmem(), vmem()),
        scratch_shapes=[
            pltpu.VMEM((rows, feat), BF16),
            pltpu.VMEM((rows, 128), jnp.int32),
            pltpu.VMEM((rows, 2 * width), BF16),
            pltpu.VMEM((rows // 16, 16, width), BF16),
            pltpu.VMEM((rows, 128), F32),
            pltpu.VMEM((cell_count, width), F32),
            pltpu.VMEM((feat, 2 * width), F32),
            pltpu.VMEM((cell_count, width), BF16),
            pltpu.VMEM((cell_count, width), BF16),
            pltpu.VMEM((cell_count, width), BF16),
            pltpu.VMEM((cell_count, width), BF16),
            pltpu.VMEM((cell_count, cw), BF16),
            pltpu.VMEM(target.shape, F32),
            pltpu.VMEM(wq.shape, BF16),
            pltpu.VMEM(wo.shape, BF16),
            pltpu.VMEM(wd.shape, BF16),
            pltpu.VMEM((cell_count, width), F32),
            pltpu.VMEM((width, 128), BF16),
            pltpu.VMEM((128, width), BF16),
            pltpu.VMEM((8 * sources, 128), jnp.int32),
            pltpu.SMEM((8 * sources, 128), jnp.int32),
            pltpu.SemaphoreType.DMA,
            pltpu.SemaphoreType.DMA((width // CHUNK,)),
            pltpu.SemaphoreType.DMA((4,)),
            pltpu.SemaphoreType.DMA((cell_count // CHUNK,)),
        ],
        compiler_params=pltpu.CompilerParams(vmem_limit_bytes=62 * 1024 * 1024),
        name="tile",
    )(weight, feats, cells, lat_flat, *disk_state, wk, wv, target, wq, wo, wd)


SIDE = 4


def lat_peer(p, k):
    y = lax.rem(p // SIDE + k // SIDE, SIDE)
    z = lax.rem(p % SIDE + k % SIDE, SIDE)
    return y * SIDE + z


def loop(count, step, start=0):
    def run(i, carry):
        step(i)
        return carry

    lax.fori_loop(start, count, run, 0)


def send_kernel(
    feats_ref,
    cells_ref,
    lat_ref,
    disk_ref,
    wdk_ref,
    wdv_ref,
    wq_ref,
    got_ref,
    gcells_ref,
    query,
    px,
    gdisk,
    mdisk,
    bkt,
    bvt,
    fsend,
    frecv,
    csend,
    crecv,
    local,
):
    lats = cells_ref.shape[0]
    p = lax.axis_index("lat")
    barrier = pltpu.get_barrier_semaphore()

    def greet(k):
        pl.semaphore_signal(
            barrier, inc=1, device_id={"lat": lat_peer(p, k)}, device_id_type=pl.DeviceIdType.MESH
        )

    loop(lats, greet, 1)
    own = pltpu.make_async_copy(feats_ref.at[p], got_ref.at[p], local.at[0])
    own.start()
    own_cells = pltpu.make_async_copy(cells_ref.at[p], gcells_ref.at[p], local.at[1])
    own_cells.start()
    pl.semaphore_wait(barrier, lats - 1)

    def feats_copy(k):
        to = lat_peer(p, k)
        return pltpu.make_async_remote_copy(
            src_ref=feats_ref.at[to],
            dst_ref=got_ref.at[p],
            send_sem=fsend.at[k],
            recv_sem=frecv.at[k],
            device_id={"lat": to},
            device_id_type=pl.DeviceIdType.MESH,
        )

    def cells_copy(k):
        to = lat_peer(p, k)
        return pltpu.make_async_remote_copy(
            src_ref=cells_ref.at[to],
            dst_ref=gcells_ref.at[p],
            send_sem=csend.at[k],
            recv_sem=crecv.at[k],
            device_id={"lat": to},
            device_id_type=pl.DeviceIdType.MESH,
        )

    def begin(k):
        feats_copy(k).start()
        cells_copy(k).start()

    def end(k):
        feats_copy(k).wait()
        cells_copy(k).wait()

    loop(lats, begin, 1)

    cells, width = lat_ref.shape
    ch = wdk_ref.shape[0]
    disks = disk_ref.shape[0] // ch
    cw = ch * HEADS
    hd = width // HEADS
    hl = gdisk.shape[1] // disks
    scale = 1.0 / math.sqrt(hd)

    def project(i):
        r = pl.ds(pl.multiple_of(i * CHUNK, CHUNK), CHUNK)
        query[r, :] = mm(lat_ref[r, :], wq_ref[...]).astype(BF16)

    loop(cells // CHUNK, project)

    spread_ch = jnp.where(
        lax.broadcasted_iota(jnp.int32, (cw, ch), 0) // HEADS
        == lax.broadcasted_iota(jnp.int32, (cw, ch), 1),
        1.0,
        0.0,
    ).astype(BF16)
    head_mask = head_match(cw, width, hd)
    bkt[...] = jnp.where(head_mask, mm(spread_ch, wdk_ref[...]), 0.0).astype(BF16)
    bvt[...] = jnp.where(head_mask, mm(spread_ch, wdv_ref[...]), 0.0).astype(BF16)
    sum_ch = channel_sum(cw, hl)
    qt = mm(query[...], bkt[...], NT)
    msum = jnp.zeros((cells, cw), F32)
    for k in range(disks):
        pxk = mm(disk_ref[k * ch : (k + 1) * ch, :], spread_ch, (((0,), (1,)), ((), ())))
        px[:, k * cw : (k + 1) * cw] = pxk.astype(BF16)
        g = jax.nn.sigmoid(mm((pxk * qt).astype(BF16), sum_ch) * scale)
        gdisk[:, k * hl : (k + 1) * hl] = g
        msum = msum + mm(g.astype(BF16), sum_ch, NT) * pxk
    mdisk[...] = msum.astype(BF16)

    own.wait()
    own_cells.wait()
    loop(lats, end, 1)


def send_rows(feats, cells, lat_flat, disk, wdk, wdv, wq):
    lats = cells.shape[0]
    count, width = lat_flat.shape
    ch = wdk.shape[0]
    disks = disk.shape[0] // ch
    cw = ch * HEADS
    dma = pltpu.SemaphoreType.DMA
    return pl.pallas_call(
        send_kernel,
        out_shape=(
            jax.ShapeDtypeStruct(feats.shape, feats.dtype),
            jax.ShapeDtypeStruct(cells.shape, cells.dtype),
            jax.ShapeDtypeStruct((count, width), BF16),
            jax.ShapeDtypeStruct((count, disks * cw), BF16),
            jax.ShapeDtypeStruct((count, disks * 128), F32),
            jax.ShapeDtypeStruct((count, cw), BF16),
            jax.ShapeDtypeStruct((cw, width), BF16),
            jax.ShapeDtypeStruct((cw, width), BF16),
        ),
        in_specs=[anywhere(), anywhere()] + [vmem()] * 5,
        out_specs=(anywhere(), anywhere()) + (vmem(),) * 6,
        scratch_shapes=[dma((lats,))] * 4 + [dma((2,))],
        compiler_params=pltpu.CompilerParams(
            collective_id=1, has_side_effects=True, vmem_limit_bytes=60 * 1024 * 1024
        ),
        name="send_rows",
    )(feats, cells, lat_flat, disk, wdk, wdv, wq)


def axis_peer(v, k):
    return lax.rem(v + k, SIDE)


def reduce_kernel(
    cut_a,
    cut_b,
    parts,
    gw_ref,
    gs_ref,
    loss_ref,
    rgrad_ref,
    share_ref,
    small_ref,
    stat_ref,
    back_ref,
    s1,
    r1,
    sg1,
    rg1,
    s2a,
    r2a,
    s2b,
    r2b,
    s2c,
    r2c,
    s3a,
    r3a,
    s3b,
    r3b,
    s3c,
    r3c,
    r4a,
    r4b,
    r4c,
    sg2,
    rg2,
    rg3,
    sg3,
    g4,
    t4,
    t5,
    t6,
    mine,
    plane,
    chips,
    local,
    s_core,
    r_core,
    s_back,
    r_back,
    s_a2,
    r_a2,
    s_b2,
    r_b2,
    s_c2,
    r_c2,
    s_p3,
    r_p3,
    s_p4,
    r_p4,
    s_g2,
    r_g2,
    s_g3,
    r_g3,
    s_g4,
    r_g4,
    s_t4,
    r_t4,
    s_g5,
    r_g5,
    s_t5,
    r_t5,
    s_g6,
    r_g6,
    s_t6,
    r_t6,
):
    xs, cores, ys, zs, slab, width = gw_ref.shape
    lons = xs * cores
    lats = ys * zs
    lon = lax.axis_index("lon")
    p = lax.axis_index("lat")
    x, c = lon // cores, lon % cores
    y, z = p // zs, p % zs
    other = 1 - c
    cols_a = pl.ds(0, cut_a)
    cols_b = pl.ds(cut_a, cut_b - cut_a)
    cols_c = pl.ds(cut_b, width - cut_b)
    piece = g4.shape[1]
    pieces = small_ref.shape[1]

    def remote(axis, target, src, dst, ssem, rsem):
        return pltpu.make_async_remote_copy(
            src_ref=src,
            dst_ref=dst,
            send_sem=ssem,
            recv_sem=rsem,
            device_id={axis: target},
            device_id_type=pl.DeviceIdType.MESH,
        )

    def to_x(k, src, dst, ssem, rsem):
        return remote("lon", axis_peer(x, k) * cores + c, src, dst, ssem, rsem)

    def to_y(k, src, dst, ssem, rsem):
        return remote("lat", axis_peer(y, k) * zs + z, src, dst, ssem, rsem)

    def to_z(k, src, dst, ssem, rsem):
        return remote("lat", y * zs + axis_peer(z, k), src, dst, ssem, rsem)

    barrier = pltpu.get_barrier_semaphore()

    def greet(axis, target):
        pl.semaphore_signal(
            barrier, inc=1, device_id={axis: target}, device_id_type=pl.DeviceIdType.MESH
        )

    loop(lats, lambda k: greet("lat", lat_peer(p, k)), 1)
    loop(xs, lambda k: greet("lon", axis_peer(x, k) * cores + c), 1)
    greet("lon", x * cores + other)

    own_small = pltpu.make_async_copy(gs_ref.at[:, c], sg1, local.at[xs])
    own_small.start()

    def own_copy(j):
        return pltpu.make_async_copy(gw_ref.at[j, c], s1.at[j], local.at[j])

    loop(xs, lambda j: own_copy(j).start())
    own_back = pltpu.make_async_copy(rgrad_ref.at[p], back_ref.at[p], local.at[xs + 1])
    own_back.start()
    pl.semaphore_wait(barrier, lats + xs - 1)

    mate = x * cores + other
    core_small = remote("lon", mate, gs_ref.at[:, other], rg1, s_core.at[xs], r_core.at[xs])
    core_small.start()

    def core_copy(k):
        j = axis_peer(x, k)
        return remote("lon", mate, gw_ref.at[j, other], r1.at[j], s_core.at[k], r_core.at[k])

    loop(xs, lambda k: core_copy(k).start(), 1)
    core_copy(0).start()

    def back_copy(k):
        to = lat_peer(p, k)
        return remote("lat", to, rgrad_ref.at[to], back_ref.at[p], s_back.at[k], r_back.at[k])

    def back_part(i):
        loop(parts[i + 1], lambda k: back_copy(k).start(), parts[i])

    back_part(0)

    def a2_copy(k):
        j = axis_peer(x, k)
        return to_x(k, s1.at[j, :, :, :, cols_a], r2a.at[k - 1], s_a2.at[k], r_a2.at[k])

    def b2_copy(k):
        return to_y(
            k, s1.at[:, axis_peer(y, k), :, :, cols_b], r2b.at[k - 1], s_b2.at[k], r_b2.at[k]
        )

    def c2_copy(k):
        return to_z(
            k, s1.at[:, :, axis_peer(z, k), :, cols_c], r2c.at[k - 1], s_c2.at[k], r_c2.at[k]
        )

    def g2_copy(k):
        return to_x(k, sg1.at[axis_peer(x, k)], rg2.at[k - 1], s_g2.at[k], r_g2.at[k])

    own_small.wait()
    core_small.wait_recv()
    sg1[...] = sg1[...] + rg1[...]
    loop(xs, lambda k: g2_copy(k).start(), 1)

    def add_core(j):
        def step(i):
            s1[j, i] = s1[j, i] + r1[j, i]

        loop(ys, step)

    def core_step(k):
        j = axis_peer(x, k)
        own_copy(j).wait()
        core_copy(k).wait_recv()
        add_core(j)
        a2_copy(k).start()

    loop(xs, core_step, 1)
    own_copy(x).wait()
    core_copy(0).wait_recv()
    add_core(x)

    def spread(k):
        b2_copy(k).start()
        c2_copy(k).start()

    loop(SIDE, spread, 1)

    def g3_copy(k):
        to = lat_peer(p, k)
        return remote("lat", to, sg2.at[to], rg3.at[k - 1], s_g3.at[k], r_g3.at[k])

    loop(xs, lambda k: g2_copy(k).wait_recv(), 1)
    total = sg1[x].astype(F32)
    for k in range(xs - 1):
        total = total + rg2[k].astype(F32)
    sg2[pieces:] = jnp.zeros((lats - pieces,) + sg2.shape[1:], BF16)
    sg2[:pieces] = total.astype(BF16).reshape(pieces, piece, total.shape[1])
    loop(lats, lambda k: g3_copy(k).start(), 1)

    def a3_copy(k):
        return to_y(k, s2a.at[axis_peer(y, k)], r3a.at[k - 1], s_p3.at[0, k], r_p3.at[0, k])

    def b3_copy(k):
        return to_z(k, s2b.at[:, axis_peer(z, k)], r3b.at[k - 1], s_p3.at[1, k], r_p3.at[1, k])

    def c3_copy(k):
        return to_x(k, s2c.at[axis_peer(x, k)], r3c.at[k - 1], s_p3.at[2, k], r_p3.at[2, k])

    loop(SIDE, lambda k: a2_copy(k).wait_recv(), 1)

    def sum_a(i):
        value = s1[x, i, :, :, :cut_a].astype(F32)
        for k in range(SIDE - 1):
            value = value + r2a[k, i].astype(F32)
        s2a[i] = value.astype(BF16)

    loop(ys, sum_a)
    loop(SIDE, lambda k: a3_copy(k).start(), 1)

    loop(SIDE, lambda k: c2_copy(k).wait_recv(), 1)

    def sum_c(i):
        value = s1[i, :, z, :, cut_b:].astype(F32)
        for k in range(SIDE - 1):
            value = value + r2c[k, i].astype(F32)
        s2c[i] = value.astype(BF16)

    loop(xs, sum_c)
    loop(SIDE, lambda k: c3_copy(k).start(), 1)
    loop(SIDE, lambda k: b2_copy(k).wait_recv(), 1)

    def sum_b(i):
        value = s1[i, y, :, :, cut_a:cut_b].astype(F32)
        for k in range(SIDE - 1):
            value = value + r2b[k, i].astype(F32)
        s2b[i] = value.astype(BF16)

    loop(xs, sum_b)
    loop(SIDE, lambda k: b3_copy(k).start(), 1)

    back_part(1)
    loop(lats, lambda k: g3_copy(k).wait_recv(), 1)

    def add_small(k, value):
        return value + rg3[k].astype(F32)

    sg3[...] = lax.fori_loop(0, lats - 1, add_small, sg2[p].astype(F32)).astype(BF16)
    g4[p] = sg3[...]

    def g4_copy(k):
        return remote("lat", lat_peer(p, k), sg3, g4.at[p], s_g4.at[k], r_g4.at[k])

    loop(lats, lambda k: g4_copy(k).start(), 1)

    def a4_copy(k):
        return to_z(k, s3a.at[axis_peer(z, k)], r4a.at[k - 1], s_p4.at[0, k], r_p4.at[0, k])

    def b4_copy(k):
        return to_x(k, s3b.at[axis_peer(x, k)], r4b.at[k - 1], s_p4.at[1, k], r_p4.at[1, k])

    def c4_copy(k):
        return to_y(k, s3c.at[axis_peer(y, k)], r4c.at[k - 1], s_p4.at[2, k], r_p4.at[2, k])

    def summed(own, others):
        value = own.astype(F32)
        for k in range(SIDE - 1):
            value = value + others[k].astype(F32)
        return value

    loop(SIDE, lambda k: a3_copy(k).wait_recv(), 1)
    s3a[...] = summed(s2a[y], r3a).astype(BF16)
    loop(SIDE, lambda k: a4_copy(k).start(), 1)
    loop(SIDE, lambda k: c3_copy(k).wait_recv(), 1)
    s3c[...] = summed(s2c[x], r3c).astype(BF16)
    loop(SIDE, lambda k: c4_copy(k).start(), 1)
    loop(SIDE, lambda k: b3_copy(k).wait_recv(), 1)
    s3b[...] = summed(s2b[:, z], r3b).astype(BF16)
    loop(SIDE, lambda k: b4_copy(k).start(), 1)
    back_part(2)

    def g5_copy(k):
        return to_x(
            k, g4.at[pl.ds(0, pieces)], small_ref.at[lon], s_g5.at[k], r_g5.at[k]
        )

    def g6_copy(j):
        at = j * cores + c
        return remote("lon", mate, small_ref.at[at], small_ref.at[at], s_g6.at[j], r_g6.at[j])

    loop(lats, lambda k: g4_copy(k).wait_recv(), 1)
    small_ref[lon] = g4[:pieces]
    loop(SIDE, lambda k: g5_copy(k).start(), 1)

    loop(SIDE, lambda k: a4_copy(k).wait_recv(), 1)
    share_a = summed(s3a[z], r4a)
    loop(SIDE, lambda k: c4_copy(k).wait_recv(), 1)
    share_c = summed(s3c[y], r4c)
    loop(SIDE, lambda k: b4_copy(k).wait_recv(), 1)
    share_b = summed(s3b[x], r4b)
    share_ref[:, :cut_a] = share_a
    share_ref[:, cut_a:cut_b] = share_b
    share_ref[:, cut_b:] = share_c
    half = slab // 2

    def lane_sums(value):
        value = jnp.sum(value, axis=0, keepdims=True)
        total = value[:, :128]
        for j in range(1, value.shape[1] // 128):
            total = total + value[:, j * 128 : (j + 1) * 128]
        return total

    square = jnp.concatenate([share_a * share_a, share_b * share_b, share_c * share_c], axis=1)
    row = lax.broadcasted_iota(jnp.int32, mine.shape, 0)
    mine[...] = jnp.where(
        row == 0,
        lane_sums(loss_ref[...]),
        jnp.where(
            row == 1,
            lane_sums(square[:half]),
            jnp.where(row == 2, lane_sums(square[half:]), 0.0),
        ),
    )

    def t4_copy(k):
        return remote("lat", lat_peer(p, k), mine, t4.at[k - 1], s_t4.at[k], r_t4.at[k])

    loop(lats, lambda k: t4_copy(k).start(), 1)
    back_part(3)
    loop(SIDE, lambda k: g5_copy(k).wait_recv(), 1)
    loop(xs, lambda j: g6_copy(j).start())

    loop(xs, lambda k: core_copy(k).wait_send())
    core_small.wait_send()

    def sent_side(k):
        a2_copy(k).wait_send()
        g2_copy(k).wait_send()
        b2_copy(k).wait_send()
        c2_copy(k).wait_send()
        a3_copy(k).wait_send()
        b3_copy(k).wait_send()
        c3_copy(k).wait_send()
        a4_copy(k).wait_send()
        b4_copy(k).wait_send()
        c4_copy(k).wait_send()

    loop(SIDE, sent_side, 1)

    loop(lats, lambda k: t4_copy(k).wait_recv(), 1)
    plane[...] = lax.fori_loop(0, lats - 1, lambda k, value: value + t4[k], mine[...])

    def t5_copy(k):
        return to_x(k, plane, t5.at[k - 1], s_t5.at[k], r_t5.at[k])

    loop(SIDE, lambda k: t5_copy(k).start(), 1)
    loop(SIDE, lambda k: t5_copy(k).wait_recv(), 1)
    chips[...] = summed(plane[...], t5)
    t6_copy = remote("lon", mate, chips, t6, s_t6.at[0], r_t6.at[0])
    t6_copy.start()

    def sent_lat(k):
        back_copy(k).wait()
        g3_copy(k).wait_send()
        g4_copy(k).wait_send()
        t4_copy(k).wait_send()

    loop(lats, sent_lat, 1)
    own_back.wait()
    loop(xs, lambda j: g6_copy(j).wait())

    def sent_x(k):
        g5_copy(k).wait_send()
        t5_copy(k).wait_send()

    loop(SIDE, sent_x, 1)
    t6_copy.wait()
    stat_ref[...] = chips[...] + t6[...]


def reduce_all(gw, gs, loss, rgrad):
    xs, cores, lats, slab, width = gw.shape
    ys, zs = lats // SIDE, SIDE
    lons = xs * cores
    small_rows = gs.shape[2]
    piece = 32
    pieces = small_rows // piece
    cut_a, cut_b = 384, 768
    parts = (1, lats, lats, lats, lats)
    wa, wb, wc = cut_a, cut_b - cut_a, width - cut_b
    dma = pltpu.SemaphoreType.DMA

    def buf(*shape, dtype=BF16):
        return pltpu.VMEM(shape, dtype)

    pairs = [
        (xs + 1,),
        (lats,),
        (SIDE,),
        (SIDE,),
        (SIDE,),
        (3, SIDE),
        (3, SIDE),
        (SIDE,),
        (lats,),
        (lats,),
        (lats,),
        (SIDE,),
        (SIDE,),
        (xs,),
        (1,),
    ]
    n = SIDE - 1
    return pl.pallas_call(
        functools.partial(reduce_kernel, cut_a, cut_b, parts),
        out_shape=(
            jax.ShapeDtypeStruct((slab, width), F32),
            jax.ShapeDtypeStruct((lons, pieces, piece, 128), BF16),
            jax.ShapeDtypeStruct((8, 128), F32),
            jax.ShapeDtypeStruct(rgrad.shape, BF16),
        ),
        in_specs=[anywhere(), anywhere(), vmem(), anywhere()],
        out_specs=(vmem(), vmem(), vmem(), anywhere()),
        scratch_shapes=[
            buf(xs, ys, zs, slab, width),
            buf(xs, ys, zs, slab, width),
            buf(xs, small_rows, 128),
            buf(xs, small_rows, 128),
            buf(ys, zs, slab, wa),
            buf(n, ys, zs, slab, wa),
            buf(xs, zs, slab, wb),
            buf(n, xs, zs, slab, wb),
            buf(xs, ys, slab, wc),
            buf(n, xs, ys, slab, wc),
            buf(zs, slab, wa),
            buf(n, zs, slab, wa),
            buf(xs, slab, wb),
            buf(n, xs, slab, wb),
            buf(ys, slab, wc),
            buf(n, ys, slab, wc),
            buf(n, slab, wa),
            buf(n, slab, wb),
            buf(n, slab, wc),
            buf(lats, piece, 128),
            buf(xs - 1, small_rows, 128),
            buf(lats - 1, piece, 128),
            buf(piece, 128),
            buf(lats, piece, 128),
            buf(lats - 1, 8, 128, dtype=F32),
            buf(n, 8, 128, dtype=F32),
            buf(8, 128, dtype=F32),
            buf(8, 128, dtype=F32),
            buf(8, 128, dtype=F32),
            buf(8, 128, dtype=F32),
            dma((xs + 2,)),
        ]
        + [dma(n) for n in pairs for _ in range(2)],
        compiler_params=pltpu.CompilerParams(
            collective_id=2, has_side_effects=True, vmem_limit_bytes=60 * 1024 * 1024
        ),
        name="reduce_all",
    )(gw.reshape((xs, cores, ys, zs, slab, width)), gs, loss, rgrad)


def finish_kernel(
    loss_scale,
    slot_ref,
    got_ref,
    share_ref,
    small_ref,
    stat_ref,
    out_ref,
    query_ref,
    wout_ref,
    key_ref,
    value_ref,
    dkey_ref,
    dvalue_ref,
    loss_ref,
):
    block_count = slot_ref.shape[0]
    block_len = out_ref.shape[0] // block_count
    half, width = query_ref.shape
    for b in range(block_count):
        out_ref[b * block_len : (b + 1) * block_len, :] = got_ref[
            pl.ds(pl.multiple_of(slot_ref[b] * block_len, block_len), block_len), :
        ]

    loss_ref[...] = jnp.sum(stat_ref[0:1, :], axis=1, keepdims=True) * loss_scale

    def scale(total, entries):
        return 1.0 / jnp.sqrt(total / entries + 1e-06)

    def whole(value):
        return jnp.sum(jnp.sum(value, axis=0, keepdims=True), axis=1, keepdims=True)

    query_ref[...] = share_ref[:half] * scale(whole(stat_ref[1:2, :]), width * width)
    wout_ref[...] = share_ref[half:] * scale(whole(stat_ref[2:3, :]), width * width)
    lons, pieces, piece, lanes = small_ref.shape
    sums = jnp.concatenate(
        [small_ref[j].reshape(pieces * piece, lanes).astype(F32) for j in range(lons)], axis=1
    )
    at = 0
    for ref in (key_ref, value_ref, dkey_ref, dvalue_ref):
        n = ref.shape[0]
        g = sums[at : at + n]
        ref[...] = g * scale(whole(g * g), n * width)
        at += n


def finish(loss_scale, slots, got, share, small, stat, rows, feat, ch):
    width = share.shape[1]
    half = share.shape[0] // 2
    shapes = [
        ((rows, got.shape[1]), BF16),
        ((half, width), F32),
        ((half, width), F32),
        ((feat, width), F32),
        ((feat, width), F32),
        ((ch, width), F32),
        ((ch, width), F32),
        ((1, 1), F32),
    ]
    return pl.pallas_call(
        functools.partial(finish_kernel, loss_scale),
        out_shape=tuple(jax.ShapeDtypeStruct(s, d) for s, d in shapes),
        in_specs=[smem()] + [vmem()] * 4,
        out_specs=(vmem(),) * len(shapes),
        compiler_params=pltpu.CompilerParams(vmem_limit_bytes=32 * 1024 * 1024),
        name="finish",
    )(slots, got, share, small, stat)


def cell_weights(row_total):
    centres = (np.arange(row_total, dtype=np.float32) + np.float32(0.5)) / np.float32(row_total)
    weight = np.cos(np.float32(math.pi / 180.0) * (np.float32(-60.0) + np.float32(120.0) * centres))
    return (weight / np.mean(weight)).astype(np.float32)


def body(
    radiances,
    block_tile,
    block_rows,
    row_cells,
    latents,
    disk_pixels,
    targets,
    w_query,
    w_key,
    w_value,
    w_disk_key,
    w_disk_value,
    w_out,
    w_decode,
):
    lat_count = lax.axis_size("lat")
    device_count = lax.axis_size(("lon", "lat"))
    rows = radiances.shape[0]
    tile_lat, tile_lon, width = latents.shape
    out_width = targets.shape[2]
    cells = tile_lat * tile_lon
    feat = radiances.shape[1]
    ch = w_disk_key.shape[0]
    sfeats, scells, slot = pack(block_tile, block_rows, radiances, row_cells, lat_count)
    lat_flat = latents.reshape(cells, width)
    got_feats, got_cells, *disk_state = send_rows(
        sfeats.reshape(lat_count, -1, feat),
        scells,
        lat_flat,
        disk_pixels.reshape(-1, cells),
        w_disk_key,
        w_disk_value,
        w_query,
    )
    lgrad, rgrad, gw, gs, loss = tile_step(
        device_count,
        jnp.asarray(cell_weights(tile_lat * lat_count)),
        got_feats.reshape(-1, feat),
        got_cells,
        lat_flat,
        disk_state,
        w_key,
        w_value,
        targets.reshape(cells, out_width),
        w_query,
        w_out,
        w_decode,
    )
    cores = 2
    xs = lax.axis_size("lon") // cores
    share, small, stat, returned = reduce_all(
        gw.reshape((xs, cores, lat_count) + gw.shape[1:]),
        gs.reshape((xs, cores) + gs.shape[1:]),
        loss,
        rgrad.reshape(lat_count, -1, feat),
    )
    row_grad, query, out, key, value, dkey, dvalue, total = finish(
        1.0 / (cells * device_count * out_width),
        slot,
        returned.reshape(-1, feat),
        share,
        small,
        stat,
        rows,
        feat,
        ch,
    )
    return (
        total.reshape(()),
        lgrad.reshape(latents.shape),
        row_grad,
        query,
        out,
        key,
        value,
        dkey,
        dvalue,
    )


def solution(mesh):
    both = ("lon", "lat")
    placed = (
        P(both, None),
        P(both),
        P(both),
        P(both),
        P("lat", "lon", None),
        P(None, None, "lat", "lon"),
        P("lat", "lon", None),
    ) + (P(),) * 7
    return jax.shard_map(
        body,
        mesh=mesh,
        in_specs=placed,
        out_specs=(
            P(),
            P("lat", "lon", None),
            P(both, None),
            P(both, None),
            P(both, None),
            P(),
            P(),
            P(),
            P(),
        ),
        check_vma=False,
    )
```

```python
import functools
import math

import jax
import jax.numpy as jnp
import numpy as np
from jax import lax
from jax.experimental import pallas as pl
from jax.experimental.pallas import tpu as pltpu
from jax.sharding import PartitionSpec as P

HEADS = 16
CAP = 2
CHUNK = 256
ROWCHUNK = 256
F32 = jnp.float32
BF16 = jnp.bfloat16

NN = (((1,), (0,)), ((), ()))
NT = (((1,), (1,)), ((), ()))
TN = (((0,), (0,)), ((), ()))


def mm(a, b, dims=NN):
    return lax.dot_general(a, b, dims, preferred_element_type=F32)


def vmem():
    return pl.BlockSpec(memory_space=pltpu.VMEM)


def anywhere():
    return pl.BlockSpec(memory_space=pl.ANY)


def smem():
    return pl.BlockSpec(memory_space=pltpu.SMEM)


def head_match(cw, width, hd):
    return (
        lax.broadcasted_iota(jnp.int32, (cw, width), 0) % HEADS
        == lax.broadcasted_iota(jnp.int32, (cw, width), 1) // hd
    )


def channel_sum(cw, lanes):
    return jnp.where(
        lax.broadcasted_iota(jnp.int32, (cw, lanes), 0) % HEADS
        == lax.broadcasted_iota(jnp.int32, (cw, lanes), 1),
        1.0,
        0.0,
    ).astype(BF16)


def pack_kernel(tile_ref, rows_ref, feats_ref, cells_ref, sfeats_ref, scells_ref, slot_ref, count):
    block_count, block_len = cells_ref.shape
    tile_total = scells_ref.shape[0]
    scells_ref[...] = jnp.full(scells_ref.shape, -1, jnp.int32)
    for t in range(tile_total):
        count[t] = 0
    lane = lax.broadcasted_iota(jnp.int32, (1, block_len), 1)
    for b in range(block_count):
        t = tile_ref[b]
        n = count[t]
        count[t] = n + 1
        slot = t * CAP + n
        slot_ref[b] = slot
        sfeats_ref[pl.ds(pl.multiple_of(slot * block_len, block_len), block_len), :] = feats_ref[
            b * block_len : (b + 1) * block_len, :
        ]
        scells_ref[t, pl.ds(n, 1), :] = jnp.where(lane < rows_ref[b], cells_ref[b : b + 1, :], -1)


def pack(block_tile, block_rows, radiances, row_cells, lat_count):
    block_count = block_tile.shape[0]
    rows, feat = radiances.shape
    block_len = rows // block_count
    slots = lat_count * CAP
    return pl.pallas_call(
        pack_kernel,
        out_shape=(
            jax.ShapeDtypeStruct((slots * block_len, feat), BF16),
            jax.ShapeDtypeStruct((lat_count, 8, block_len), jnp.int32),
            jax.ShapeDtypeStruct((block_count,), jnp.int32),
        ),
        in_specs=[smem(), smem(), vmem(), vmem()],
        out_specs=(vmem(), vmem(), smem()),
        scratch_shapes=[pltpu.SMEM((lat_count,), jnp.int32)],
        name="pack",
    )(block_tile, block_rows, radiances, row_cells.reshape(block_count, block_len))


def tile_kernel(
    weight_ref,
    feats_ref,
    cells_ref,
    lat_ref,
    query,
    px,
    gdisk,
    mdisk,
    bkt,
    bvt,
    wk_ref,
    wv_ref,
    target_hbm,
    wq_hbm,
    wo_hbm,
    wd_hbm,
    lgrad_hbm,
    rgrad_ref,
    gw_ref,
    gs_ref,
    loss_ref,
    comp,
    cellb,
    kv,
    qr,
    gate,
    acc,
    gkv,
    gquery,
    mixed,
    gul,
    gmix,
    ndisk,
    target_ref,
    wq_ref,
    wo_ref,
    wd_ref,
    lgrad_ref,
    hsum,
    hspread,
    wkv,
    countv,
    counts,
    csem,
    osem,
    isem,
    lsem,
):
    sources, _, block_len = cells_ref.shape
    slots = sources * CAP
    cells, width = lat_ref.shape
    feat = feats_ref.shape[1]
    cw = bkt.shape[0]
    ch = cw // HEADS
    disks = px.shape[1] // cw
    hd = width // HEADS
    scale = 1.0 / math.sqrt(hd)
    out_width = target_ref.shape[1]
    hl = hsum.shape[1]
    grid_rows = cells // 128

    def place(s):
        return (s // CAP) * 8 + s % CAP

    loads = [
        pltpu.make_async_copy(hbm, held, isem.at[i])
        for i, (hbm, held) in enumerate(
            ((wo_hbm, wo_ref), (wd_hbm, wd_ref), (target_hbm, target_ref), (wq_hbm, wq_ref))
        )
    ]
    for load in loads:
        load.start()

    got_cells = cells_ref[...].reshape(sources * 8, block_len)
    valid = (got_cells >= 0).astype(jnp.int32)
    countv[...] = jnp.broadcast_to(jnp.sum(valid, axis=1, keepdims=True), countv.shape)
    copy = pltpu.make_async_copy(countv, counts, csem)
    copy.start()

    hsum[...] = jnp.where(
        lax.broadcasted_iota(jnp.int32, (width, hl), 0) // hd
        == lax.broadcasted_iota(jnp.int32, (width, hl), 1),
        1.0,
        0.0,
    ).astype(BF16)
    hspread[...] = jnp.where(
        lax.broadcasted_iota(jnp.int32, (hl, width), 1) // hd
        == lax.broadcasted_iota(jnp.int32, (hl, width), 0),
        1.0,
        0.0,
    ).astype(BF16)
    wkv[:, :width] = wk_ref[...]
    wkv[:, width:] = wv_ref[...]
    comp[...] = jnp.zeros(comp.shape, BF16)
    cellb[...] = jnp.full(cellb.shape, -1, jnp.int32)

    def disk_mix(i, _):
        r = pl.ds(pl.multiple_of(i * CHUNK, CHUNK), CHUNK)
        acc[r, :] = mm(mdisk[r, :], bvt[...])
        return 0

    lax.fori_loop(0, cells // CHUNK, disk_mix, 0)

    copy.wait()
    columns = jnp.transpose(got_cells.astype(F32)).astype(jnp.int32)
    row = lax.broadcasted_iota(jnp.int32, (block_len, feat), 0)
    offset = jnp.int32(0)
    for s in range(slots):
        at = pl.ds(pl.multiple_of(offset, 16), block_len)
        got = feats_ref[s * block_len : (s + 1) * block_len, :]
        comp[at, :] = jnp.where(row < counts[place(s), 0], got, jnp.zeros_like(got))
        cellb[at, :] = jnp.broadcast_to(columns[:, place(s) : place(s) + 1], (block_len, 128))
        offset = offset + ((counts[place(s), 0] + 15) // 16) * 16
    chunk_total = (offset + (ROWCHUNK - 1)) // ROWCHUNK

    lane = lax.broadcasted_iota(jnp.int32, (ROWCHUNK, 128), 1)

    def one_hot(r):
        cb = cellb[r, :]
        return jnp.concatenate(
            [
                jnp.where(cb == lane + 128 * j, 1.0, 0.0).astype(BF16)
                for j in range(cells // 128)
            ],
            axis=1,
        )

    def forward(i, _):
        r = pl.ds(pl.multiple_of(i * ROWCHUNK, ROWCHUNK), ROWCHUNK)
        f = comp[r, :]
        both = mm(f, wkv[...]).astype(BF16)
        kv[r, :] = both
        oh = one_hot(r)
        q = mm(oh, query[...]).astype(BF16)
        qr[pl.ds(pl.multiple_of(i * (ROWCHUNK // 16), ROWCHUNK // 16), ROWCHUNK // 16)] = q.reshape(
            ROWCHUNK // 16, 16, width
        )
        g = jax.nn.sigmoid(mm(q * both[:, :width], hsum[...]) * scale)
        gate[r, :] = g
        term = mm(g.astype(BF16), hspread[...]).astype(BF16) * both[:, width:]
        acc[...] += mm(oh, term, TN)
        return 0

    lax.fori_loop(0, chunk_total, forward, 0)

    lat_at = lax.axis_index("lat") * grid_rows
    tile = CHUNK
    lines = tile // 128
    for load in loads[:3]:
        load.wait()

    def middle(i, loss):
        r = pl.ds(pl.multiple_of(i * tile, tile), tile)
        m = acc[r, :].astype(BF16)
        mixed[r, :] = m
        updated = (lat_ref[r, :].astype(F32) + mm(m, wo_ref[...])).astype(BF16)
        err = mm(updated, wd_ref[...]) - target_ref[r, :]
        at = lat_at + i * lines
        gp = jnp.concatenate(
            [weight_ref[at + j] * err[j * 128 : (j + 1) * 128] for j in range(lines)], axis=0
        )
        gu = mm(gp.astype(BF16), wd_ref[...], NT)
        lgrad_ref[r, :] = gu
        gu_low = gu.astype(BF16)
        gul[r, :] = gu_low
        gmix[r, :] = mm(gu_low, wo_ref[...], NT).astype(BF16)
        return loss + jnp.sum((0.5 * gp * err).reshape(tile // 8, 8, out_width), axis=0)

    loss_ref[...] = lax.fori_loop(0, cells // tile, middle, jnp.zeros((8, out_width), F32))

    head_mask = head_match(cw, width, hd)
    sum_ch = channel_sum(cw, hl)
    gt = mm(gmix[...], bvt[...], NT)
    nsum = jnp.zeros((cells, cw), F32)
    for k in range(disks):
        pxk = px[:, k * cw : (k + 1) * cw].astype(F32)
        g = gdisk[:, k * hl : (k + 1) * hl]
        ds = mm((pxk * gt).astype(BF16), sum_ch) * g * (1.0 - g) * scale
        nsum = nsum + mm(ds.astype(BF16), sum_ch, NT) * pxk
    ndisk[...] = nsum.astype(BF16)

    def disk_weight(left, right):
        full = jnp.where(head_mask, mm(left, right, TN), 0.0)
        return jnp.sum(full.reshape(ch, HEADS, width), axis=1)

    def small_out(at, value):
        low = value.astype(gs_ref.dtype)
        for j in range(gs_ref.shape[0]):
            gs_ref[j, at : at + value.shape[0], :] = low[:, j * 128 : (j + 1) * 128]

    small_out(2 * feat, disk_weight(ndisk[...], query[...]))
    small_out(2 * feat + ch, disk_weight(mdisk[...], gmix[...]))

    def disk_query(i, _):
        r = pl.ds(pl.multiple_of(i * CHUNK, CHUNK), CHUNK)
        acc[r, :] = mm(ndisk[r, :], bkt[...])
        return 0

    lax.fori_loop(0, cells // CHUNK, disk_query, 0)
    gkv[...] = jnp.zeros(gkv.shape, F32)

    def backward(i, _):
        r = pl.ds(pl.multiple_of(i * ROWCHUNK, ROWCHUNK), ROWCHUNK)
        oh = one_hot(r)
        gm = mm(oh, gmix[...]).astype(BF16)
        g = gate[r, :]
        ds = mm(gm * kv[r, width:], hsum[...]) * g * (1.0 - g) * scale
        ds_wide = mm(ds.astype(BF16), hspread[...]).astype(BF16)
        acc[...] += mm(oh, ds_wide * kv[r, :width], TN)
        g_wide = mm(g.astype(BF16), hspread[...]).astype(BF16)
        q = qr[pl.ds(pl.multiple_of(i * (ROWCHUNK // 16), ROWCHUNK // 16), ROWCHUNK // 16)]
        grads = jnp.concatenate([ds_wide * q.reshape(ROWCHUNK, width), g_wide * gm], axis=1)
        gkv[...] += mm(comp[r, :], grads, TN)
        comp[r, :] = mm(grads, wkv[...], NT).astype(BF16)
        return 0

    lax.fori_loop(0, chunk_total, backward, 0)
    small_out(0, gkv[:, :width])
    small_out(feat, gkv[:, width:])

    offset = jnp.int32(0)
    for s in range(slots):
        at = pl.ds(pl.multiple_of(offset, 16), block_len)
        got = comp[at, :]
        rgrad_ref[s * block_len : (s + 1) * block_len, :] = jnp.where(
            row < counts[place(s), 0], got, jnp.zeros_like(got)
        )
        offset = offset + ((counts[place(s), 0] + 15) // 16) * 16

    loads[3].wait()

    def lgrad_copy(i):
        r = pl.ds(pl.multiple_of(i * tile, tile), tile)
        return pltpu.make_async_copy(lgrad_ref.at[r], lgrad_hbm.at[r], lsem.at[i])

    def finish(i, _):
        r = pl.ds(pl.multiple_of(i * tile, tile), tile)
        gq = acc[r, :].astype(BF16)
        gquery[r, :] = gq
        lgrad_ref[r, :] += mm(gq, wq_ref[...], NT)
        lgrad_copy(i).start()
        return 0

    lax.fori_loop(0, cells // tile, finish, 0)

    half = gw_ref.shape[1] // 2
    slabs = CHUNK // half

    def out_copy(i):
        part = pl.ds(pl.multiple_of(i * slabs, slabs), slabs)
        return pltpu.make_async_copy(stage.at[part], gw_ref.at[part], osem.at[i])

    def weights(i, _):
        c = pl.ds(pl.multiple_of(i * CHUNK, CHUNK), CHUNK)
        gq = mm(lat_ref[:, c], gquery[...], TN).reshape(slabs, half, width)
        go = mm(mixed[:, c], gul[...], TN).reshape(slabs, half, width)
        part = pl.ds(pl.multiple_of(i * slabs, slabs), slabs)
        stage[part] = jnp.concatenate([gq, go], axis=1).astype(BF16)
        out_copy(i).start()
        return 0

    stage = qr.at[: gw_ref.shape[0]]
    lax.fori_loop(0, width // CHUNK, weights, 0)
    for i in range(width // CHUNK):
        out_copy(i).wait()
    for i in range(cells // tile):
        lgrad_copy(i).wait()


def tile_step(devices, weight, feats, cells, lat_flat, disk_state, wk, wv, target, wq, wo, wd):
    rows, feat = feats.shape
    cell_count, width = lat_flat.shape
    cw = disk_state[-1].shape[0]
    ch = cw // HEADS
    sources = cells.shape[0]
    return pl.pallas_call(
        tile_kernel,
        out_shape=(
            jax.ShapeDtypeStruct((cell_count, width), F32),
            jax.ShapeDtypeStruct((rows, feat), BF16),
            jax.ShapeDtypeStruct((devices, 2 * width // devices, width), BF16),
            jax.ShapeDtypeStruct((width // 128, 2 * feat + 2 * ch, 128), BF16),
            jax.ShapeDtypeStruct((8, target.shape[1]), F32),
        ),
        in_specs=[smem()] + [vmem()] * 11 + [anywhere()] * 4,
        out_specs=(anywhere(), vmem(), anywhere(), vmem(), vmem()),
        scratch_shapes=[
            pltpu.VMEM((rows, feat), BF16),
            pltpu.VMEM((rows, 128), jnp.int32),
            pltpu.VMEM((rows, 2 * width), BF16),
            pltpu.VMEM((rows // 16, 16, width), BF16),
            pltpu.VMEM((rows, 128), F32),
            pltpu.VMEM((cell_count, width), F32),
            pltpu.VMEM((feat, 2 * width), F32),
            pltpu.VMEM((cell_count, width), BF16),
            pltpu.VMEM((cell_count, width), BF16),
            pltpu.VMEM((cell_count, width), BF16),
            pltpu.VMEM((cell_count, width), BF16),
            pltpu.VMEM((cell_count, cw), BF16),
            pltpu.VMEM(target.shape, F32),
            pltpu.VMEM(wq.shape, BF16),
            pltpu.VMEM(wo.shape, BF16),
            pltpu.VMEM(wd.shape, BF16),
            pltpu.VMEM((cell_count, width), F32),
            pltpu.VMEM((width, 128), BF16),
            pltpu.VMEM((128, width), BF16),
            pltpu.VMEM((feat, 2 * width), BF16),
            pltpu.VMEM((8 * sources, 128), jnp.int32),
            pltpu.SMEM((8 * sources, 128), jnp.int32),
            pltpu.SemaphoreType.DMA,
            pltpu.SemaphoreType.DMA((width // CHUNK,)),
            pltpu.SemaphoreType.DMA((4,)),
            pltpu.SemaphoreType.DMA((cell_count // CHUNK,)),
        ],
        compiler_params=pltpu.CompilerParams(vmem_limit_bytes=62 * 1024 * 1024),
        name="tile",
    )(weight, feats, cells, lat_flat, *disk_state, wk, wv, target, wq, wo, wd)


SIDE = 4


def lat_peer(p, k):
    y = lax.rem(p // SIDE + k // SIDE, SIDE)
    z = lax.rem(p % SIDE + k % SIDE, SIDE)
    return y * SIDE + z


def loop(count, step, start=0):
    def run(i, carry):
        step(i)
        return carry

    lax.fori_loop(start, count, run, 0)


def send_kernel(
    feats_ref,
    cells_ref,
    lat_hbm,
    wq_hbm,
    disk_ref,
    wdk_ref,
    wdv_ref,
    got_ref,
    gcells_ref,
    query_hbm,
    px_hbm,
    gdisk_hbm,
    mdisk,
    bkt,
    bvt,
    lat_ref,
    wq_ref,
    query,
    px,
    gdisk,
    fsend,
    frecv,
    csend,
    crecv,
    local,
    loads,
    stores,
):
    lats = cells_ref.shape[0]
    p = lax.axis_index("lat")
    barrier = pltpu.get_barrier_semaphore()

    def greet(k):
        pl.semaphore_signal(
            barrier, inc=1, device_id={"lat": lat_peer(p, k)}, device_id_type=pl.DeviceIdType.MESH
        )

    loop(lats, greet, 1)
    own = pltpu.make_async_copy(feats_ref.at[p], got_ref.at[p], local.at[0])
    own.start()
    own_cells = pltpu.make_async_copy(cells_ref.at[p], gcells_ref.at[p], local.at[1])
    own_cells.start()
    pl.semaphore_wait(barrier, lats - 1)

    def feats_copy(k):
        to = lat_peer(p, k)
        return pltpu.make_async_remote_copy(
            src_ref=feats_ref.at[to],
            dst_ref=got_ref.at[p],
            send_sem=fsend.at[k],
            recv_sem=frecv.at[k],
            device_id={"lat": to},
            device_id_type=pl.DeviceIdType.MESH,
        )

    def cells_copy(k):
        to = lat_peer(p, k)
        return pltpu.make_async_remote_copy(
            src_ref=cells_ref.at[to],
            dst_ref=gcells_ref.at[p],
            send_sem=csend.at[k],
            recv_sem=crecv.at[k],
            device_id={"lat": to},
            device_id_type=pl.DeviceIdType.MESH,
        )

    def begin(k):
        feats_copy(k).start()
        cells_copy(k).start()

    def end(k):
        feats_copy(k).wait()
        cells_copy(k).wait()

    load_lat = pltpu.make_async_copy(lat_hbm, lat_ref, loads.at[0])
    load_wq = pltpu.make_async_copy(wq_hbm, wq_ref, loads.at[1])
    load_lat.start()
    load_wq.start()
    loop(lats, begin, 1)

    load_lat.wait()
    load_wq.wait()
    cells, width = lat_ref.shape
    ch = wdk_ref.shape[0]
    disks = disk_ref.shape[0] // ch
    cw = ch * HEADS
    hd = width // HEADS
    hl = gdisk.shape[1] // disks
    scale = 1.0 / math.sqrt(hd)

    def project(i):
        r = pl.ds(pl.multiple_of(i * CHUNK, CHUNK), CHUNK)
        query[r, :] = mm(lat_ref[r, :], wq_ref[...]).astype(BF16)

    loop(cells // CHUNK, project)
    store_query = pltpu.make_async_copy(query, query_hbm, stores.at[0])
    store_query.start()

    spread_ch = jnp.where(
        lax.broadcasted_iota(jnp.int32, (cw, ch), 0) // HEADS
        == lax.broadcasted_iota(jnp.int32, (cw, ch), 1),
        1.0,
        0.0,
    ).astype(BF16)
    head_mask = head_match(cw, width, hd)
    bkt[...] = jnp.where(head_mask, mm(spread_ch, wdk_ref[...]), 0.0).astype(BF16)
    bvt[...] = jnp.where(head_mask, mm(spread_ch, wdv_ref[...]), 0.0).astype(BF16)
    sum_ch = channel_sum(cw, hl)
    qt = mm(query[...], bkt[...], NT)
    msum = jnp.zeros((cells, cw), F32)
    for k in range(disks):
        pxk = mm(disk_ref[k * ch : (k + 1) * ch, :], spread_ch, (((0,), (1,)), ((), ())))
        px[:, k * cw : (k + 1) * cw] = pxk.astype(BF16)
        g = jax.nn.sigmoid(mm((pxk * qt).astype(BF16), sum_ch) * scale)
        gdisk[:, k * hl : (k + 1) * hl] = g
        msum = msum + mm(g.astype(BF16), sum_ch, NT) * pxk
    mdisk[...] = msum.astype(BF16)
    store_px = pltpu.make_async_copy(px, px_hbm, stores.at[1])
    store_px.start()
    store_gdisk = pltpu.make_async_copy(gdisk, gdisk_hbm, stores.at[2])
    store_gdisk.start()

    own.wait()
    own_cells.wait()
    loop(lats, end, 1)
    store_query.wait()
    store_px.wait()
    store_gdisk.wait()


def send_rows(feats, cells, lat_flat, disk, wdk, wdv, wq):
    lats = cells.shape[0]
    count, width = lat_flat.shape
    ch = wdk.shape[0]
    disks = disk.shape[0] // ch
    cw = ch * HEADS
    dma = pltpu.SemaphoreType.DMA
    return pl.pallas_call(
        send_kernel,
        out_shape=(
            jax.ShapeDtypeStruct(feats.shape, feats.dtype),
            jax.ShapeDtypeStruct(cells.shape, cells.dtype),
            jax.ShapeDtypeStruct((count, width), BF16),
            jax.ShapeDtypeStruct((count, disks * cw), BF16),
            jax.ShapeDtypeStruct((count, disks * 128), F32),
            jax.ShapeDtypeStruct((count, cw), BF16),
            jax.ShapeDtypeStruct((cw, width), BF16),
            jax.ShapeDtypeStruct((cw, width), BF16),
        ),
        in_specs=[anywhere()] * 4 + [vmem()] * 3,
        out_specs=(anywhere(),) * 5 + (vmem(),) * 3,
        scratch_shapes=[
            pltpu.VMEM((count, width), BF16),
            pltpu.VMEM((width, width), BF16),
            pltpu.VMEM((count, width), BF16),
            pltpu.VMEM((count, disks * cw), BF16),
            pltpu.VMEM((count, disks * 128), F32),
        ]
        + [dma((lats,))] * 4
        + [dma((2,)), dma((2,)), dma((3,))],
        compiler_params=pltpu.CompilerParams(
            collective_id=1, has_side_effects=True, vmem_limit_bytes=60 * 1024 * 1024
        ),
        name="send_rows",
    )(feats, cells, lat_flat, wq, disk, wdk, wdv)


def axis_peer(v, k):
    return lax.rem(v + k, SIDE)


def reduce_kernel(
    cut_a,
    cut_b,
    parts,
    gw_ref,
    gs_ref,
    loss_ref,
    rgrad_ref,
    share_ref,
    small_ref,
    stat_ref,
    back_ref,
    s1,
    r1,
    sg1,
    rg1,
    s2a,
    r2a,
    s2b,
    r2b,
    s2c,
    r2c,
    s3a,
    r3a,
    s3b,
    r3b,
    s3c,
    r3c,
    r4a,
    r4b,
    r4c,
    sg2,
    rg2,
    rg3,
    sg3,
    g4,
    t4,
    t5,
    t6,
    mine,
    plane,
    chips,
    local,
    s_core,
    r_core,
    s_back,
    r_back,
    s_a2,
    r_a2,
    s_b2,
    r_b2,
    s_c2,
    r_c2,
    s_p3,
    r_p3,
    s_p4,
    r_p4,
    s_g2,
    r_g2,
    s_g3,
    r_g3,
    s_g4,
    r_g4,
    s_t4,
    r_t4,
    s_g5,
    r_g5,
    s_t5,
    r_t5,
    s_g6,
    r_g6,
    s_t6,
    r_t6,
):
    xs, cores, ys, zs, slab, width = gw_ref.shape
    lons = xs * cores
    lats = ys * zs
    lon = lax.axis_index("lon")
    p = lax.axis_index("lat")
    x, c = lon // cores, lon % cores
    y, z = p // zs, p % zs
    other = 1 - c
    cols_a = pl.ds(0, cut_a)
    cols_b = pl.ds(cut_a, cut_b - cut_a)
    cols_c = pl.ds(cut_b, width - cut_b)
    piece = g4.shape[1]
    pieces = small_ref.shape[1]

    def remote(axis, target, src, dst, ssem, rsem):
        return pltpu.make_async_remote_copy(
            src_ref=src,
            dst_ref=dst,
            send_sem=ssem,
            recv_sem=rsem,
            device_id={axis: target},
            device_id_type=pl.DeviceIdType.MESH,
        )

    def to_x(k, src, dst, ssem, rsem):
        return remote("lon", axis_peer(x, k) * cores + c, src, dst, ssem, rsem)

    def to_y(k, src, dst, ssem, rsem):
        return remote("lat", axis_peer(y, k) * zs + z, src, dst, ssem, rsem)

    def to_z(k, src, dst, ssem, rsem):
        return remote("lat", y * zs + axis_peer(z, k), src, dst, ssem, rsem)

    barrier = pltpu.get_barrier_semaphore()

    def greet(axis, target):
        pl.semaphore_signal(
            barrier, inc=1, device_id={axis: target}, device_id_type=pl.DeviceIdType.MESH
        )

    loop(lats, lambda k: greet("lat", lat_peer(p, k)), 1)
    loop(xs, lambda k: greet("lon", axis_peer(x, k) * cores + c), 1)
    greet("lon", x * cores + other)

    own_small = pltpu.make_async_copy(gs_ref.at[:, c], sg1, local.at[xs])
    own_small.start()

    def own_copy(j):
        return pltpu.make_async_copy(gw_ref.at[j, c], s1.at[j], local.at[j])

    loop(xs, lambda j: own_copy(j).start())
    own_back = pltpu.make_async_copy(rgrad_ref.at[p], back_ref.at[p], local.at[xs + 1])
    own_back.start()
    pl.semaphore_wait(barrier, lats + xs - 1)

    mate = x * cores + other
    core_small = remote("lon", mate, gs_ref.at[:, other], rg1, s_core.at[xs], r_core.at[xs])
    core_small.start()

    def core_copy(k):
        j = axis_peer(x, k)
        return remote("lon", mate, gw_ref.at[j, other], r1.at[j], s_core.at[k], r_core.at[k])

    loop(xs, lambda k: core_copy(k).start(), 1)
    core_copy(0).start()

    def back_copy(k):
        to = lat_peer(p, k)
        return remote("lat", to, rgrad_ref.at[to], back_ref.at[p], s_back.at[k], r_back.at[k])

    def back_part(i):
        loop(parts[i + 1], lambda k: back_copy(k).start(), parts[i])

    back_part(0)

    def a2_copy(k):
        j = axis_peer(x, k)
        return to_x(k, s1.at[j, :, :, :, cols_a], r2a.at[k - 1], s_a2.at[k], r_a2.at[k])

    def b2_copy(k):
        return to_y(
            k, s1.at[:, axis_peer(y, k), :, :, cols_b], r2b.at[k - 1], s_b2.at[k], r_b2.at[k]
        )

    def c2_copy(k):
        return to_z(
            k, s1.at[:, :, axis_peer(z, k), :, cols_c], r2c.at[k - 1], s_c2.at[k], r_c2.at[k]
        )

    def g2_copy(k):
        return to_x(k, sg1.at[axis_peer(x, k)], rg2.at[k - 1], s_g2.at[k], r_g2.at[k])

    own_small.wait()
    core_small.wait_recv()
    sg1[...] = sg1[...] + rg1[...]
    loop(xs, lambda k: g2_copy(k).start(), 1)

    def add_core(j):
        def step(i):
            s1[j, i] = s1[j, i] + r1[j, i]

        loop(ys, step)

    def core_step(k):
        j = axis_peer(x, k)
        own_copy(j).wait()
        core_copy(k).wait_recv()
        add_core(j)
        a2_copy(k).start()

    loop(xs, core_step, 1)
    own_copy(x).wait()
    core_copy(0).wait_recv()
    add_core(x)

    def spread(k):
        b2_copy(k).start()
        c2_copy(k).start()

    loop(SIDE, spread, 1)

    def g3_copy(k):
        to = lat_peer(p, k)
        return remote("lat", to, sg2.at[to], rg3.at[k - 1], s_g3.at[k], r_g3.at[k])

    loop(xs, lambda k: g2_copy(k).wait_recv(), 1)
    total = sg1[x].astype(F32)
    for k in range(xs - 1):
        total = total + rg2[k].astype(F32)
    sg2[pieces:] = jnp.zeros((lats - pieces,) + sg2.shape[1:], BF16)
    sg2[:pieces] = total.astype(BF16).reshape(pieces, piece, total.shape[1])
    loop(lats, lambda k: g3_copy(k).start(), 1)

    def a3_copy(k):
        return to_y(k, s2a.at[axis_peer(y, k)], r3a.at[k - 1], s_p3.at[0, k], r_p3.at[0, k])

    def b3_copy(k):
        return to_z(k, s2b.at[:, axis_peer(z, k)], r3b.at[k - 1], s_p3.at[1, k], r_p3.at[1, k])

    def c3_copy(k):
        return to_x(k, s2c.at[axis_peer(x, k)], r3c.at[k - 1], s_p3.at[2, k], r_p3.at[2, k])

    loop(SIDE, lambda k: a2_copy(k).wait_recv(), 1)

    def sum_a(i):
        value = s1[x, i, :, :, :cut_a].astype(F32)
        for k in range(SIDE - 1):
            value = value + r2a[k, i].astype(F32)
        s2a[i] = value.astype(BF16)

    loop(ys, sum_a)
    loop(SIDE, lambda k: a3_copy(k).start(), 1)

    loop(SIDE, lambda k: c2_copy(k).wait_recv(), 1)

    def sum_c(i):
        value = s1[i, :, z, :, cut_b:].astype(F32)
        for k in range(SIDE - 1):
            value = value + r2c[k, i].astype(F32)
        s2c[i] = value.astype(BF16)

    loop(xs, sum_c)
    loop(SIDE, lambda k: c3_copy(k).start(), 1)
    loop(SIDE, lambda k: b2_copy(k).wait_recv(), 1)

    def sum_b(i):
        value = s1[i, y, :, :, cut_a:cut_b].astype(F32)
        for k in range(SIDE - 1):
            value = value + r2b[k, i].astype(F32)
        s2b[i] = value.astype(BF16)

    loop(xs, sum_b)
    loop(SIDE, lambda k: b3_copy(k).start(), 1)

    back_part(1)
    loop(lats, lambda k: g3_copy(k).wait_recv(), 1)

    def add_small(k, value):
        return value + rg3[k].astype(F32)

    sg3[...] = lax.fori_loop(0, lats - 1, add_small, sg2[p].astype(F32)).astype(BF16)
    g4[p] = sg3[...]

    def g4_copy(k):
        return remote("lat", lat_peer(p, k), sg3, g4.at[p], s_g4.at[k], r_g4.at[k])

    loop(lats, lambda k: g4_copy(k).start(), 1)

    def a4_copy(k):
        return to_z(k, s3a.at[axis_peer(z, k)], r4a.at[k - 1], s_p4.at[0, k], r_p4.at[0, k])

    def b4_copy(k):
        return to_x(k, s3b.at[axis_peer(x, k)], r4b.at[k - 1], s_p4.at[1, k], r_p4.at[1, k])

    def c4_copy(k):
        return to_y(k, s3c.at[axis_peer(y, k)], r4c.at[k - 1], s_p4.at[2, k], r_p4.at[2, k])

    def summed(own, others):
        value = own.astype(F32)
        for k in range(SIDE - 1):
            value = value + others[k].astype(F32)
        return value

    loop(SIDE, lambda k: a3_copy(k).wait_recv(), 1)
    s3a[...] = summed(s2a[y], r3a).astype(BF16)
    loop(SIDE, lambda k: a4_copy(k).start(), 1)
    loop(SIDE, lambda k: c3_copy(k).wait_recv(), 1)
    s3c[...] = summed(s2c[x], r3c).astype(BF16)
    loop(SIDE, lambda k: c4_copy(k).start(), 1)
    loop(SIDE, lambda k: b3_copy(k).wait_recv(), 1)
    s3b[...] = summed(s2b[:, z], r3b).astype(BF16)
    loop(SIDE, lambda k: b4_copy(k).start(), 1)
    back_part(2)

    def g5_copy(k):
        return to_x(
            k, g4.at[pl.ds(0, pieces)], small_ref.at[lon], s_g5.at[k], r_g5.at[k]
        )

    def g6_copy(j):
        at = j * cores + c
        return remote("lon", mate, small_ref.at[at], small_ref.at[at], s_g6.at[j], r_g6.at[j])

    loop(lats, lambda k: g4_copy(k).wait_recv(), 1)
    small_ref[lon] = g4[:pieces]
    loop(SIDE, lambda k: g5_copy(k).start(), 1)

    loop(SIDE, lambda k: a4_copy(k).wait_recv(), 1)
    share_a = summed(s3a[z], r4a)
    loop(SIDE, lambda k: c4_copy(k).wait_recv(), 1)
    share_c = summed(s3c[y], r4c)
    loop(SIDE, lambda k: b4_copy(k).wait_recv(), 1)
    share_b = summed(s3b[x], r4b)
    share_ref[:, :cut_a] = share_a
    share_ref[:, cut_a:cut_b] = share_b
    share_ref[:, cut_b:] = share_c
    half = slab // 2

    def lane_sums(value):
        value = jnp.sum(value, axis=0, keepdims=True)
        total = value[:, :128]
        for j in range(1, value.shape[1] // 128):
            total = total + value[:, j * 128 : (j + 1) * 128]
        return total

    square = jnp.concatenate([share_a * share_a, share_b * share_b, share_c * share_c], axis=1)
    row = lax.broadcasted_iota(jnp.int32, mine.shape, 0)
    mine[...] = jnp.where(
        row == 0,
        lane_sums(loss_ref[...]),
        jnp.where(
            row == 1,
            lane_sums(square[:half]),
            jnp.where(row == 2, lane_sums(square[half:]), 0.0),
        ),
    )

    def t4_copy(k):
        return remote("lat", lat_peer(p, k), mine, t4.at[k - 1], s_t4.at[k], r_t4.at[k])

    loop(lats, lambda k: t4_copy(k).start(), 1)
    back_part(3)
    loop(SIDE, lambda k: g5_copy(k).wait_recv(), 1)
    loop(xs, lambda j: g6_copy(j).start())

    loop(xs, lambda k: core_copy(k).wait_send())
    core_small.wait_send()

    def sent_side(k):
        a2_copy(k).wait_send()
        g2_copy(k).wait_send()
        b2_copy(k).wait_send()
        c2_copy(k).wait_send()
        a3_copy(k).wait_send()
        b3_copy(k).wait_send()
        c3_copy(k).wait_send()
        a4_copy(k).wait_send()
        b4_copy(k).wait_send()
        c4_copy(k).wait_send()

    loop(SIDE, sent_side, 1)

    loop(lats, lambda k: t4_copy(k).wait_recv(), 1)
    plane[...] = lax.fori_loop(0, lats - 1, lambda k, value: value + t4[k], mine[...])

    def t5_copy(k):
        return to_x(k, plane, t5.at[k - 1], s_t5.at[k], r_t5.at[k])

    loop(SIDE, lambda k: t5_copy(k).start(), 1)
    loop(SIDE, lambda k: t5_copy(k).wait_recv(), 1)
    chips[...] = summed(plane[...], t5)
    t6_copy = remote("lon", mate, chips, t6, s_t6.at[0], r_t6.at[0])
    t6_copy.start()

    def sent_lat(k):
        back_copy(k).wait()
        g3_copy(k).wait_send()
        g4_copy(k).wait_send()
        t4_copy(k).wait_send()

    loop(lats, sent_lat, 1)
    own_back.wait()
    loop(xs, lambda j: g6_copy(j).wait())

    def sent_x(k):
        g5_copy(k).wait_send()
        t5_copy(k).wait_send()

    loop(SIDE, sent_x, 1)
    t6_copy.wait()
    stat_ref[...] = chips[...] + t6[...]


def reduce_all(gw, gs, loss, rgrad):
    xs, cores, lats, slab, width = gw.shape
    ys, zs = lats // SIDE, SIDE
    lons = xs * cores
    small_rows = gs.shape[2]
    piece = 32
    pieces = small_rows // piece
    cut_a, cut_b = 512, 768
    parts = (1, lats, lats, lats, lats)
    wa, wb, wc = cut_a, cut_b - cut_a, width - cut_b
    dma = pltpu.SemaphoreType.DMA

    def buf(*shape, dtype=BF16):
        return pltpu.VMEM(shape, dtype)

    pairs = [
        (xs + 1,),
        (lats,),
        (SIDE,),
        (SIDE,),
        (SIDE,),
        (3, SIDE),
        (3, SIDE),
        (SIDE,),
        (lats,),
        (lats,),
        (lats,),
        (SIDE,),
        (SIDE,),
        (xs,),
        (1,),
    ]
    n = SIDE - 1
    return pl.pallas_call(
        functools.partial(reduce_kernel, cut_a, cut_b, parts),
        out_shape=(
            jax.ShapeDtypeStruct((slab, width), F32),
            jax.ShapeDtypeStruct((lons, pieces, piece, 128), BF16),
            jax.ShapeDtypeStruct((8, 128), F32),
            jax.ShapeDtypeStruct(rgrad.shape, BF16),
        ),
        in_specs=[anywhere(), anywhere(), vmem(), anywhere()],
        out_specs=(vmem(), vmem(), vmem(), anywhere()),
        scratch_shapes=[
            buf(xs, ys, zs, slab, width),
            buf(xs, ys, zs, slab, width),
            buf(xs, small_rows, 128),
            buf(xs, small_rows, 128),
            buf(ys, zs, slab, wa),
            buf(n, ys, zs, slab, wa),
            buf(xs, zs, slab, wb),
            buf(n, xs, zs, slab, wb),
            buf(xs, ys, slab, wc),
            buf(n, xs, ys, slab, wc),
            buf(zs, slab, wa),
            buf(n, zs, slab, wa),
            buf(xs, slab, wb),
            buf(n, xs, slab, wb),
            buf(ys, slab, wc),
            buf(n, ys, slab, wc),
            buf(n, slab, wa),
            buf(n, slab, wb),
            buf(n, slab, wc),
            buf(lats, piece, 128),
            buf(xs - 1, small_rows, 128),
            buf(lats - 1, piece, 128),
            buf(piece, 128),
            buf(lats, piece, 128),
            buf(lats - 1, 8, 128, dtype=F32),
            buf(n, 8, 128, dtype=F32),
            buf(8, 128, dtype=F32),
            buf(8, 128, dtype=F32),
            buf(8, 128, dtype=F32),
            buf(8, 128, dtype=F32),
            dma((xs + 2,)),
        ]
        + [dma(n) for n in pairs for _ in range(2)],
        compiler_params=pltpu.CompilerParams(
            collective_id=2, has_side_effects=True, vmem_limit_bytes=60 * 1024 * 1024
        ),
        name="reduce_all",
    )(gw.reshape((xs, cores, ys, zs, slab, width)), gs, loss, rgrad)


def finish_kernel(
    loss_scale,
    slot_ref,
    got_ref,
    share_ref,
    small_ref,
    stat_ref,
    out_ref,
    query_ref,
    wout_ref,
    key_ref,
    value_ref,
    dkey_ref,
    dvalue_ref,
    loss_ref,
):
    block_count = slot_ref.shape[0]
    block_len = out_ref.shape[0] // block_count
    half, width = query_ref.shape
    for b in range(block_count):
        out_ref[b * block_len : (b + 1) * block_len, :] = got_ref[
            pl.ds(pl.multiple_of(slot_ref[b] * block_len, block_len), block_len), :
        ]

    loss_ref[...] = jnp.sum(stat_ref[0:1, :], axis=1, keepdims=True) * loss_scale

    def scale(total, entries):
        return 1.0 / jnp.sqrt(total / entries + 1e-06)

    def whole(value):
        return jnp.sum(jnp.sum(value, axis=0, keepdims=True), axis=1, keepdims=True)

    query_ref[...] = share_ref[:half] * scale(whole(stat_ref[1:2, :]), width * width)
    wout_ref[...] = share_ref[half:] * scale(whole(stat_ref[2:3, :]), width * width)
    lons, pieces, piece, lanes = small_ref.shape
    sums = jnp.concatenate(
        [small_ref[j].reshape(pieces * piece, lanes).astype(F32) for j in range(lons)], axis=1
    )
    at = 0
    for ref in (key_ref, value_ref, dkey_ref, dvalue_ref):
        n = ref.shape[0]
        g = sums[at : at + n]
        ref[...] = g * scale(whole(g * g), n * width)
        at += n


def finish(loss_scale, slots, got, share, small, stat, rows, feat, ch):
    width = share.shape[1]
    half = share.shape[0] // 2
    shapes = [
        ((rows, got.shape[1]), BF16),
        ((half, width), F32),
        ((half, width), F32),
        ((feat, width), F32),
        ((feat, width), F32),
        ((ch, width), F32),
        ((ch, width), F32),
        ((1, 1), F32),
    ]
    return pl.pallas_call(
        functools.partial(finish_kernel, loss_scale),
        out_shape=tuple(jax.ShapeDtypeStruct(s, d) for s, d in shapes),
        in_specs=[smem()] + [vmem()] * 4,
        out_specs=(vmem(),) * len(shapes),
        compiler_params=pltpu.CompilerParams(vmem_limit_bytes=60 * 1024 * 1024),
        name="finish",
    )(slots, got, share, small, stat)


def cell_weights(row_total):
    centres = (np.arange(row_total, dtype=np.float32) + np.float32(0.5)) / np.float32(row_total)
    weight = np.cos(np.float32(math.pi / 180.0) * (np.float32(-60.0) + np.float32(120.0) * centres))
    return (weight / np.mean(weight)).astype(np.float32)


def body(
    radiances,
    block_tile,
    block_rows,
    row_cells,
    latents,
    disk_pixels,
    targets,
    w_query,
    w_key,
    w_value,
    w_disk_key,
    w_disk_value,
    w_out,
    w_decode,
):
    lat_count = lax.axis_size("lat")
    device_count = lax.axis_size(("lon", "lat"))
    rows = radiances.shape[0]
    tile_lat, tile_lon, width = latents.shape
    out_width = targets.shape[2]
    cells = tile_lat * tile_lon
    feat = radiances.shape[1]
    ch = w_disk_key.shape[0]
    sfeats, scells, slot = pack(block_tile, block_rows, radiances, row_cells, lat_count)
    lat_flat = latents.reshape(cells, width)
    got_feats, got_cells, *disk_state = send_rows(
        sfeats.reshape(lat_count, -1, feat),
        scells,
        lat_flat,
        disk_pixels.reshape(-1, cells),
        w_disk_key,
        w_disk_value,
        w_query,
    )
    lgrad, rgrad, gw, gs, loss = tile_step(
        device_count,
        jnp.asarray(cell_weights(tile_lat * lat_count)),
        got_feats.reshape(-1, feat),
        got_cells,
        lat_flat,
        disk_state,
        w_key,
        w_value,
        targets.reshape(cells, out_width),
        w_query,
        w_out,
        w_decode,
    )
    cores = 2
    xs = lax.axis_size("lon") // cores
    share, small, stat, returned = reduce_all(
        gw.reshape((xs, cores, lat_count) + gw.shape[1:]),
        gs.reshape((xs, cores) + gs.shape[1:]),
        loss,
        rgrad.reshape(lat_count, -1, feat),
    )
    row_grad, query, out, key, value, dkey, dvalue, total = finish(
        1.0 / (cells * device_count * out_width),
        slot,
        returned.reshape(-1, feat),
        share,
        small,
        stat,
        rows,
        feat,
        ch,
    )
    return (
        total.reshape(()),
        lgrad.reshape(latents.shape),
        row_grad,
        query,
        out,
        key,
        value,
        dkey,
        dvalue,
    )


def solution(mesh):
    both = ("lon", "lat")
    placed = (
        P(both, None),
        P(both),
        P(both),
        P(both),
        P("lat", "lon", None),
        P(None, None, "lat", "lon"),
        P("lat", "lon", None),
    ) + (P(),) * 7
    return jax.shard_map(
        body,
        mesh=mesh,
        in_specs=placed,
        out_specs=(
            P(),
            P("lat", "lon", None),
            P(both, None),
            P(both, None),
            P(both, None),
            P(),
            P(),
            P(),
            P(),
        ),
        check_vma=False,
    )
```

```python
import functools
import math

import jax
import jax.numpy as jnp
import numpy as np
from jax import lax
from jax.experimental import pallas as pl
from jax.experimental.pallas import tpu as pltpu
from jax.sharding import PartitionSpec as P

HEADS = 16
CAP = 2
CHUNK = 256
ROWCHUNK = 256
F32 = jnp.float32
BF16 = jnp.bfloat16

NN = (((1,), (0,)), ((), ()))
NT = (((1,), (1,)), ((), ()))
TN = (((0,), (0,)), ((), ()))


def mm(a, b, dims=NN):
    return lax.dot_general(a, b, dims, preferred_element_type=F32)


def vmem():
    return pl.BlockSpec(memory_space=pltpu.VMEM)


def anywhere():
    return pl.BlockSpec(memory_space=pl.ANY)


def smem():
    return pl.BlockSpec(memory_space=pltpu.SMEM)


def head_match(cw, width, hd):
    return (
        lax.broadcasted_iota(jnp.int32, (cw, width), 0) % HEADS
        == lax.broadcasted_iota(jnp.int32, (cw, width), 1) // hd
    )


def channel_sum(cw, lanes):
    return jnp.where(
        lax.broadcasted_iota(jnp.int32, (cw, lanes), 0) % HEADS
        == lax.broadcasted_iota(jnp.int32, (cw, lanes), 1),
        1.0,
        0.0,
    ).astype(BF16)


def pack_kernel(tile_ref, rows_ref, feats_ref, cells_ref, sfeats_ref, scells_ref, slot_ref, count):
    block_count, block_len = cells_ref.shape
    tile_total = scells_ref.shape[0]
    scells_ref[...] = jnp.full(scells_ref.shape, -1, jnp.int32)
    for t in range(tile_total):
        count[t] = 0
    lane = lax.broadcasted_iota(jnp.int32, (1, block_len), 1)
    for b in range(block_count):
        t = tile_ref[b]
        n = count[t]
        count[t] = n + 1
        slot = t * CAP + n
        slot_ref[b] = slot
        sfeats_ref[pl.ds(pl.multiple_of(slot * block_len, block_len), block_len), :] = feats_ref[
            b * block_len : (b + 1) * block_len, :
        ]
        scells_ref[t, pl.ds(n, 1), :] = jnp.where(lane < rows_ref[b], cells_ref[b : b + 1, :], -1)


def pack(block_tile, block_rows, radiances, row_cells, lat_count):
    block_count = block_tile.shape[0]
    rows, feat = radiances.shape
    block_len = rows // block_count
    slots = lat_count * CAP
    return pl.pallas_call(
        pack_kernel,
        out_shape=(
            jax.ShapeDtypeStruct((slots * block_len, feat), BF16),
            jax.ShapeDtypeStruct((lat_count, 8, block_len), jnp.int32),
            jax.ShapeDtypeStruct((block_count,), jnp.int32),
        ),
        in_specs=[smem(), smem(), vmem(), vmem()],
        out_specs=(vmem(), vmem(), smem()),
        scratch_shapes=[pltpu.SMEM((lat_count,), jnp.int32)],
        name="pack",
    )(block_tile, block_rows, radiances, row_cells.reshape(block_count, block_len))


def tile_kernel(
    weight_ref,
    feats_ref,
    cells_ref,
    lat_hbm,
    query,
    px_hbm,
    gdisk_hbm,
    mdisk,
    bkt,
    bvt,
    wk_ref,
    wv_ref,
    target_hbm,
    wq_hbm,
    wo_hbm,
    wd_hbm,
    lgrad_hbm,
    rgrad_ref,
    gw_ref,
    gs_ref,
    loss_ref,
    comp,
    cellb,
    kv,
    qr,
    gate,
    acc,
    gkv,
    gquery,
    mixed,
    gul,
    gmix,
    ndisk,
    lat_ref,
    px,
    gdisk,
    target_ref,
    wq_ref,
    wo_ref,
    wd_ref,
    lgrad_ref,
    hsum,
    hspread,
    wkv,
    countv,
    counts,
    csem,
    osem,
    isem,
    lsem,
):
    sources, _, block_len = cells_ref.shape
    slots = sources * CAP
    cells, width = lat_ref.shape
    feat = feats_ref.shape[1]
    cw = bkt.shape[0]
    ch = cw // HEADS
    disks = px.shape[1] // cw
    hd = width // HEADS
    scale = 1.0 / math.sqrt(hd)
    out_width = target_ref.shape[1]
    hl = hsum.shape[1]
    grid_rows = cells // 128

    def place(s):
        return (s // CAP) * 8 + s % CAP

    loads = [
        pltpu.make_async_copy(hbm, held, isem.at[i])
        for i, (hbm, held) in enumerate(
            (
                (wo_hbm, wo_ref),
                (wd_hbm, wd_ref),
                (target_hbm, target_ref),
                (lat_hbm, lat_ref),
                (px_hbm, px),
                (gdisk_hbm, gdisk),
                (wq_hbm, wq_ref),
            )
        )
    ]
    for load in loads:
        load.start()

    got_cells = cells_ref[...].reshape(sources * 8, block_len)
    valid = (got_cells >= 0).astype(jnp.int32)
    countv[...] = jnp.broadcast_to(jnp.sum(valid, axis=1, keepdims=True), countv.shape)
    copy = pltpu.make_async_copy(countv, counts, csem)
    copy.start()

    hsum[...] = jnp.where(
        lax.broadcasted_iota(jnp.int32, (width, hl), 0) // hd
        == lax.broadcasted_iota(jnp.int32, (width, hl), 1),
        1.0,
        0.0,
    ).astype(BF16)
    hspread[...] = jnp.where(
        lax.broadcasted_iota(jnp.int32, (hl, width), 1) // hd
        == lax.broadcasted_iota(jnp.int32, (hl, width), 0),
        1.0,
        0.0,
    ).astype(BF16)
    wkv[:, :width] = wk_ref[...]
    wkv[:, width:] = wv_ref[...]
    comp[...] = jnp.zeros(comp.shape, BF16)
    cellb[...] = jnp.full(cellb.shape, -1, jnp.int32)

    def disk_mix(i, _):
        r = pl.ds(pl.multiple_of(i * CHUNK, CHUNK), CHUNK)
        acc[r, :] = mm(mdisk[r, :], bvt[...])
        return 0

    lax.fori_loop(0, cells // CHUNK, disk_mix, 0)

    copy.wait()
    columns = jnp.transpose(got_cells.astype(F32)).astype(jnp.int32)
    row = lax.broadcasted_iota(jnp.int32, (block_len, feat), 0)
    offset = jnp.int32(0)
    for s in range(slots):
        at = pl.ds(pl.multiple_of(offset, 16), block_len)
        got = feats_ref[s * block_len : (s + 1) * block_len, :]
        comp[at, :] = jnp.where(row < counts[place(s), 0], got, jnp.zeros_like(got))
        cellb[at, :] = jnp.broadcast_to(columns[:, place(s) : place(s) + 1], (block_len, 128))
        offset = offset + ((counts[place(s), 0] + 15) // 16) * 16
    chunk_total = (offset + (ROWCHUNK - 1)) // ROWCHUNK

    lane = lax.broadcasted_iota(jnp.int32, (ROWCHUNK, 128), 1)

    def one_hot(r):
        cb = cellb[r, :]
        return jnp.concatenate(
            [
                jnp.where(cb == lane + 128 * j, 1.0, 0.0).astype(BF16)
                for j in range(cells // 128)
            ],
            axis=1,
        )

    def one_hot_t(r):
        row = jnp.transpose(cellb[r, :].astype(F32))[0:1, :]
        line = lax.broadcasted_iota(jnp.int32, (cells, ROWCHUNK), 0).astype(F32)
        return jnp.where(row == line, 1.0, 0.0).astype(BF16)

    def forward(i, _):
        r = pl.ds(pl.multiple_of(i * ROWCHUNK, ROWCHUNK), ROWCHUNK)
        f = comp[r, :]
        both = mm(f, wkv[...]).astype(BF16)
        kv[r, :] = both
        oh = one_hot(r)
        q = mm(oh, query[...]).astype(BF16)
        qr[pl.ds(pl.multiple_of(i * (ROWCHUNK // 16), ROWCHUNK // 16), ROWCHUNK // 16)] = q.reshape(
            ROWCHUNK // 16, 16, width
        )
        g = jax.nn.sigmoid(mm(q * both[:, :width], hsum[...]) * scale)
        gate[r, :] = g
        term = mm(g.astype(BF16), hspread[...]).astype(BF16) * both[:, width:]
        acc[...] += mm(one_hot_t(r), term)
        return 0

    lax.fori_loop(0, chunk_total, forward, 0)

    lat_at = lax.axis_index("lat") * grid_rows
    tile = CHUNK
    lines = tile // 128
    for load in loads[:4]:
        load.wait()

    def middle(i, loss):
        r = pl.ds(pl.multiple_of(i * tile, tile), tile)
        m = acc[r, :].astype(BF16)
        mixed[r, :] = m
        updated = (lat_ref[r, :].astype(F32) + mm(m, wo_ref[...])).astype(BF16)
        err = mm(updated, wd_ref[...]) - target_ref[r, :]
        at = lat_at + i * lines
        gp = jnp.concatenate(
            [weight_ref[at + j] * err[j * 128 : (j + 1) * 128] for j in range(lines)], axis=0
        )
        gu = mm(gp.astype(BF16), wd_ref[...], NT)
        lgrad_ref[r, :] = gu
        gu_low = gu.astype(BF16)
        gul[r, :] = gu_low
        gmix[r, :] = mm(gu_low, wo_ref[...], NT).astype(BF16)
        return loss + jnp.sum((0.5 * gp * err).reshape(tile // 8, 8, out_width), axis=0)

    loss_ref[...] = lax.fori_loop(0, cells // tile, middle, jnp.zeros((8, out_width), F32))

    loads[4].wait()
    loads[5].wait()
    head_mask = head_match(cw, width, hd)
    sum_ch = channel_sum(cw, hl)
    gt = mm(gmix[...], bvt[...], NT)
    nsum = jnp.zeros((cells, cw), F32)
    for k in range(disks):
        pxk = px[:, k * cw : (k + 1) * cw].astype(F32)
        g = gdisk[:, k * hl : (k + 1) * hl]
        ds = mm((pxk * gt).astype(BF16), sum_ch) * g * (1.0 - g) * scale
        nsum = nsum + mm(ds.astype(BF16), sum_ch, NT) * pxk
    ndisk[...] = nsum.astype(BF16)

    def disk_weight(left, right):
        full = jnp.where(head_mask, mm(left, right, TN), 0.0)
        return jnp.sum(full.reshape(ch, HEADS, width), axis=1)

    def small_out(at, value):
        low = value.astype(gs_ref.dtype)
        for j in range(gs_ref.shape[0]):
            gs_ref[j, at : at + value.shape[0], :] = low[:, j * 128 : (j + 1) * 128]

    small_out(2 * feat, disk_weight(ndisk[...], query[...]))
    small_out(2 * feat + ch, disk_weight(mdisk[...], gmix[...]))

    def disk_query(i, _):
        r = pl.ds(pl.multiple_of(i * CHUNK, CHUNK), CHUNK)
        acc[r, :] = mm(ndisk[r, :], bkt[...])
        return 0

    lax.fori_loop(0, cells // CHUNK, disk_query, 0)
    gkv[...] = jnp.zeros(gkv.shape, F32)

    def backward(i, _):
        r = pl.ds(pl.multiple_of(i * ROWCHUNK, ROWCHUNK), ROWCHUNK)
        oh = one_hot(r)
        gm = mm(oh, gmix[...]).astype(BF16)
        g = gate[r, :]
        ds = mm(gm * kv[r, width:], hsum[...]) * g * (1.0 - g) * scale
        ds_wide = mm(ds.astype(BF16), hspread[...]).astype(BF16)
        acc[...] += mm(one_hot_t(r), ds_wide * kv[r, :width])
        g_wide = mm(g.astype(BF16), hspread[...]).astype(BF16)
        q = qr[pl.ds(pl.multiple_of(i * (ROWCHUNK // 16), ROWCHUNK // 16), ROWCHUNK // 16)]
        grads = jnp.concatenate([ds_wide * q.reshape(ROWCHUNK, width), g_wide * gm], axis=1)
        gkv[...] += mm(comp[r, :], grads, TN)
        comp[r, :] = mm(grads, wkv[...], NT).astype(BF16)
        return 0

    lax.fori_loop(0, chunk_total, backward, 0)
    small_out(0, gkv[:, :width])
    small_out(feat, gkv[:, width:])

    offset = jnp.int32(0)
    for s in range(slots):
        at = pl.ds(pl.multiple_of(offset, 16), block_len)
        got = comp[at, :]
        rgrad_ref[s * block_len : (s + 1) * block_len, :] = jnp.where(
            row < counts[place(s), 0], got, jnp.zeros_like(got)
        )
        offset = offset + ((counts[place(s), 0] + 15) // 16) * 16

    loads[6].wait()

    def lgrad_copy(i):
        r = pl.ds(pl.multiple_of(i * tile, tile), tile)
        return pltpu.make_async_copy(lgrad_ref.at[r], lgrad_hbm.at[r], lsem.at[i])

    def finish(i, _):
        r = pl.ds(pl.multiple_of(i * tile, tile), tile)
        gq = acc[r, :].astype(BF16)
        gquery[r, :] = gq
        lgrad_ref[r, :] += mm(gq, wq_ref[...], NT)
        lgrad_copy(i).start()
        return 0

    lax.fori_loop(0, cells // tile, finish, 0)

    half = gw_ref.shape[1] // 2
    slabs = CHUNK // half

    def out_copy(i):
        part = pl.ds(pl.multiple_of(i * slabs, slabs), slabs)
        return pltpu.make_async_copy(stage.at[part], gw_ref.at[part], osem.at[i])

    def weights(i, _):
        c = pl.ds(pl.multiple_of(i * CHUNK, CHUNK), CHUNK)
        gq = mm(lat_ref[:, c], gquery[...], TN).reshape(slabs, half, width)
        go = mm(mixed[:, c], gul[...], TN).reshape(slabs, half, width)
        part = pl.ds(pl.multiple_of(i * slabs, slabs), slabs)
        stage[part] = jnp.concatenate([gq, go], axis=1).astype(BF16)
        out_copy(i).start()
        return 0

    stage = qr.at[: gw_ref.shape[0]]
    lax.fori_loop(0, width // CHUNK, weights, 0)
    for i in range(width // CHUNK):
        out_copy(i).wait()
    for i in range(cells // tile):
        lgrad_copy(i).wait()


def tile_step(devices, weight, feats, cells, lat_flat, disk_state, wk, wv, target, wq, wo, wd):
    rows, feat = feats.shape
    cell_count, width = lat_flat.shape
    cw = disk_state[-1].shape[0]
    ch = cw // HEADS
    sources = cells.shape[0]
    return pl.pallas_call(
        tile_kernel,
        out_shape=(
            jax.ShapeDtypeStruct((cell_count, width), F32),
            jax.ShapeDtypeStruct((rows, feat), BF16),
            jax.ShapeDtypeStruct((devices, 2 * width // devices, width), BF16),
            jax.ShapeDtypeStruct((width // 128, 2 * feat + 2 * ch, 128), BF16),
            jax.ShapeDtypeStruct((8, target.shape[1]), F32),
        ),
        in_specs=[smem(), vmem(), vmem(), anywhere(), vmem()]
        + [anywhere()] * 2
        + [vmem()] * 5
        + [anywhere()] * 4,
        out_specs=(anywhere(), vmem(), anywhere(), vmem(), vmem()),
        scratch_shapes=[
            pltpu.VMEM((rows, feat), BF16),
            pltpu.VMEM((rows, 128), jnp.int32),
            pltpu.VMEM((rows, 2 * width), BF16),
            pltpu.VMEM((rows // 16, 16, width), BF16),
            pltpu.VMEM((rows, 128), F32),
            pltpu.VMEM((cell_count, width), F32),
            pltpu.VMEM((feat, 2 * width), F32),
            pltpu.VMEM((cell_count, width), BF16),
            pltpu.VMEM((cell_count, width), BF16),
            pltpu.VMEM((cell_count, width), BF16),
            pltpu.VMEM((cell_count, width), BF16),
            pltpu.VMEM((cell_count, cw), BF16),
            pltpu.VMEM(lat_flat.shape, BF16),
            pltpu.VMEM(disk_state[1].shape, BF16),
            pltpu.VMEM(disk_state[2].shape, F32),
            pltpu.VMEM(target.shape, F32),
            pltpu.VMEM(wq.shape, BF16),
            pltpu.VMEM(wo.shape, BF16),
            pltpu.VMEM(wd.shape, BF16),
            pltpu.VMEM((cell_count, width), F32),
            pltpu.VMEM((width, 128), BF16),
            pltpu.VMEM((128, width), BF16),
            pltpu.VMEM((feat, 2 * width), BF16),
            pltpu.VMEM((8 * sources, 128), jnp.int32),
            pltpu.SMEM((8 * sources, 128), jnp.int32),
            pltpu.SemaphoreType.DMA,
            pltpu.SemaphoreType.DMA((width // CHUNK,)),
            pltpu.SemaphoreType.DMA((7,)),
            pltpu.SemaphoreType.DMA((cell_count // CHUNK,)),
        ],
        compiler_params=pltpu.CompilerParams(vmem_limit_bytes=62 * 1024 * 1024),
        name="tile",
    )(weight, feats, cells, lat_flat, *disk_state, wk, wv, target, wq, wo, wd)


SIDE = 4


def lat_peer(p, k):
    y = lax.rem(p // SIDE + k // SIDE, SIDE)
    z = lax.rem(p % SIDE + k % SIDE, SIDE)
    return y * SIDE + z


def loop(count, step, start=0):
    def run(i, carry):
        step(i)
        return carry

    lax.fori_loop(start, count, run, 0)


def send_kernel(
    feats_ref,
    cells_ref,
    lat_hbm,
    wq_hbm,
    disk_ref,
    wdk_ref,
    wdv_ref,
    got_ref,
    gcells_ref,
    query_hbm,
    px_hbm,
    gdisk_hbm,
    mdisk,
    bkt,
    bvt,
    lat_ref,
    wq_ref,
    query,
    px,
    gdisk,
    fsend,
    frecv,
    csend,
    crecv,
    local,
    loads,
    stores,
):
    lats = cells_ref.shape[0]
    p = lax.axis_index("lat")
    barrier = pltpu.get_barrier_semaphore()

    def greet(k):
        pl.semaphore_signal(
            barrier, inc=1, device_id={"lat": lat_peer(p, k)}, device_id_type=pl.DeviceIdType.MESH
        )

    loop(lats, greet, 1)
    own = pltpu.make_async_copy(feats_ref.at[p], got_ref.at[p], local.at[0])
    own.start()
    own_cells = pltpu.make_async_copy(cells_ref.at[p], gcells_ref.at[p], local.at[1])
    own_cells.start()
    pl.semaphore_wait(barrier, lats - 1)

    def feats_copy(k):
        to = lat_peer(p, k)
        return pltpu.make_async_remote_copy(
            src_ref=feats_ref.at[to],
            dst_ref=got_ref.at[p],
            send_sem=fsend.at[k],
            recv_sem=frecv.at[k],
            device_id={"lat": to},
            device_id_type=pl.DeviceIdType.MESH,
        )

    def cells_copy(k):
        to = lat_peer(p, k)
        return pltpu.make_async_remote_copy(
            src_ref=cells_ref.at[to],
            dst_ref=gcells_ref.at[p],
            send_sem=csend.at[k],
            recv_sem=crecv.at[k],
            device_id={"lat": to},
            device_id_type=pl.DeviceIdType.MESH,
        )

    def begin(k):
        feats_copy(k).start()
        cells_copy(k).start()

    def end(k):
        feats_copy(k).wait()
        cells_copy(k).wait()

    load_lat = pltpu.make_async_copy(lat_hbm, lat_ref, loads.at[0])
    load_wq = pltpu.make_async_copy(wq_hbm, wq_ref, loads.at[1])
    load_lat.start()
    load_wq.start()
    loop(lats, begin, 1)

    load_lat.wait()
    load_wq.wait()
    cells, width = lat_ref.shape
    ch = wdk_ref.shape[0]
    disks = disk_ref.shape[0] // ch
    cw = ch * HEADS
    hd = width // HEADS
    hl = gdisk.shape[1] // disks
    scale = 1.0 / math.sqrt(hd)

    def project(i):
        r = pl.ds(pl.multiple_of(i * CHUNK, CHUNK), CHUNK)
        query[r, :] = mm(lat_ref[r, :], wq_ref[...]).astype(BF16)

    loop(cells // CHUNK, project)
    store_query = pltpu.make_async_copy(query, query_hbm, stores.at[0])
    store_query.start()

    spread_ch = jnp.where(
        lax.broadcasted_iota(jnp.int32, (cw, ch), 0) // HEADS
        == lax.broadcasted_iota(jnp.int32, (cw, ch), 1),
        1.0,
        0.0,
    ).astype(BF16)
    head_mask = head_match(cw, width, hd)
    bkt[...] = jnp.where(head_mask, mm(spread_ch, wdk_ref[...]), 0.0).astype(BF16)
    bvt[...] = jnp.where(head_mask, mm(spread_ch, wdv_ref[...]), 0.0).astype(BF16)
    sum_ch = channel_sum(cw, hl)
    qt = mm(query[...], bkt[...], NT)
    msum = jnp.zeros((cells, cw), F32)
    for k in range(disks):
        pxk = mm(disk_ref[k * ch : (k + 1) * ch, :], spread_ch, (((0,), (1,)), ((), ())))
        px[:, k * cw : (k + 1) * cw] = pxk.astype(BF16)
        g = jax.nn.sigmoid(mm((pxk * qt).astype(BF16), sum_ch) * scale)
        gdisk[:, k * hl : (k + 1) * hl] = g
        msum = msum + mm(g.astype(BF16), sum_ch, NT) * pxk
    mdisk[...] = msum.astype(BF16)
    store_px = pltpu.make_async_copy(px, px_hbm, stores.at[1])
    store_px.start()
    store_gdisk = pltpu.make_async_copy(gdisk, gdisk_hbm, stores.at[2])
    store_gdisk.start()

    own.wait()
    own_cells.wait()
    loop(lats, end, 1)
    store_query.wait()
    store_px.wait()
    store_gdisk.wait()


def send_rows(feats, cells, lat_flat, disk, wdk, wdv, wq):
    lats = cells.shape[0]
    count, width = lat_flat.shape
    ch = wdk.shape[0]
    disks = disk.shape[0] // ch
    cw = ch * HEADS
    dma = pltpu.SemaphoreType.DMA
    return pl.pallas_call(
        send_kernel,
        out_shape=(
            jax.ShapeDtypeStruct(feats.shape, feats.dtype),
            jax.ShapeDtypeStruct(cells.shape, cells.dtype),
            jax.ShapeDtypeStruct((count, width), BF16),
            jax.ShapeDtypeStruct((count, disks * cw), BF16),
            jax.ShapeDtypeStruct((count, disks * 128), F32),
            jax.ShapeDtypeStruct((count, cw), BF16),
            jax.ShapeDtypeStruct((cw, width), BF16),
            jax.ShapeDtypeStruct((cw, width), BF16),
        ),
        in_specs=[anywhere()] * 4 + [vmem()] * 3,
        out_specs=(anywhere(),) * 5 + (vmem(),) * 3,
        scratch_shapes=[
            pltpu.VMEM((count, width), BF16),
            pltpu.VMEM((width, width), BF16),
            pltpu.VMEM((count, width), BF16),
            pltpu.VMEM((count, disks * cw), BF16),
            pltpu.VMEM((count, disks * 128), F32),
        ]
        + [dma((lats,))] * 4
        + [dma((2,)), dma((2,)), dma((3,))],
        compiler_params=pltpu.CompilerParams(
            collective_id=1, has_side_effects=True, vmem_limit_bytes=60 * 1024 * 1024
        ),
        name="send_rows",
    )(feats, cells, lat_flat, wq, disk, wdk, wdv)


def axis_peer(v, k):
    return lax.rem(v + k, SIDE)


def reduce_kernel(
    cut_a,
    cut_b,
    parts,
    gw_ref,
    gs_ref,
    loss_ref,
    rgrad_ref,
    share_ref,
    small_ref,
    stat_ref,
    back_ref,
    s1,
    r1,
    sg1,
    rg1,
    s2a,
    r2a,
    s2b,
    r2b,
    s2c,
    r2c,
    s3a,
    r3a,
    s3b,
    r3b,
    s3c,
    r3c,
    r4a,
    r4b,
    r4c,
    sg2,
    rg2,
    rg3,
    sg3,
    g4,
    t4,
    t5,
    t6,
    mine,
    plane,
    chips,
    local,
    s_core,
    r_core,
    s_back,
    r_back,
    s_a2,
    r_a2,
    s_b2,
    r_b2,
    s_c2,
    r_c2,
    s_p3,
    r_p3,
    s_p4,
    r_p4,
    s_g2,
    r_g2,
    s_g3,
    r_g3,
    s_g4,
    r_g4,
    s_t4,
    r_t4,
    s_g5,
    r_g5,
    s_t5,
    r_t5,
    s_g6,
    r_g6,
    s_t6,
    r_t6,
):
    xs, cores, ys, zs, slab, width = gw_ref.shape
    lons = xs * cores
    lats = ys * zs
    lon = lax.axis_index("lon")
    p = lax.axis_index("lat")
    x, c = lon // cores, lon % cores
    y, z = p // zs, p % zs
    other = 1 - c
    cols_a = pl.ds(0, cut_a)
    cols_b = pl.ds(cut_a, cut_b - cut_a)
    cols_c = pl.ds(cut_b, width - cut_b)
    piece = g4.shape[1]
    pieces = small_ref.shape[1]

    def remote(axis, target, src, dst, ssem, rsem):
        return pltpu.make_async_remote_copy(
            src_ref=src,
            dst_ref=dst,
            send_sem=ssem,
            recv_sem=rsem,
            device_id={axis: target},
            device_id_type=pl.DeviceIdType.MESH,
        )

    def to_x(k, src, dst, ssem, rsem):
        return remote("lon", axis_peer(x, k) * cores + c, src, dst, ssem, rsem)

    def to_y(k, src, dst, ssem, rsem):
        return remote("lat", axis_peer(y, k) * zs + z, src, dst, ssem, rsem)

    def to_z(k, src, dst, ssem, rsem):
        return remote("lat", y * zs + axis_peer(z, k), src, dst, ssem, rsem)

    barrier = pltpu.get_barrier_semaphore()

    def greet(axis, target):
        pl.semaphore_signal(
            barrier, inc=1, device_id={axis: target}, device_id_type=pl.DeviceIdType.MESH
        )

    loop(lats, lambda k: greet("lat", lat_peer(p, k)), 1)
    loop(xs, lambda k: greet("lon", axis_peer(x, k) * cores + c), 1)
    greet("lon", x * cores + other)

    own_small = pltpu.make_async_copy(gs_ref.at[:, c], sg1, local.at[xs])
    own_small.start()

    def own_copy(j):
        return pltpu.make_async_copy(gw_ref.at[j, c], s1.at[j], local.at[j])

    loop(xs, lambda j: own_copy(j).start())
    own_back = pltpu.make_async_copy(rgrad_ref.at[p], back_ref.at[p], local.at[xs + 1])
    own_back.start()
    pl.semaphore_wait(barrier, lats + xs - 1)

    mate = x * cores + other
    core_small = remote("lon", mate, gs_ref.at[:, other], rg1, s_core.at[xs], r_core.at[xs])
    core_small.start()

    def core_copy(k):
        j = axis_peer(x, k)
        return remote("lon", mate, gw_ref.at[j, other], r1.at[j], s_core.at[k], r_core.at[k])

    loop(xs, lambda k: core_copy(k).start(), 1)
    core_copy(0).start()

    def back_copy(k):
        to = lat_peer(p, k)
        return remote("lat", to, rgrad_ref.at[to], back_ref.at[p], s_back.at[k], r_back.at[k])

    def back_part(i):
        loop(parts[i + 1], lambda k: back_copy(k).start(), parts[i])

    back_part(0)

    def a2_copy(k):
        j = axis_peer(x, k)
        return to_x(k, s1.at[j, :, :, :, cols_a], r2a.at[k - 1], s_a2.at[k], r_a2.at[k])

    def b2_copy(k):
        return to_y(
            k, s1.at[:, axis_peer(y, k), :, :, cols_b], r2b.at[k - 1], s_b2.at[k], r_b2.at[k]
        )

    def c2_copy(k):
        return to_z(
            k, s1.at[:, :, axis_peer(z, k), :, cols_c], r2c.at[k - 1], s_c2.at[k], r_c2.at[k]
        )

    def g2_copy(k):
        return to_x(k, sg1.at[axis_peer(x, k)], rg2.at[k - 1], s_g2.at[k], r_g2.at[k])

    own_small.wait()
    core_small.wait_recv()
    sg1[...] = sg1[...] + rg1[...]
    loop(xs, lambda k: g2_copy(k).start(), 1)

    def add_core(j):
        def step(i):
            s1[j, i] = s1[j, i] + r1[j, i]

        loop(ys, step)

    def core_step(k):
        j = axis_peer(x, k)
        own_copy(j).wait()
        core_copy(k).wait_recv()
        add_core(j)
        a2_copy(k).start()

    loop(xs, core_step, 1)
    own_copy(x).wait()
    core_copy(0).wait_recv()
    add_core(x)

    def spread(k):
        b2_copy(k).start()
        c2_copy(k).start()

    loop(SIDE, spread, 1)

    def g3_copy(k):
        to = lat_peer(p, k)
        return remote("lat", to, sg2.at[to], rg3.at[k - 1], s_g3.at[k], r_g3.at[k])

    loop(xs, lambda k: g2_copy(k).wait_recv(), 1)
    total = sg1[x].astype(F32)
    for k in range(xs - 1):
        total = total + rg2[k].astype(F32)
    sg2[pieces:] = jnp.zeros((lats - pieces,) + sg2.shape[1:], BF16)
    sg2[:pieces] = total.astype(BF16).reshape(pieces, piece, total.shape[1])
    loop(lats, lambda k: g3_copy(k).start(), 1)

    def a3_copy(k):
        return to_y(k, s2a.at[axis_peer(y, k)], r3a.at[k - 1], s_p3.at[0, k], r_p3.at[0, k])

    def b3_copy(k):
        return to_z(k, s2b.at[:, axis_peer(z, k)], r3b.at[k - 1], s_p3.at[1, k], r_p3.at[1, k])

    def c3_copy(k):
        return to_x(k, s2c.at[axis_peer(x, k)], r3c.at[k - 1], s_p3.at[2, k], r_p3.at[2, k])

    loop(SIDE, lambda k: a2_copy(k).wait_recv(), 1)

    def sum_a(i):
        value = s1[x, i, :, :, :cut_a].astype(F32)
        for k in range(SIDE - 1):
            value = value + r2a[k, i].astype(F32)
        s2a[i] = value.astype(BF16)

    loop(ys, sum_a)
    loop(SIDE, lambda k: a3_copy(k).start(), 1)

    loop(SIDE, lambda k: c2_copy(k).wait_recv(), 1)

    def sum_c(i):
        value = s1[i, :, z, :, cut_b:].astype(F32)
        for k in range(SIDE - 1):
            value = value + r2c[k, i].astype(F32)
        s2c[i] = value.astype(BF16)

    loop(xs, sum_c)
    loop(SIDE, lambda k: c3_copy(k).start(), 1)
    loop(SIDE, lambda k: b2_copy(k).wait_recv(), 1)

    def sum_b(i):
        value = s1[i, y, :, :, cut_a:cut_b].astype(F32)
        for k in range(SIDE - 1):
            value = value + r2b[k, i].astype(F32)
        s2b[i] = value.astype(BF16)

    loop(xs, sum_b)
    loop(SIDE, lambda k: b3_copy(k).start(), 1)

    back_part(1)
    loop(lats, lambda k: g3_copy(k).wait_recv(), 1)

    def add_small(k, value):
        return value + rg3[k].astype(F32)

    sg3[...] = lax.fori_loop(0, lats - 1, add_small, sg2[p].astype(F32)).astype(BF16)
    g4[p] = sg3[...]

    def g4_copy(k):
        return remote("lat", lat_peer(p, k), sg3, g4.at[p], s_g4.at[k], r_g4.at[k])

    loop(lats, lambda k: g4_copy(k).start(), 1)

    def a4_copy(k):
        return to_z(k, s3a.at[axis_peer(z, k)], r4a.at[k - 1], s_p4.at[0, k], r_p4.at[0, k])

    def b4_copy(k):
        return to_x(k, s3b.at[axis_peer(x, k)], r4b.at[k - 1], s_p4.at[1, k], r_p4.at[1, k])

    def c4_copy(k):
        return to_y(k, s3c.at[axis_peer(y, k)], r4c.at[k - 1], s_p4.at[2, k], r_p4.at[2, k])

    def summed(own, others):
        value = own.astype(F32)
        for k in range(SIDE - 1):
            value = value + others[k].astype(F32)
        return value

    loop(SIDE, lambda k: a3_copy(k).wait_recv(), 1)
    s3a[...] = summed(s2a[y], r3a).astype(BF16)
    loop(SIDE, lambda k: a4_copy(k).start(), 1)
    loop(SIDE, lambda k: c3_copy(k).wait_recv(), 1)
    s3c[...] = summed(s2c[x], r3c).astype(BF16)
    loop(SIDE, lambda k: c4_copy(k).start(), 1)
    loop(SIDE, lambda k: b3_copy(k).wait_recv(), 1)
    s3b[...] = summed(s2b[:, z], r3b).astype(BF16)
    loop(SIDE, lambda k: b4_copy(k).start(), 1)
    back_part(2)

    def g5_copy(k):
        return to_x(
            k, g4.at[pl.ds(0, pieces)], small_ref.at[lon], s_g5.at[k], r_g5.at[k]
        )

    def g6_copy(j):
        at = j * cores + c
        return remote("lon", mate, small_ref.at[at], small_ref.at[at], s_g6.at[j], r_g6.at[j])

    loop(lats, lambda k: g4_copy(k).wait_recv(), 1)
    small_ref[lon] = g4[:pieces]
    loop(SIDE, lambda k: g5_copy(k).start(), 1)

    loop(SIDE, lambda k: a4_copy(k).wait_recv(), 1)
    share_a = summed(s3a[z], r4a)
    loop(SIDE, lambda k: c4_copy(k).wait_recv(), 1)
    share_c = summed(s3c[y], r4c)
    loop(SIDE, lambda k: b4_copy(k).wait_recv(), 1)
    share_b = summed(s3b[x], r4b)
    share_ref[:, :cut_a] = share_a
    share_ref[:, cut_a:cut_b] = share_b
    share_ref[:, cut_b:] = share_c
    half = slab // 2

    def lane_sums(value):
        value = jnp.sum(value, axis=0, keepdims=True)
        total = value[:, :128]
        for j in range(1, value.shape[1] // 128):
            total = total + value[:, j * 128 : (j + 1) * 128]
        return total

    square = jnp.concatenate([share_a * share_a, share_b * share_b, share_c * share_c], axis=1)
    row = lax.broadcasted_iota(jnp.int32, mine.shape, 0)
    mine[...] = jnp.where(
        row == 0,
        lane_sums(loss_ref[...]),
        jnp.where(
            row == 1,
            lane_sums(square[:half]),
            jnp.where(row == 2, lane_sums(square[half:]), 0.0),
        ),
    )

    def t4_copy(k):
        return remote("lat", lat_peer(p, k), mine, t4.at[k - 1], s_t4.at[k], r_t4.at[k])

    loop(lats, lambda k: t4_copy(k).start(), 1)
    back_part(3)
    loop(SIDE, lambda k: g5_copy(k).wait_recv(), 1)
    loop(xs, lambda j: g6_copy(j).start())

    loop(xs, lambda k: core_copy(k).wait_send())
    core_small.wait_send()

    def sent_side(k):
        a2_copy(k).wait_send()
        g2_copy(k).wait_send()
        b2_copy(k).wait_send()
        c2_copy(k).wait_send()
        a3_copy(k).wait_send()
        b3_copy(k).wait_send()
        c3_copy(k).wait_send()
        a4_copy(k).wait_send()
        b4_copy(k).wait_send()
        c4_copy(k).wait_send()

    loop(SIDE, sent_side, 1)

    loop(lats, lambda k: t4_copy(k).wait_recv(), 1)
    plane[...] = lax.fori_loop(0, lats - 1, lambda k, value: value + t4[k], mine[...])

    def t5_copy(k):
        return to_x(k, plane, t5.at[k - 1], s_t5.at[k], r_t5.at[k])

    loop(SIDE, lambda k: t5_copy(k).start(), 1)
    loop(SIDE, lambda k: t5_copy(k).wait_recv(), 1)
    chips[...] = summed(plane[...], t5)
    t6_copy = remote("lon", mate, chips, t6, s_t6.at[0], r_t6.at[0])
    t6_copy.start()

    def sent_lat(k):
        back_copy(k).wait()
        g3_copy(k).wait_send()
        g4_copy(k).wait_send()
        t4_copy(k).wait_send()

    loop(lats, sent_lat, 1)
    own_back.wait()
    loop(xs, lambda j: g6_copy(j).wait())

    def sent_x(k):
        g5_copy(k).wait_send()
        t5_copy(k).wait_send()

    loop(SIDE, sent_x, 1)
    t6_copy.wait()
    stat_ref[...] = chips[...] + t6[...]


def reduce_all(gw, gs, loss, rgrad):
    xs, cores, lats, slab, width = gw.shape
    ys, zs = lats // SIDE, SIDE
    lons = xs * cores
    small_rows = gs.shape[2]
    piece = 32
    pieces = small_rows // piece
    cut_a, cut_b = 512, 768
    parts = (1, lats, lats, lats, lats)
    wa, wb, wc = cut_a, cut_b - cut_a, width - cut_b
    dma = pltpu.SemaphoreType.DMA

    def buf(*shape, dtype=BF16):
        return pltpu.VMEM(shape, dtype)

    pairs = [
        (xs + 1,),
        (lats,),
        (SIDE,),
        (SIDE,),
        (SIDE,),
        (3, SIDE),
        (3, SIDE),
        (SIDE,),
        (lats,),
        (lats,),
        (lats,),
        (SIDE,),
        (SIDE,),
        (xs,),
        (1,),
    ]
    n = SIDE - 1
    return pl.pallas_call(
        functools.partial(reduce_kernel, cut_a, cut_b, parts),
        out_shape=(
            jax.ShapeDtypeStruct((slab, width), F32),
            jax.ShapeDtypeStruct((lons, pieces, piece, 128), BF16),
            jax.ShapeDtypeStruct((8, 128), F32),
            jax.ShapeDtypeStruct(rgrad.shape, BF16),
        ),
        in_specs=[anywhere(), anywhere(), vmem(), anywhere()],
        out_specs=(vmem(), vmem(), vmem(), anywhere()),
        scratch_shapes=[
            buf(xs, ys, zs, slab, width),
            buf(xs, ys, zs, slab, width),
            buf(xs, small_rows, 128),
            buf(xs, small_rows, 128),
            buf(ys, zs, slab, wa),
            buf(n, ys, zs, slab, wa),
            buf(xs, zs, slab, wb),
            buf(n, xs, zs, slab, wb),
            buf(xs, ys, slab, wc),
            buf(n, xs, ys, slab, wc),
            buf(zs, slab, wa),
            buf(n, zs, slab, wa),
            buf(xs, slab, wb),
            buf(n, xs, slab, wb),
            buf(ys, slab, wc),
            buf(n, ys, slab, wc),
            buf(n, slab, wa),
            buf(n, slab, wb),
            buf(n, slab, wc),
            buf(lats, piece, 128),
            buf(xs - 1, small_rows, 128),
            buf(lats - 1, piece, 128),
            buf(piece, 128),
            buf(lats, piece, 128),
            buf(lats - 1, 8, 128, dtype=F32),
            buf(n, 8, 128, dtype=F32),
            buf(8, 128, dtype=F32),
            buf(8, 128, dtype=F32),
            buf(8, 128, dtype=F32),
            buf(8, 128, dtype=F32),
            dma((xs + 2,)),
        ]
        + [dma(n) for n in pairs for _ in range(2)],
        compiler_params=pltpu.CompilerParams(
            collective_id=2, has_side_effects=True, vmem_limit_bytes=60 * 1024 * 1024
        ),
        name="reduce_all",
    )(gw.reshape((xs, cores, ys, zs, slab, width)), gs, loss, rgrad)


def finish_kernel(
    loss_scale,
    slot_ref,
    got_ref,
    share_ref,
    small_ref,
    stat_ref,
    out_ref,
    query_ref,
    wout_ref,
    key_ref,
    value_ref,
    dkey_ref,
    dvalue_ref,
    loss_ref,
):
    block_count = slot_ref.shape[0]
    block_len = out_ref.shape[0] // block_count
    half, width = query_ref.shape
    for b in range(block_count):
        out_ref[b * block_len : (b + 1) * block_len, :] = got_ref[
            pl.ds(pl.multiple_of(slot_ref[b] * block_len, block_len), block_len), :
        ]

    loss_ref[...] = jnp.sum(stat_ref[0:1, :], axis=1, keepdims=True) * loss_scale

    def scale(total, entries):
        return 1.0 / jnp.sqrt(total / entries + 1e-06)

    def whole(value):
        return jnp.sum(jnp.sum(value, axis=0, keepdims=True), axis=1, keepdims=True)

    query_ref[...] = share_ref[:half] * scale(whole(stat_ref[1:2, :]), width * width)
    wout_ref[...] = share_ref[half:] * scale(whole(stat_ref[2:3, :]), width * width)
    lons, pieces, piece, lanes = small_ref.shape
    sums = jnp.concatenate(
        [small_ref[j].reshape(pieces * piece, lanes).astype(F32) for j in range(lons)], axis=1
    )
    at = 0
    for ref in (key_ref, value_ref, dkey_ref, dvalue_ref):
        n = ref.shape[0]
        g = sums[at : at + n]
        ref[...] = g * scale(whole(g * g), n * width)
        at += n


def finish(loss_scale, slots, got, share, small, stat, rows, feat, ch):
    width = share.shape[1]
    half = share.shape[0] // 2
    shapes = [
        ((rows, got.shape[1]), BF16),
        ((half, width), F32),
        ((half, width), F32),
        ((feat, width), F32),
        ((feat, width), F32),
        ((ch, width), F32),
        ((ch, width), F32),
        ((1, 1), F32),
    ]
    return pl.pallas_call(
        functools.partial(finish_kernel, loss_scale),
        out_shape=tuple(jax.ShapeDtypeStruct(s, d) for s, d in shapes),
        in_specs=[smem()] + [vmem()] * 4,
        out_specs=(vmem(),) * len(shapes),
        compiler_params=pltpu.CompilerParams(vmem_limit_bytes=60 * 1024 * 1024),
        name="finish",
    )(slots, got, share, small, stat)


def cell_weights(row_total):
    centres = (np.arange(row_total, dtype=np.float32) + np.float32(0.5)) / np.float32(row_total)
    weight = np.cos(np.float32(math.pi / 180.0) * (np.float32(-60.0) + np.float32(120.0) * centres))
    return (weight / np.mean(weight)).astype(np.float32)


def body(
    radiances,
    block_tile,
    block_rows,
    row_cells,
    latents,
    disk_pixels,
    targets,
    w_query,
    w_key,
    w_value,
    w_disk_key,
    w_disk_value,
    w_out,
    w_decode,
):
    lat_count = lax.axis_size("lat")
    device_count = lax.axis_size(("lon", "lat"))
    rows = radiances.shape[0]
    tile_lat, tile_lon, width = latents.shape
    out_width = targets.shape[2]
    cells = tile_lat * tile_lon
    feat = radiances.shape[1]
    ch = w_disk_key.shape[0]
    sfeats, scells, slot = pack(block_tile, block_rows, radiances, row_cells, lat_count)
    lat_flat = latents.reshape(cells, width)
    got_feats, got_cells, *disk_state = send_rows(
        sfeats.reshape(lat_count, -1, feat),
        scells,
        lat_flat,
        disk_pixels.reshape(-1, cells),
        w_disk_key,
        w_disk_value,
        w_query,
    )
    lgrad, rgrad, gw, gs, loss = tile_step(
        device_count,
        jnp.asarray(cell_weights(tile_lat * lat_count)),
        got_feats.reshape(-1, feat),
        got_cells,
        lat_flat,
        disk_state,
        w_key,
        w_value,
        targets.reshape(cells, out_width),
        w_query,
        w_out,
        w_decode,
    )
    cores = 2
    xs = lax.axis_size("lon") // cores
    share, small, stat, returned = reduce_all(
        gw.reshape((xs, cores, lat_count) + gw.shape[1:]),
        gs.reshape((xs, cores) + gs.shape[1:]),
        loss,
        rgrad.reshape(lat_count, -1, feat),
    )
    row_grad, query, out, key, value, dkey, dvalue, total = finish(
        1.0 / (cells * device_count * out_width),
        slot,
        returned.reshape(-1, feat),
        share,
        small,
        stat,
        rows,
        feat,
        ch,
    )
    return (
        total.reshape(()),
        lgrad.reshape(latents.shape),
        row_grad,
        query,
        out,
        key,
        value,
        dkey,
        dvalue,
    )


def solution(mesh):
    both = ("lon", "lat")
    placed = (
        P(both, None),
        P(both),
        P(both),
        P(both),
        P("lat", "lon", None),
        P(None, None, "lat", "lon"),
        P("lat", "lon", None),
    ) + (P(),) * 7
    return jax.shard_map(
        body,
        mesh=mesh,
        in_specs=placed,
        out_specs=(
            P(),
            P("lat", "lon", None),
            P(both, None),
            P(both, None),
            P(both, None),
            P(),
            P(),
            P(),
            P(),
        ),
        check_vma=False,
    )
```
